32 devices in a mesh: groups: 2 (over y), blk: 4 (over z), eig: 2 (over x), rep: 2 (over core).
Axes of the slice: x: 2, y: 2, z: 4, core: 2. Of those that a mesh axis runs over, the one named last changes fastest.
Arguments:
- acts: bfloat16 [6144, 28672], P(('groups', 'blk'), ('eig', 'rep')), parts along dimension 0, may hold values from -6 to 6
- out_grads: bfloat16 [6144, 8192], P(('groups', 'blk'), ('eig', 'rep')), parts along dimension 0, may hold values from -6 to 6
- basis_in: bfloat16 [256, 28672], P('blk', ('eig', 'rep')), may hold values from -0.03125 to 0.03125
- basis_out: bfloat16 [128, 8192], P(None, ('eig', 'rep')), may hold values from -0.0625 to 0.0625
- eigvals: bfloat16 [256, 128], P('blk'), may hold values from 0.049804688 to 5
- query_out: bfloat16 [8192, 256], P(('eig', 'rep'), 'groups'), parts along dimension 1, may hold values from -0.017944336 to 0.017944336
- query_in: bfloat16 [28672, 256], P(('eig', 'rep'), 'groups'), parts along dimension 1, may hold values from -0.017944336 to 0.017944336
- seq_ids: int32 [6144], P(('groups', 'blk')), parts along dimension 0, may hold values from 0 to 7, never falling along the last dimension, each value on 1 to 1536 neighbouring positions
- owner: int32 [16], P('groups'), parts along dimension 0, may hold values from 0 to 7, each once
Outputs:
- scores: float32 [8, 8], P(('groups', 'eig', 'rep'), 'blk'), parts along dimension 0
The draws below stay inside these ranges and needn't reach their ends.
There are 2 independent parts, one for each index of `groups`. The reference program is written for one: setup_inputs(seed, part) draws one part's arguments, and reference() takes and returns one part's arrays. A program takes and returns all parts, laid end to end along the dimension named above; an argument that names none is the same for every part. Nothing has to cross between parts.
Inputs may be any that keep to these rules, and one draw needn't show every extreme that they name: `seq_ids`: ids never fall along the tokens; every one of the 8 sequences has 1 to 1536 tokens, one exactly 1536. `owner`: a permutation: each column belongs to one sequence.
All inputs are finite; a program needn't handle non-finite values.
Results may differ from the reference program's by a relative error of at most 0.0068.
Values may be sent and summed in bfloat16 or wider, within the bound.
No kernel may reach another device: no remote copies, remote signals or barrier semaphores. Data moves between devices by JAX's collectives and lax.ppermute only.
A program may use at most 64 MiB of HBM per device.

```python
import math
import jax
import jax.numpy as jnp
import numpy as np
from jax import lax

DIN = 28672
DOUT = 8192
R = 32
ES = 128
TOKENS = 3072
EA = 256
NQ = 4
PAIRS = 128
SEQS = 8
MOST = 1536


def steps_of(rng, shape, cuts, smallest, high):
    def one(dim, parts):
        draws = jax.random.uniform(jax.random.fold_in(jax.random.fold_in(rng, 6), dim), (parts,), jnp.float32, smallest / len(cuts), high / len(cuts))
        return jnp.repeat(jnp.exp(draws), shape[dim] // parts).reshape((-1,) + (1,) * (len(shape) - dim - 1))

    gain = one(*cuts[0])
    for cut in cuts[1:]:
        gain = gain * one(*cut)
    return gain


def profile(amount, total, limit, lean):
    weights = [(1 << 20) // math.isqrt(grade ** lean) + 1 for grade in range(2, amount + 1)]
    spare, holding = total - limit - (amount - 1), [1] * (amount - 1)
    while spare > 0:
        movable = [i for i in range(amount - 1) if holding[i] < limit]
        pool, budget = sum([weights[i] for i in movable]), spare
        for i in movable:
            more = min(limit - holding[i], max(1, budget * weights[i] // pool), spare)
            holding[i] = holding[i] + more
            spare = spare - more
    return np.array([limit] + holding)


def ragged(rng, amount, total, most, lean):
    if amount == 2:
        one = jax.random.randint(rng, (), max(1, total - most), min(most, total - 1) + 1)
        return jnp.stack([one, total - one])
    sizes = jnp.asarray(profile(amount, total, most, lean), jnp.int32)
    couples = (amount - 1) // 2
    donor, sink = sizes[1:1 + 2 * couples:2], sizes[2:2 + 2 * couples:2]
    slack = jnp.minimum(donor - 1, most - sink)
    moved = jax.random.randint(jax.random.fold_in(rng, 1), (couples,), 0, 1 << 20) % (slack + 1)
    sizes = sizes.at[1:1 + 2 * couples:2].set(donor - moved).at[2:2 + 2 * couples:2].set(sink + moved)
    return sizes[jax.random.permutation(jax.random.fold_in(rng, 2), amount)]


def bell_draw(stream_key, shape, width, reach, shards=(), held_as=jnp.bfloat16):
    array = width * jax.random.normal(stream_key, shape, jnp.float32)
    if shards:
        array = array * steps_of(stream_key, shape, shards, -0.22, 0.18)
    return jnp.clip(array, -reach, reach).astype(held_as)


def setup_inputs(seed: int = 0, part: int = 0) -> dict:
    seeds = jax.random.split(jax.random.key(seed), 10)
    part_keys = jax.random.split(jax.random.fold_in(seeds[9], part), 10)
    return {
        "acts": bell_draw(part_keys[0], (TOKENS, DIN), 1.0, 6.0, ((0, 4), (1, 4))),
        "out_grads": bell_draw(part_keys[1], (TOKENS, DOUT), 1.0, 6.0, ((0, 4), (1, 4))),
        "basis_in": bell_draw(seeds[2], (EA, DIN), DIN ** -0.5, 0.03125, ((0, 4), (1, 4))),
        "basis_out": bell_draw(seeds[3], (ES, DOUT), DOUT ** -0.5, 0.0625, ((1, 4),)),
        "eigvals": jnp.clip(jnp.exp(math.log(5.0) - 4.609084 * jax.random.uniform(seeds[4], (EA, ES), jnp.float32) ** steps_of(seeds[4], (EA, ES), ((0, 4),), -0.2, 0.2)), 0.049804688, 5.0).astype(jnp.bfloat16),
        "query_out": bell_draw(part_keys[5], (DOUT, PAIRS), 0.003, 0.017944336, ((0, 4),)),
        "query_in": bell_draw(part_keys[6], (DIN, PAIRS), 0.003, 0.017944336, ((0, 4),)),
        "seq_ids": jnp.searchsorted(jnp.cumsum(ragged(part_keys[7], SEQS, TOKENS, MOST, 0)), jnp.arange(TOKENS), side="right").astype(jnp.int32),
        "owner": jax.random.permutation(part_keys[8], SEQS).astype(jnp.int32),
    }


def precondition(in_query, eig_rows, out_query):
    row_count = in_query.shape[0]
    left_side = in_query.astype(jnp.float32).reshape(row_count, NQ, R)
    right_side = out_query.astype(jnp.float32).reshape(ES, NQ, R)
    outer_sum = jnp.einsum("jqr,iqr->jqi", left_side, right_side, precision=lax.Precision.HIGHEST)
    inverse = 1.0 / (eig_rows.astype(jnp.float32) + 0.05)
    return (outer_sum * inverse[:, None, :]).astype(jnp.bfloat16)


def reference(acts, out_grads, basis_in, basis_out, eigvals, query_out, query_in, seq_ids, owner):
    grad_proj = jnp.dot(out_grads, basis_out.T, preferred_element_type=jnp.float32).astype(jnp.bfloat16)
    out_query = jnp.dot(basis_out, query_out, preferred_element_type=jnp.float32).astype(jnp.bfloat16)
    in_query = jnp.dot(basis_in, query_in, preferred_element_type=jnp.float32).astype(jnp.bfloat16)
    weighted = precondition(in_query, eigvals, out_query)
    projected = jnp.dot(acts, basis_in.T, preferred_element_type=jnp.float32)

    def per_query(slab):
        mixed_rows = jnp.dot(grad_proj, slab.T, preferred_element_type=jnp.float32)
        return jnp.sum(mixed_rows * projected, axis=1)

    per_token = lax.map(per_query, jnp.transpose(weighted, (1, 0, 2)))
    per_sequence = jax.ops.segment_sum(per_token.T, seq_ids, num_segments=SEQS).T
    return jnp.zeros((NQ, SEQS), jnp.float32).at[:, owner].set(per_sequence)
```

```python
import jax
import jax.numpy as jnp
from jax import lax
from jax.sharding import PartitionSpec as P

R = 32


damping = 0.05


def contract_last(left_side, right_side):
    return lax.dot_general(
        left_side, right_side, (((1,), (1,)), ((), ())), preferred_element_type=jnp.float32
    )


def swap_sum(value, axis, send_as):
    size = lax.axis_size(axis)
    if size & (size - 1):
        return lax.psum(value, axis)
    step = 1
    while step < size:
        pairs = [(i, i ^ step) for i in range(size)]
        value = value + lax.ppermute(value.astype(send_as), axis, pairs).astype(jnp.float32)
        step *= 2
    return value


def by_distance(value):
    size = lax.axis_size("blk")
    return [value] + [
        lax.ppermute(value, "blk", [(i, i ^ k) for i in range(size)]) for k in range(1, size)
    ]


def halves_by_distance(half):
    place = lax.axis_index("blk")
    inner = (place == 1) | (place == 2)
    middle = [(1, 2), (2, 1)]
    outward = [(1, 0), (2, 3)]
    first = lax.ppermute(half, "blk", [(0, 1), (1, 0), (2, 3), (3, 2)])
    across = lax.ppermute(half, "blk", middle)
    across_out = lax.ppermute(across, "blk", outward)
    first_over = lax.ppermute(first, "blk", middle)
    first_out = lax.ppermute(first_over, "blk", outward)
    return [
        first,
        jnp.where(inner, first_over, across_out),
        jnp.where(inner, across, first_out),
    ]


def precondition(in_rows, eig_rows, out_query):
    row_count = in_rows.shape[0]
    basis_width = out_query.shape[0]
    query_count = out_query.shape[1] // R
    outer_sum = jnp.einsum(
        "jqr,iqr->qji",
        in_rows.reshape(row_count, query_count, R),
        out_query.reshape(basis_width, query_count, R),
        preferred_element_type=jnp.float32,
    )
    inverse = 1.0 / (eig_rows.astype(jnp.float32) + damping)
    return (outer_sum * inverse[None, :, :]).astype(jnp.bfloat16)


def on_device(acts, out_grads, basis_in, basis_out, eigvals, query_out, query_in, seq_ids, owner):
    rows = basis_in.shape[0]
    group = lax.axis_index("groups")
    stepped = lax.axis_size("blk") == 4 and lax.axis_size("groups") == 2

    if stepped:
        half = lax.dynamic_slice_in_dim(basis_in, group * (rows // 2), rows // 2, 0)
        own_way = halves_by_distance(half)
        swap = [(0, 1), (1, 0)]
        other_way = [lax.ppermute(piece, "groups", swap) for piece in own_way]

    in_part = jnp.dot(basis_in, query_in, preferred_element_type=jnp.float32)
    out_part = jnp.dot(basis_out, query_out, preferred_element_type=jnp.float32)
    small = jnp.concatenate([in_part, out_part], axis=0)
    small = swap_sum(swap_sum(small, "rep", jnp.float32), "eig", jnp.float32).astype(jnp.bfloat16)
    in_query, out_query = small[:rows], small[rows:]
    grad_part = contract_last(out_grads, basis_out)
    grad_proj = swap_sum(swap_sum(grad_part, "rep", jnp.float32), "eig", jnp.bfloat16)
    grad_proj = grad_proj.astype(jnp.bfloat16)

    if stepped:
        pack = jnp.concatenate([in_query, eigvals], axis=1)
        swapped = jnp.concatenate([pack[rows // 2 :], pack[: rows // 2]], axis=0)
        ordered = jnp.where(group == 0, pack, swapped)
        pack = jnp.concatenate([pack] + by_distance(ordered)[1:], axis=0)
        pieces = [basis_in]
        for mine, theirs in zip(own_way, other_way):
            pieces += [mine, theirs]
    else:
        pack = jnp.concatenate([in_query, eigvals], axis=1)
        pack = lax.all_gather(pack, "blk", axis=0, tiled=True)
        pieces = [lax.all_gather(basis_in, "blk", axis=0, tiled=True)]
    pairs = in_query.shape[1]
    weighted = precondition(pack[:, :pairs], pack[:, pairs:], out_query)
    query_count = weighted.shape[0]
    mixed = [contract_last(grad_proj, weighted[q]) for q in range(query_count)]

    projected = jnp.concatenate([contract_last(acts, piece) for piece in pieces], axis=1)
    per_token = jnp.stack([jnp.sum(projected * mixed[q], axis=1) for q in range(query_count)])

    seq_count = owner.shape[0]
    labels = jnp.arange(seq_count, dtype=jnp.int32)
    column_of = jnp.sum(jnp.where(seq_ids[None, :] == labels[:, None], owner[:, None], 0), axis=0)
    onehot = (labels[:, None] == column_of[None, :]).astype(jnp.float32)
    part_scores = lax.dot_general(
        per_token,
        onehot,
        (((1,), (1,)), ((), ())),
        precision=lax.Precision.HIGHEST,
        preferred_element_type=jnp.float32,
    )
    scores = lax.psum(part_scores, ("blk", "eig", "rep"))
    own_queries = query_count // lax.axis_size(("eig", "rep"))
    own_columns = seq_count // lax.axis_size("blk")
    return lax.dynamic_slice(
        scores,
        (lax.axis_index(("eig", "rep")) * own_queries, lax.axis_index("blk") * own_columns),
        (own_queries, own_columns),
    )


def solution(mesh):
    return jax.shard_map(
        on_device,
        mesh=mesh,
        in_specs=(
            P(("groups", "blk"), ("eig", "rep")),
            P(("groups", "blk"), ("eig", "rep")),
            P("blk", ("eig", "rep")),
            P(None, ("eig", "rep")),
            P("blk", None),
            P(("eig", "rep"), "groups"),
            P(("eig", "rep"), "groups"),
            P(("groups", "blk")),
            P("groups"),
        ),
        out_specs=P(("groups", "eig", "rep"), "blk"),
        check_vma=False,
    )
```

```python
import functools

import jax
import jax.numpy as jnp
from jax import lax
from jax.experimental import pallas as pl
from jax.experimental.pallas import tpu as pltpu
from jax.sharding import PartitionSpec as P

R = 32
LANES = 128
BLOCK = 256
VMEM_LIMIT = 24 * 1024 * 1024
AXES = ("groups", "blk", "eig", "rep")


damping = 0.05


def contract_last(left_side, right_side, precision=None):
    return lax.dot_general(
        left_side,
        right_side,
        (((1,), (1,)), ((), ())),
        precision=precision,
        preferred_element_type=jnp.float32,
    )


def swap_sum(value, axis, send_as):
    size = lax.axis_size(axis)
    if size & (size - 1):
        return lax.psum(value, axis)
    step = 1
    while step < size:
        pairs = [(i, i ^ step) for i in range(size)]
        value = value + lax.ppermute(value.astype(send_as), axis, pairs).astype(jnp.float32)
        step *= 2
    return value


def by_distance(value, axis="blk"):
    size = lax.axis_size(axis)
    return [value] + [
        lax.ppermute(value, axis, [(i, i ^ k) for i in range(size)]) for k in range(1, size)
    ]


def held(value, *until):
    return lax.optimization_barrier((value, *until))[0]


def half_kernel(whole_ref, half_ref, copied):
    columns = half_ref.shape[1]
    start = pl.multiple_of(lax.axis_index("groups") * columns, LANES)
    copy = pltpu.make_async_copy(whole_ref.at[:, pl.ds(start, columns)], half_ref, copied)
    copy.start()
    copy.wait()


def take_half(whole):
    rows, columns = whole.shape
    return pl.pallas_call(
        half_kernel,
        in_specs=[pl.BlockSpec(memory_space=pl.ANY)],
        out_specs=pl.BlockSpec(memory_space=pltpu.VMEM),
        out_shape=jax.ShapeDtypeStruct((rows, columns // 2), whole.dtype),
        scratch_shapes=[pltpu.SemaphoreType.DMA],
    )(whole)


def parts_kernel(in_ref, in_query_ref, out_ref, out_query_ref, grads_ref, sum_ref):
    rows, width = in_ref.shape[0], out_ref.shape[0]
    sum_ref[:rows] = jnp.dot(in_ref[...], in_query_ref[...], preferred_element_type=jnp.float32)
    sum_ref[rows : rows + width] = jnp.dot(
        out_ref[...], out_query_ref[...], preferred_element_type=jnp.float32
    )
    tokens = grads_ref.shape[0]
    block = tokens // 3 if tokens % 48 == 0 else tokens

    @pl.loop(0, tokens // block)
    def _(step):
        start = pl.multiple_of(step * block, 16)
        sum_ref[pl.ds(rows + width + start, block), :] = contract_last(
            grads_ref[pl.ds(start, block), :], out_ref[...]
        )


def small_parts(basis_in, query_in, basis_out, query_out, out_grads):
    high = basis_in.shape[0] + basis_out.shape[0] + out_grads.shape[0]
    return pl.pallas_call(
        parts_kernel,
        out_shape=jax.ShapeDtypeStruct((high, query_in.shape[1]), jnp.float32),
        compiler_params=pltpu.CompilerParams(vmem_limit_bytes=VMEM_LIMIT),
    )(basis_in, query_in, basis_out, query_out, out_grads)


def weigh(query_count, packs, out_query, weighted_ref):
    rows, pairs = packs[0].shape[0], out_query.shape[1]
    query_of = lax.broadcasted_iota(jnp.int32, (rows, pairs), 1) // R
    for slot, pack_ref in enumerate(packs):
        in_query = pack_ref[:, :pairs].astype(jnp.float32)
        inverse = 1.0 / (pack_ref[:, pairs:].astype(jnp.float32) + damping)
        for query in range(query_count):
            own = jnp.where(query_of == query, in_query, 0.0).astype(jnp.bfloat16)
            outer_sum = contract_last(own, out_query)
            weighted_ref[slot, pl.ds(query * rows, rows), :] = (outer_sum * inverse).astype(
                jnp.bfloat16
            )


def score_block(acts_ref, tokens, start, columns, pieces, slots, grad_ref, weighted_ref, onehot_ref):
    rows = pieces[0].shape[0]
    copies = LANES // rows
    stacked = jnp.concatenate([piece[...] for piece in pieces for _ in range(copies)], axis=0)
    projected = contract_last(acts_ref[pl.ds(start, tokens), columns], stacked)
    grad = grad_ref[pl.ds(start, tokens), :]
    onehot = onehot_ref[:, pl.ds(start, tokens)]
    summed = 0.0
    for place, slot in enumerate(slots):
        mixed = contract_last(grad, weighted_ref[slot])
        own = projected[:, place * LANES : (place + 1) * LANES]
        product = jnp.concatenate([own] * (mixed.shape[1] // LANES), axis=1) * mixed
        high = product.astype(jnp.bfloat16)
        low = (product - high.astype(jnp.float32)).astype(jnp.bfloat16)
        summed += jnp.dot(onehot, high, preferred_element_type=jnp.float32)
        summed += jnp.dot(onehot, low, preferred_element_type=jnp.float32)
    return summed


def score_kernel(parts, query_count, make_weights, last, acts_ref, grad_ref, onehot_ref, *refs):
    counts = [len(slots) for slots, _ in parts]
    pieces = [refs[sum(counts[:i]) : sum(counts[: i + 1])] for i in range(len(parts))]
    refs = refs[sum(counts) :]
    if make_weights:
        packs, out_query_ref, out_ref, weighted_ref = refs[:-3], *refs[-3:]
        weigh(query_count, packs, out_query_ref[...], weighted_ref)
        before = jnp.zeros(out_ref.shape, jnp.float32)
    else:
        weighted_ref, before_ref, out_ref = refs
        before = before_ref[...]
    block = BLOCK
    group = lax.axis_index("groups")

    def add_block(step, summed):
        start = pl.multiple_of(step * block, LANES)
        for (slots, which), own in zip(parts, pieces):
            columns = slice(None)
            if which != "all":
                width = own[0].shape[1]
                half = group if which == "here" else 1 - group
                columns = pl.ds(pl.multiple_of(half * width, LANES), width)
            summed = summed + score_block(
                acts_ref, block, start, columns, own, slots, grad_ref, weighted_ref, onehot_ref
            )
        return summed

    summed = lax.fori_loop(0, acts_ref.shape[0] // block, add_block, before)
    if last:
        width = summed.shape[1]
        query_of = lax.broadcasted_iota(jnp.int32, (query_count, width), 1) // (
            width // query_count
        )
        chosen = query_of == lax.broadcasted_iota(jnp.int32, (query_count, width), 0)
        out_ref[...] = contract_last(
            chosen.astype(jnp.float32), summed, precision=lax.Precision.HIGHEST
        )
    else:
        out_ref[...] = summed


def add_scores(acts, grad_proj, onehot, parts, pieces, more, query_count, last=False):
    seq_count = onehot.shape[0]
    first = isinstance(more[0], list)
    rows = pieces[0].shape[0]
    width = query_count * rows
    out_shape = jax.ShapeDtypeStruct((query_count, seq_count) if last else (seq_count, width), jnp.float32)
    if first:
        weights = jax.ShapeDtypeStruct((len(more[0]), width, more[1].shape[0]), jnp.bfloat16)
        out_shape = [out_shape, weights]
        more = [*more[0], more[1]]
    flops = 2 * sum(piece.shape[1] for piece in pieces) * acts.shape[0] * LANES
    return pl.pallas_call(
        functools.partial(score_kernel, parts, query_count, first, last),
        out_shape=out_shape,
        compiler_params=pltpu.CompilerParams(vmem_limit_bytes=VMEM_LIMIT),
        cost_estimate=pl.CostEstimate(flops=flops, bytes_accessed=acts.shape[0] * 1024, transcendentals=0),
    )(acts, grad_proj, onehot, *pieces, *more)


def precondition(in_rows, eig_rows, out_query):
    row_count = in_rows.shape[0]
    basis_width = out_query.shape[0]
    query_count = out_query.shape[1] // R
    outer_sum = jnp.einsum(
        "jqr,iqr->qji",
        in_rows.reshape(row_count, query_count, R),
        out_query.reshape(basis_width, query_count, R),
        preferred_element_type=jnp.float32,
    )
    inverse = 1.0 / (eig_rows.astype(jnp.float32) + damping)
    return (outer_sum * inverse[None, :, :]).astype(jnp.bfloat16)


def plain_scores(acts, basis_in, pack, out_query, grad_proj, onehot):
    pack = lax.all_gather(pack, "blk", axis=0, tiled=True)
    piece = lax.all_gather(basis_in, "blk", axis=0, tiled=True)
    pairs = out_query.shape[1]
    weighted = precondition(pack[:, :pairs], pack[:, pairs:], out_query)
    projected = contract_last(acts, piece)
    per_token = jnp.stack(
        [jnp.sum(projected * contract_last(grad_proj, slab), axis=1) for slab in weighted]
    )
    return contract_last(per_token, onehot, precision=lax.Precision.HIGHEST)


def to_send(part, split):
    high = lax.reduce_precision(part[:split], 8, 7)
    low = part[:split] - high
    return jnp.concatenate([high, low, part[split:]], axis=0).astype(jnp.bfloat16)


def add_sent(part, other, split):
    high, low, rest = other[:split], other[split : 2 * split], other[2 * split :]
    first = part[:split] + high.astype(jnp.float32) + low.astype(jnp.float32)
    return jnp.concatenate([first, part[split:] + rest.astype(jnp.float32)], axis=0)


def stepped_scores(
    acts, out_grads, basis_in, basis_out, eigvals, query_out, query_in, onehot
):
    rows, width = basis_in.shape[0], basis_out.shape[0]
    query_count = query_in.shape[1] // R
    place = lax.axis_index("blk")
    inner = (place == 1) | (place == 2)
    pair = [(0, 1), (1, 0)]
    middle = [(1, 2), (2, 1)]
    outward = [(1, 0), (2, 3)]
    along = functools.partial(lax.ppermute, axis_name="blk")
    swapped = functools.partial(lax.ppermute, axis_name="groups", perm=pair)

    half = take_half(basis_in)
    mine_1 = along(half, perm=[(0, 1), (1, 0), (2, 3), (3, 2)])
    across = along(half, perm=middle)

    split = rows + width
    part = small_parts(held(basis_in, half), query_in, basis_out, query_out, out_grads)
    other = lax.ppermute(to_send(part, split), "rep", pair)
    part = add_sent(part, held(other, mine_1, across), split)
    other = lax.ppermute(to_send(part, split), "eig", pair)
    part = add_sent(part, other, split).astype(jnp.bfloat16)
    in_query, out_query, grad_proj = part[:rows], part[rows:split], part[split:]

    first_over = along(mine_1, perm=middle)
    across_out = along(across, perm=outward)
    theirs_1 = swapped(mine_1)

    in_query = held(in_query, first_over, across_out)
    packs = by_distance(jnp.concatenate([in_query, eigvals], axis=1))

    mine_2 = jnp.where(inner, first_over, held(across_out, theirs_1))
    theirs_2 = swapped(mine_2)
    first_out = along(first_over, perm=outward)

    add = functools.partial(add_scores, acts, grad_proj, onehot, query_count=query_count)
    sums, weights = add([((0,), "all")], [basis_in], (packs, out_query))
    sums = add([((1, 2), "here")], [mine_1, mine_2], (weights, sums))
    mine_3 = jnp.where(inner, across, held(first_out, sums))
    theirs_3 = swapped(mine_3)
    sums = add(
        [((1, 2), "there"), ((3,), "here")], [theirs_1, theirs_2, mine_3], (weights, sums)
    )
    scores = add([((3,), "there")], [theirs_3], (weights, sums), last=True)
    for axis in (("eig", "rep"), "blk"):
        scores = sum(by_distance(scores, axis))
    return scores


def plain_path(acts, out_grads, basis_in, basis_out, eigvals, query_out, query_in, onehot):
    def whole_sum(part, send_as):
        return swap_sum(swap_sum(part, "rep", jnp.float32), "eig", send_as).astype(jnp.bfloat16)

    in_query = whole_sum(jnp.dot(basis_in, query_in, preferred_element_type=jnp.float32), jnp.float32)
    out_query = whole_sum(
        jnp.dot(basis_out, query_out, preferred_element_type=jnp.float32), jnp.float32
    )
    grad_proj = whole_sum(contract_last(out_grads, basis_out), jnp.bfloat16)
    pack = jnp.concatenate([in_query, eigvals], axis=1)
    scores = plain_scores(acts, basis_in, pack, out_query, grad_proj, onehot.astype(jnp.float32))
    return lax.psum(scores, ("blk", "eig", "rep"))


def on_device(acts, out_grads, basis_in, basis_out, eigvals, query_out, query_in, seq_ids, owner):
    rows, features = basis_in.shape
    pairs = query_in.shape[1]
    seq_count = owner.shape[0]
    labels = jnp.arange(seq_count, dtype=jnp.int32)
    column_of = jnp.sum(jnp.where(seq_ids[None, :] == labels[:, None], owner[:, None], 0), axis=0)
    onehot = (labels[:, None] == column_of[None, :]).astype(jnp.bfloat16)
    stepped = (
        all(lax.axis_size(axis) == size for axis, size in zip(AXES, (2, 4, 2, 2)))
        and LANES % rows == 0
        and (pairs // R * rows) % LANES == 0
        and features % (2 * LANES) == 0
        and acts.shape[0] % BLOCK == 0
        and pairs == basis_out.shape[0] == LANES
    )
    way = stepped_scores if stepped else plain_path
    scores = way(acts, out_grads, basis_in, basis_out, eigvals, query_out, query_in, onehot)
    own_queries = pairs // R // lax.axis_size(("eig", "rep"))
    own_columns = seq_count // lax.axis_size("blk")
    return lax.dynamic_slice(
        scores,
        (lax.axis_index(("eig", "rep")) * own_queries, lax.axis_index("blk") * own_columns),
        (own_queries, own_columns),
    )


def solution(mesh):
    return jax.shard_map(
        on_device,
        mesh=mesh,
        in_specs=(
            P(("groups", "blk"), ("eig", "rep")),
            P(("groups", "blk"), ("eig", "rep")),
            P("blk", ("eig", "rep")),
            P(None, ("eig", "rep")),
            P("blk", None),
            P(("eig", "rep"), "groups"),
            P(("eig", "rep"), "groups"),
            P(("groups", "blk")),
            P("groups"),
        ),
        out_specs=P(("groups", "eig", "rep"), "blk"),
        check_vma=False,
    )
```

```python
import functools

import jax
import jax.numpy as jnp
from jax import lax
from jax.experimental import pallas as pl
from jax.experimental.pallas import tpu as pltpu
from jax.sharding import PartitionSpec as P

R = 32
LANES = 128
BLOCK = 256
VMEM_LIMIT = 16 * 1024 * 1024
AXES = ("groups", "blk", "eig", "rep")


damping = 0.05


def contract_last(left_side, right_side, precision=None):
    return lax.dot_general(
        left_side,
        right_side,
        (((1,), (1,)), ((), ())),
        precision=precision,
        preferred_element_type=jnp.float32,
    )


def swap_sum(value, axis, send_as):
    size = lax.axis_size(axis)
    if size & (size - 1):
        return lax.psum(value, axis)
    step = 1
    while step < size:
        pairs = [(i, i ^ step) for i in range(size)]
        value = value + lax.ppermute(value.astype(send_as), axis, pairs).astype(jnp.float32)
        step *= 2
    return value


def by_distance(value, axis="blk"):
    size = lax.axis_size(axis)
    return [value] + [
        lax.ppermute(value, axis, [(i, i ^ k) for i in range(size)]) for k in range(1, size)
    ]


def held(value, *until):
    return lax.optimization_barrier((value, *until))[0]


def in_hbm(value):
    return pltpu.with_memory_space_constraint(value, pltpu.HBM)


def parts_kernel(*refs):
    sources, half_ref, sum_ref, copied = refs[:5], refs[5], refs[6], refs[-1]
    held_refs = out_ref, out_query_ref, in_ref, in_query_ref, grads_ref = refs[7:-1]
    columns = half_ref.shape[1]
    begin = pl.multiple_of(lax.axis_index("groups") * columns, LANES)
    moves = [(sources[2].at[:, pl.ds(begin, columns)], half_ref), *zip(sources, held_refs)]
    copies = [
        pltpu.make_async_copy(source, target, copied.at[place])
        for place, (source, target) in enumerate(moves)
    ]
    for copy in copies:
        copy.start()
    rows, width = in_ref.shape[0], out_ref.shape[0]
    copies[1].wait()
    copies[2].wait()
    sum_ref[rows : rows + width] = jnp.dot(
        out_ref[...], out_query_ref[...], preferred_element_type=jnp.float32
    )
    copies[3].wait()
    copies[4].wait()
    sum_ref[:rows] = jnp.dot(in_ref[...], in_query_ref[...], preferred_element_type=jnp.float32)
    copies[5].wait()

    @pl.loop(0, grads_ref.shape[0] // BLOCK)
    def _(step):
        start = pl.multiple_of(step * BLOCK, LANES)
        sum_ref[pl.ds(rows + width + start, BLOCK), :] = contract_last(
            grads_ref[pl.ds(start, BLOCK), :], out_ref[...]
        )

    copies[0].wait()


def small_parts(basis_in, query_in, basis_out, query_out, out_grads):
    rows, features = basis_in.shape
    high = rows + basis_out.shape[0] + out_grads.shape[0]
    sources = (basis_out, query_out, basis_in, query_in, out_grads)
    return pl.pallas_call(
        parts_kernel,
        in_specs=[pl.BlockSpec(memory_space=pl.ANY)] * len(sources),
        out_shape=[
            pltpu.VMEM((rows, features // 2), basis_in.dtype),
            jax.ShapeDtypeStruct((high, query_in.shape[1]), jnp.float32),
        ],
        scratch_shapes=[pltpu.VMEM(source.shape, source.dtype) for source in sources]
        + [pltpu.SemaphoreType.DMA((len(sources) + 1,))],
        compiler_params=pltpu.CompilerParams(vmem_limit_bytes=VMEM_LIMIT),
    )(*[in_hbm(source) for source in sources])


def weigh(query_count, packs, out_query, weighted_ref):
    rows, pairs = packs[0].shape[0], out_query.shape[1]
    query_of = lax.broadcasted_iota(jnp.int32, (rows, pairs), 1) // R
    for slot, pack_ref in enumerate(packs):
        in_query = pack_ref[:, :pairs].astype(jnp.float32)
        inverse = 1.0 / (pack_ref[:, pairs:].astype(jnp.float32) + damping)
        for query in range(query_count):
            own = jnp.where(query_of == query, in_query, 0.0).astype(jnp.bfloat16)
            outer_sum = contract_last(own, out_query)
            weighted_ref[slot, pl.ds(query * rows, rows), :] = (outer_sum * inverse).astype(
                jnp.bfloat16
            )


def project(acts_ref, start, piece, group, first=0):
    rows, width = piece.shape
    columns = slice(None)
    if width < acts_ref.shape[1]:
        half = acts_ref.shape[1] // 2
        columns = pl.ds(pl.multiple_of(group * half + first, LANES), width)
    repeated = jnp.concatenate([piece[...]] * (LANES // rows), axis=0)
    return contract_last(acts_ref[pl.ds(start, BLOCK), columns], repeated)


def mix(start, projected, weights, grad_ref, onehot_ref):
    mixed = contract_last(grad_ref[pl.ds(start, BLOCK), :], weights)
    product = jnp.concatenate([projected] * (mixed.shape[1] // LANES), axis=1) * mixed
    high = product.astype(jnp.bfloat16)
    low = (product - high.astype(jnp.float32)).astype(jnp.bfloat16)
    onehot = onehot_ref[:, pl.ds(start, BLOCK)]
    return jnp.dot(onehot, high, preferred_element_type=jnp.float32) + jnp.dot(
        onehot, low, preferred_element_type=jnp.float32
    )


def blocks(acts_or_projected, body, initial):
    def step(index, carry):
        return body(pl.multiple_of(index * BLOCK, LANES), carry)

    return lax.fori_loop(0, acts_or_projected.shape[0] // BLOCK, step, initial)


def first_kernel(source_ref, own_ref, acts_ref, total_ref, copied):
    copies = [
        pltpu.make_async_copy(
            source_ref.at[pl.ds(start, BLOCK)], acts_ref.at[pl.ds(start, BLOCK)], copied.at[place]
        )
        for place, start in enumerate(range(0, acts_ref.shape[0], BLOCK))
    ]
    for copy in copies:
        copy.start()
    for place, copy in enumerate(copies):
        copy.wait()
        start = place * BLOCK
        total_ref[pl.ds(start, BLOCK), :] = project(acts_ref, start, own_ref, 0)


def weight_kernel(query_count, *refs):
    packs, refs = refs[:4], refs[4:]
    out_query_ref, grad_ref, onehot_ref, total_ref, sums_ref, weights_ref = refs
    weigh(query_count, packs, out_query_ref[...], weights_ref)

    def body(start, sums):
        total = total_ref[pl.ds(start, BLOCK), :]
        return sums + mix(start, total, weights_ref[0], grad_ref, onehot_ref)

    sums_ref[...] = blocks(total_ref, body, jnp.zeros(sums_ref.shape, jnp.float32))


def slot_kernel(
    slot, acts_ref, mine_ref, theirs_ref, weights_ref, grad_ref, onehot_ref, before_ref, sums_ref
):
    group = lax.axis_index("groups")

    def body(start, sums):
        total = project(acts_ref, start, mine_ref, group)
        total = total + project(acts_ref, start, theirs_ref, 1 - group)
        return sums + mix(start, total, weights_ref[slot], grad_ref, onehot_ref)

    sums_ref[...] = blocks(acts_ref, body, before_ref[...])


def mine_kernel(acts_ref, mine_ref, total_ref):
    group = lax.axis_index("groups")

    def body(start, carry):
        total_ref[pl.ds(start, BLOCK), :] = project(acts_ref, start, mine_ref, group)
        return carry

    blocks(acts_ref, body, 0)


def last_kernel(
    acts_ref, left_ref, right_ref, total_ref, weights_ref, grad_ref, onehot_ref, before_ref, out_ref
):
    other = 1 - lax.axis_index("groups")

    def body(start, sums):
        total = total_ref[pl.ds(start, BLOCK), :]
        total = total + project(acts_ref, start, left_ref, other)
        total = total + project(acts_ref, start, right_ref, other, left_ref.shape[1])
        return sums + mix(start, total, weights_ref[3], grad_ref, onehot_ref)

    sums = blocks(acts_ref, body, before_ref[...])
    queries, width = out_ref.shape[0], sums.shape[1]
    query_of = lax.broadcasted_iota(jnp.int32, (queries, width), 1) // (width // queries)
    chosen = query_of == lax.broadcasted_iota(jnp.int32, (queries, width), 0)
    out_ref[...] = contract_last(chosen.astype(jnp.float32), sums, precision=lax.Precision.HIGHEST)


def call(kernel, out_shape, *operands, **options):
    return pl.pallas_call(
        kernel,
        out_shape=out_shape,
        compiler_params=pltpu.CompilerParams(vmem_limit_bytes=VMEM_LIMIT),
        cost_estimate=pl.CostEstimate(flops=1, bytes_accessed=1, transcendentals=0),
        **options,
    )(*operands)


def precondition(in_rows, eig_rows, out_query):
    row_count = in_rows.shape[0]
    basis_width = out_query.shape[0]
    query_count = out_query.shape[1] // R
    outer_sum = jnp.einsum(
        "jqr,iqr->qji",
        in_rows.reshape(row_count, query_count, R),
        out_query.reshape(basis_width, query_count, R),
        preferred_element_type=jnp.float32,
    )
    inverse = 1.0 / (eig_rows.astype(jnp.float32) + damping)
    return (outer_sum * inverse[None, :, :]).astype(jnp.bfloat16)


def plain_scores(acts, basis_in, pack, out_query, grad_proj, onehot):
    pack = lax.all_gather(pack, "blk", axis=0, tiled=True)
    piece = lax.all_gather(basis_in, "blk", axis=0, tiled=True)
    pairs = out_query.shape[1]
    weighted = precondition(pack[:, :pairs], pack[:, pairs:], out_query)
    projected = contract_last(acts, piece)
    per_token = jnp.stack(
        [jnp.sum(projected * contract_last(grad_proj, slab), axis=1) for slab in weighted]
    )
    return contract_last(per_token, onehot, precision=lax.Precision.HIGHEST)


def to_send(part, split):
    high = lax.reduce_precision(part[:split], 8, 7)
    low = part[:split] - high
    return jnp.concatenate([high, low, part[split:]], axis=0).astype(jnp.bfloat16)


def add_sent(part, other, split):
    high, low, rest = other[:split], other[split : 2 * split], other[2 * split :]
    first = part[:split] + high.astype(jnp.float32) + low.astype(jnp.float32)
    return jnp.concatenate([first, part[split:] + rest.astype(jnp.float32)], axis=0)


def stepped_scores(
    acts, out_grads, basis_in, basis_out, eigvals, query_out, query_in, onehot
):
    rows, width = basis_in.shape[0], basis_out.shape[0]
    tokens, seq_count = acts.shape[0], onehot.shape[0]
    query_count = query_in.shape[1] // R
    pair = [(0, 1), (1, 0)]

    def along(value, distance):
        return lax.ppermute(value, "blk", [(i, i ^ distance) for i in range(4)])

    def swapped(value):
        return lax.ppermute(value, "groups", pair)

    half, part = small_parts(basis_in, query_in, basis_out, query_out, out_grads)
    mine_1 = along(half, 1)
    mine_2 = along(half, 2)

    split = rows + width
    other = lax.ppermute(to_send(part, split), "rep", pair)
    part = add_sent(part, held(other, mine_1), split)
    other = lax.ppermute(to_send(part, split), "eig", pair)
    theirs_1 = swapped(mine_1)
    acts, total = call(
        first_kernel,
        [pltpu.VMEM(acts.shape, acts.dtype), jax.ShapeDtypeStruct((tokens, LANES), jnp.float32)],
        in_hbm(held(acts, mine_1)),
        basis_in,
        in_specs=[pl.BlockSpec(memory_space=pl.ANY), pl.BlockSpec(memory_space=pltpu.VMEM)],
        scratch_shapes=[pltpu.SemaphoreType.DMA((tokens // BLOCK,))],
    )
    mine_2 = held(mine_2, theirs_1, other, total)
    part = add_sent(part, held(other, mine_2), split).astype(jnp.bfloat16)
    in_query, out_query, grad_proj = part[:rows], part[rows:split], part[split:]
    packs = by_distance(jnp.concatenate([in_query, eigvals], axis=1))

    theirs_2 = swapped(mine_2)
    mine_3 = along(mine_2, 1)
    sums_shape = jax.ShapeDtypeStruct((seq_count, query_count * rows), jnp.float32)
    weights_shape = jax.ShapeDtypeStruct((4, query_count * rows, width), jnp.bfloat16)
    sums, weights = call(
        functools.partial(weight_kernel, query_count),
        [sums_shape, weights_shape],
        *packs, out_query, grad_proj, onehot, total,
    )
    fixed = (weights, grad_proj, onehot)
    sums = call(
        functools.partial(slot_kernel, 1), sums_shape, acts, mine_1, theirs_1, *fixed, sums
    )

    middle = mine_3.shape[1] // 2
    left_3 = along(held(theirs_2, sums)[:, :middle], 1)
    right_3 = swapped(held(mine_3, sums)[:, middle:])
    sums = call(
        functools.partial(slot_kernel, 2), sums_shape, acts, mine_2, theirs_2, *fixed, sums
    )
    total = call(mine_kernel, jax.ShapeDtypeStruct((tokens, LANES), jnp.float32), acts, mine_3)
    scores = call(
        last_kernel,
        jax.ShapeDtypeStruct((query_count, seq_count), jnp.float32),
        acts, left_3, right_3, total, *fixed, sums,
    )
    return swap_sum(sum(by_distance(scores, ("eig", "rep"))), "blk", jnp.float32)


def plain_path(acts, out_grads, basis_in, basis_out, eigvals, query_out, query_in, onehot):
    def whole_sum(part, send_as):
        return swap_sum(swap_sum(part, "rep", jnp.float32), "eig", send_as).astype(jnp.bfloat16)

    in_query = whole_sum(jnp.dot(basis_in, query_in, preferred_element_type=jnp.float32), jnp.float32)
    out_query = whole_sum(
        jnp.dot(basis_out, query_out, preferred_element_type=jnp.float32), jnp.float32
    )
    grad_proj = whole_sum(contract_last(out_grads, basis_out), jnp.bfloat16)
    pack = jnp.concatenate([in_query, eigvals], axis=1)
    scores = plain_scores(acts, basis_in, pack, out_query, grad_proj, onehot.astype(jnp.float32))
    return lax.psum(scores, ("blk", "eig", "rep"))


def on_device(acts, out_grads, basis_in, basis_out, eigvals, query_out, query_in, seq_ids, owner):
    rows, features = basis_in.shape
    pairs = query_in.shape[1]
    seq_count = owner.shape[0]
    labels = jnp.arange(seq_count, dtype=jnp.int32)
    column_of = jnp.sum(jnp.where(seq_ids[None, :] == labels[:, None], owner[:, None], 0), axis=0)
    onehot = (labels[:, None] == column_of[None, :]).astype(jnp.bfloat16)
    stepped = (
        all(lax.axis_size(axis) == size for axis, size in zip(AXES, (2, 4, 2, 2)))
        and LANES % rows == 0
        and (pairs // R * rows) % LANES == 0
        and features % (4 * LANES) == 0
        and acts.shape[0] % BLOCK == 0
        and pairs == basis_out.shape[0] == LANES
    )
    way = stepped_scores if stepped else plain_path
    scores = way(acts, out_grads, basis_in, basis_out, eigvals, query_out, query_in, onehot)
    own_queries = pairs // R // lax.axis_size(("eig", "rep"))
    own_columns = seq_count // lax.axis_size("blk")
    return lax.dynamic_slice(
        scores,
        (lax.axis_index(("eig", "rep")) * own_queries, lax.axis_index("blk") * own_columns),
        (own_queries, own_columns),
    )


def solution(mesh):
    return jax.shard_map(
        on_device,
        mesh=mesh,
        in_specs=(
            P(("groups", "blk"), ("eig", "rep")),
            P(("groups", "blk"), ("eig", "rep")),
            P("blk", ("eig", "rep")),
            P(None, ("eig", "rep")),
            P("blk", None),
            P(("eig", "rep"), "groups"),
            P(("eig", "rep"), "groups"),
            P(("groups", "blk")),
            P("groups"),
        ),
        out_specs=P(("groups", "eig", "rep"), "blk"),
        check_vma=False,
    )
```

```python
import functools
import itertools

import jax
import jax.numpy as jnp
from jax import lax
from jax.experimental import pallas as pl
from jax.experimental.pallas import tpu as pltpu
from jax.sharding import PartitionSpec as P

R = 32
LANES = 128
BLOCK = 256
VMEM_LIMIT = 16 * 1024 * 1024
AXES = ("groups", "blk", "eig", "rep")


damping = 0.05


def contract_last(left_side, right_side, precision=None):
    return lax.dot_general(
        left_side,
        right_side,
        (((1,), (1,)), ((), ())),
        precision=precision,
        preferred_element_type=jnp.float32,
    )


def swap_sum(value, axis, send_as):
    size = lax.axis_size(axis)
    if size & (size - 1):
        return lax.psum(value, axis)
    step = 1
    while step < size:
        pairs = [(i, i ^ step) for i in range(size)]
        value = value + lax.ppermute(value.astype(send_as), axis, pairs).astype(jnp.float32)
        step *= 2
    return value


def by_distance(value, axis="blk"):
    size = lax.axis_size(axis)
    return [value] + [
        lax.ppermute(value, axis, [(i, i ^ k) for i in range(size)]) for k in range(1, size)
    ]


def held(value, *until):
    return lax.optimization_barrier((value, *until))[0]


def in_hbm(value):
    return pltpu.with_memory_space_constraint(value, pltpu.HBM)


def in_vmem(value):
    return pltpu.with_memory_space_constraint(value, pltpu.VMEM)


def pairing(partner):
    sizes = [lax.axis_size(axis) for axis in AXES]
    places = list(itertools.product(*map(range, sizes)))
    return [(number, places.index(partner(*place))) for number, place in enumerate(places)]


def halves_kernel(whole_ref, mine_ref, other_ref, copied):
    columns = mine_ref.shape[1]
    group = lax.axis_index("groups")
    copies = [
        pltpu.make_async_copy(
            whole_ref.at[:, pl.ds(pl.multiple_of(half * columns, LANES), columns)],
            half_ref,
            copied.at[place],
        )
        for place, (half, half_ref) in enumerate([(group, mine_ref), (1 - group, other_ref)])
    ]
    for copy in copies:
        copy.start()
    for copy in copies:
        copy.wait()


def take_halves(whole):
    rows, columns = whole.shape
    half = pltpu.VMEM((rows, columns // 2), whole.dtype)
    return pl.pallas_call(
        halves_kernel,
        in_specs=[pl.BlockSpec(memory_space=pl.ANY)],
        out_shape=[half, half],
        scratch_shapes=[pltpu.SemaphoreType.DMA((2,))],
    )(in_hbm(whole))


def parts_kernel(*refs):
    sources, sum_ref, copied = refs[:5], refs[5], refs[-1]
    held_refs = out_ref, out_query_ref, in_ref, in_query_ref, grads_ref = refs[6:-1]
    copies = [
        pltpu.make_async_copy(source, target, copied.at[place])
        for place, (source, target) in enumerate(zip(sources, held_refs))
    ]
    for copy in copies:
        copy.start()
    rows, width = in_ref.shape[0], out_ref.shape[0]
    copies[0].wait()
    copies[1].wait()
    sum_ref[rows : rows + width] = jnp.dot(
        out_ref[...], out_query_ref[...], preferred_element_type=jnp.float32
    )
    copies[2].wait()
    copies[3].wait()
    sum_ref[:rows] = jnp.dot(in_ref[...], in_query_ref[...], preferred_element_type=jnp.float32)
    copies[4].wait()

    @pl.loop(0, grads_ref.shape[0] // BLOCK)
    def _(step):
        start = pl.multiple_of(step * BLOCK, LANES)
        sum_ref[pl.ds(rows + width + start, BLOCK), :] = contract_last(
            grads_ref[pl.ds(start, BLOCK), :], out_ref[...]
        )


def small_parts(basis_in, query_in, basis_out, query_out, out_grads):
    high = basis_in.shape[0] + basis_out.shape[0] + out_grads.shape[0]
    sources = (basis_out, query_out, basis_in, query_in, out_grads)
    return pl.pallas_call(
        parts_kernel,
        in_specs=[pl.BlockSpec(memory_space=pl.ANY)] * len(sources),
        out_shape=jax.ShapeDtypeStruct((high, query_in.shape[1]), jnp.float32),
        scratch_shapes=[pltpu.VMEM(source.shape, source.dtype) for source in sources]
        + [pltpu.SemaphoreType.DMA((len(sources),))],
        compiler_params=pltpu.CompilerParams(vmem_limit_bytes=VMEM_LIMIT),
    )(*[in_hbm(source) for source in sources])


def weigh(query_count, packs, out_query, weighted_ref):
    rows, pairs = packs[0].shape[0], out_query.shape[1]
    query_of = lax.broadcasted_iota(jnp.int32, (rows, pairs), 1) // R
    for slot, pack_ref in enumerate(packs):
        in_query = pack_ref[:, :pairs].astype(jnp.float32)
        inverse = 1.0 / (pack_ref[:, pairs:].astype(jnp.float32) + damping)
        for query in range(query_count):
            own = jnp.where(query_of == query, in_query, 0.0).astype(jnp.bfloat16)
            outer_sum = contract_last(own, out_query)
            weighted_ref[slot, pl.ds(query * rows, rows), :] = (outer_sum * inverse).astype(
                jnp.bfloat16
            )


def project(acts_ref, start, piece, group, first=0):
    rows, width = piece.shape
    columns = slice(None)
    if width < acts_ref.shape[1]:
        half = acts_ref.shape[1] // 2
        columns = pl.ds(pl.multiple_of(group * half + first, LANES), width)
    repeated = jnp.concatenate([piece[...]] * (LANES // rows), axis=0)
    return contract_last(acts_ref[pl.ds(start, BLOCK), columns], repeated)


def mix(start, projected, weights, grad_ref, onehot_ref):
    mixed = contract_last(grad_ref[pl.ds(start, BLOCK), :], weights)
    product = jnp.concatenate([projected] * (mixed.shape[1] // LANES), axis=1) * mixed
    high = product.astype(jnp.bfloat16)
    low = (product - high.astype(jnp.float32)).astype(jnp.bfloat16)
    onehot = onehot_ref[:, pl.ds(start, BLOCK)]
    return jnp.dot(onehot, high, preferred_element_type=jnp.float32) + jnp.dot(
        onehot, low, preferred_element_type=jnp.float32
    )


def blocks(acts_or_projected, body, initial):
    def step(index, carry):
        return body(pl.multiple_of(index * BLOCK, LANES), carry)

    return lax.fori_loop(0, acts_or_projected.shape[0] // BLOCK, step, initial)


def first_kernel(source_ref, own_ref, acts_ref, total_ref, copied):
    copies = [
        pltpu.make_async_copy(
            source_ref.at[pl.ds(start, BLOCK)], acts_ref.at[pl.ds(start, BLOCK)], copied.at[place]
        )
        for place, start in enumerate(range(0, acts_ref.shape[0], BLOCK))
    ]
    for copy in copies:
        copy.start()
    for place, copy in enumerate(copies):
        copy.wait()
        start = place * BLOCK
        total_ref[pl.ds(start, BLOCK), :] = project(acts_ref, start, own_ref, 0)


def weight_kernel(query_count, *refs):
    packs, refs = refs[:4], refs[4:]
    out_query_ref, grad_ref, onehot_ref, total_ref, sums_ref, weights_ref = refs
    weigh(query_count, packs, out_query_ref[...], weights_ref)

    def body(start, sums):
        total = total_ref[pl.ds(start, BLOCK), :]
        return sums + mix(start, total, weights_ref[0], grad_ref, onehot_ref)

    sums_ref[...] = blocks(total_ref, body, jnp.zeros(sums_ref.shape, jnp.float32))


def slot_kernel(
    slot, acts_ref, mine_ref, theirs_ref, weights_ref, grad_ref, onehot_ref, before_ref, sums_ref
):
    group = lax.axis_index("groups")

    def body(start, sums):
        total = project(acts_ref, start, mine_ref, group)
        total = total + project(acts_ref, start, theirs_ref, 1 - group)
        return sums + mix(start, total, weights_ref[slot], grad_ref, onehot_ref)

    sums_ref[...] = blocks(acts_ref, body, before_ref[...])


def mine_kernel(acts_ref, mine_ref, total_ref):
    group = lax.axis_index("groups")

    def body(start, carry):
        total_ref[pl.ds(start, BLOCK), :] = project(acts_ref, start, mine_ref, group)
        return carry

    blocks(acts_ref, body, 0)


def last_kernel(
    queries, acts_ref, left_ref, right_ref, total_ref, weights_ref, grad_ref, onehot_ref, before_ref, out_ref
):
    other = 1 - lax.axis_index("groups")

    def body(start, sums):
        total = total_ref[pl.ds(start, BLOCK), :]
        total = total + project(acts_ref, start, left_ref, other)
        total = total + project(acts_ref, start, right_ref, other, left_ref.shape[1])
        return sums + mix(start, total, weights_ref[3], grad_ref, onehot_ref)

    sums = blocks(acts_ref, body, before_ref[...])
    width = sums.shape[1]
    query_of = lax.broadcasted_iota(jnp.int32, (queries, width), 1) // (width // queries)
    chosen = query_of == lax.broadcasted_iota(jnp.int32, (queries, width), 0)
    scores = contract_last(chosen.astype(jnp.float32), sums, precision=lax.Precision.HIGHEST)
    columns = out_ref.shape[1]
    for place in range(out_ref.shape[0] // queries):
        out_ref[pl.ds(place * queries, queries), :] = scores[
            :, place * columns : (place + 1) * columns
        ]


def call(kernel, out_shape, *operands, **options):
    return pl.pallas_call(
        kernel,
        out_shape=out_shape,
        compiler_params=pltpu.CompilerParams(vmem_limit_bytes=VMEM_LIMIT),
        cost_estimate=pl.CostEstimate(flops=1, bytes_accessed=1, transcendentals=0),
        **options,
    )(*operands)


def precondition(in_rows, eig_rows, out_query):
    row_count = in_rows.shape[0]
    basis_width = out_query.shape[0]
    query_count = out_query.shape[1] // R
    outer_sum = jnp.einsum(
        "jqr,iqr->qji",
        in_rows.reshape(row_count, query_count, R),
        out_query.reshape(basis_width, query_count, R),
        preferred_element_type=jnp.float32,
    )
    inverse = 1.0 / (eig_rows.astype(jnp.float32) + damping)
    return (outer_sum * inverse[None, :, :]).astype(jnp.bfloat16)


def plain_scores(acts, basis_in, pack, out_query, grad_proj, onehot):
    pack = lax.all_gather(pack, "blk", axis=0, tiled=True)
    piece = lax.all_gather(basis_in, "blk", axis=0, tiled=True)
    pairs = out_query.shape[1]
    weighted = precondition(pack[:, :pairs], pack[:, pairs:], out_query)
    projected = contract_last(acts, piece)
    per_token = jnp.stack(
        [jnp.sum(projected * contract_last(grad_proj, slab), axis=1) for slab in weighted]
    )
    return contract_last(per_token, onehot, precision=lax.Precision.HIGHEST)


def to_send(part, split):
    high = lax.reduce_precision(part[:split], 8, 7)
    low = part[:split] - high
    return jnp.concatenate([high, low, part[split:]], axis=0).astype(jnp.bfloat16)


def add_sent(part, other, split):
    high, low, rest = other[:split], other[split : 2 * split], other[2 * split :]
    first = part[:split] + high.astype(jnp.float32) + low.astype(jnp.float32)
    return jnp.concatenate([first, part[split:] + rest.astype(jnp.float32)], axis=0)


def stepped_scores(
    acts, out_grads, basis_in, basis_out, eigvals, query_out, query_in, onehot
):
    rows, width = basis_in.shape[0], basis_out.shape[0]
    tokens, seq_count = acts.shape[0], onehot.shape[0]
    query_count = query_in.shape[1] // R
    pair = [(0, 1), (1, 0)]
    place = lax.axis_index("blk")
    inner = (place == 1) | (place == 2)

    def along(value):
        return lax.ppermute(value, "blk", [(i, i ^ 1) for i in range(4)])

    def swapped(value):
        return lax.ppermute(value, "groups", pair)

    def across(value, at_ends):
        return lax.ppermute(
            value,
            AXES,
            pairing(lambda g, b, e, r: (g, 3 - b, e, r) if b in (1, 2) else at_ends(g, b, e, r)),
        )

    half, other_half = take_halves(basis_in)
    mine_1 = along(half)
    middle_3 = across(half, lambda g, b, e, r: (g, b, e, 1 - r))

    split = rows + width
    part = small_parts(held(basis_in, half), query_in, basis_out, query_out, out_grads)
    other = lax.ppermute(to_send(part, split), "rep", pair)
    part = add_sent(part, other, split)
    sent = to_send(part, split)
    other = lax.ppermute(sent, "eig", pair)
    total_shape = jax.ShapeDtypeStruct((tokens, LANES), jnp.float32)
    acts, total = call(
        first_kernel,
        [pltpu.VMEM(acts.shape, acts.dtype), total_shape],
        in_hbm(held(acts, sent)),
        basis_in,
        in_specs=[pl.BlockSpec(memory_space=pl.ANY), pl.BlockSpec(memory_space=pltpu.VMEM)],
        scratch_shapes=[pltpu.SemaphoreType.DMA((tokens // BLOCK,))],
    )
    acts = in_vmem(acts)

    middle_3 = held(middle_3, mine_1, total)
    from_pair = along(jnp.where(inner, middle_3, other_half))
    from_across = across(held(mine_1, middle_3), lambda g, b, e, r: (1 - g, b, e, r))
    part = add_sent(part, held(other, mine_1), split).astype(jnp.bfloat16)
    in_query, out_query, grad_proj = part[:rows], part[rows:split], part[split:]
    packs = by_distance(jnp.concatenate([in_query, eigvals], axis=1))

    mine_2 = jnp.where(inner, from_across, from_pair)
    theirs_2 = swapped(mine_2)
    mine_3 = along(mine_2)
    theirs_1 = jnp.where(inner, held(from_pair, mine_2), held(from_across, mine_2))
    sums_shape = jax.ShapeDtypeStruct((seq_count, query_count * rows), jnp.float32)
    weights_shape = jax.ShapeDtypeStruct((4, query_count * rows, width), jnp.bfloat16)
    sums, weights = call(
        functools.partial(weight_kernel, query_count),
        [sums_shape, weights_shape],
        *packs, held(out_query, mine_2), grad_proj, onehot, total,
    )
    fixed = (weights, grad_proj, onehot)
    sums = call(
        functools.partial(slot_kernel, 1), sums_shape, acts, mine_1, theirs_1, *fixed, sums
    )

    cut = mine_3.shape[1] // 2
    left_3 = along(held(theirs_2, sums)[:, :cut])
    right_3 = swapped(held(mine_3, sums)[:, cut:])
    sums = call(
        functools.partial(slot_kernel, 2), sums_shape, acts, mine_2, theirs_2, *fixed, sums
    )
    total = call(mine_kernel, total_shape, acts, mine_3)
    places = lax.axis_size("blk")
    return call(
        functools.partial(last_kernel, query_count),
        jax.ShapeDtypeStruct((places * query_count, seq_count // places), jnp.float32),
        acts, left_3, right_3, total, *fixed, sums,
    )


def plain_path(acts, out_grads, basis_in, basis_out, eigvals, query_out, query_in, onehot):
    def whole_sum(part, send_as):
        return swap_sum(swap_sum(part, "rep", jnp.float32), "eig", send_as).astype(jnp.bfloat16)

    in_query = whole_sum(jnp.dot(basis_in, query_in, preferred_element_type=jnp.float32), jnp.float32)
    out_query = whole_sum(
        jnp.dot(basis_out, query_out, preferred_element_type=jnp.float32), jnp.float32
    )
    grad_proj = whole_sum(contract_last(out_grads, basis_out), jnp.bfloat16)
    pack = jnp.concatenate([in_query, eigvals], axis=1)
    scores = plain_scores(acts, basis_in, pack, out_query, grad_proj, onehot.astype(jnp.float32))
    queries, columns = scores.shape
    places = lax.axis_size("blk")
    parts = scores.reshape(queries, places, columns // places)
    return parts.transpose(1, 0, 2).reshape(places * queries, columns // places)


def on_device(acts, out_grads, basis_in, basis_out, eigvals, query_out, query_in, seq_ids, owner):
    rows, features = basis_in.shape
    pairs = query_in.shape[1]
    seq_count = owner.shape[0]
    labels = jnp.arange(seq_count, dtype=jnp.int32)
    column_of = jnp.sum(jnp.where(seq_ids[None, :] == labels[:, None], owner[:, None], 0), axis=0)
    onehot = (labels[:, None] == column_of[None, :]).astype(jnp.bfloat16)
    stepped = (
        all(lax.axis_size(axis) == size for axis, size in zip(AXES, (2, 4, 2, 2)))
        and LANES % rows == 0
        and (pairs // R * rows) % LANES == 0
        and features % (4 * LANES) == 0
        and acts.shape[0] % BLOCK == 0
        and pairs == basis_out.shape[0] == LANES
    )
    way = stepped_scores if stepped else plain_path
    parts = way(acts, out_grads, basis_in, basis_out, eigvals, query_out, query_in, onehot)
    own_queries = pairs // R // lax.axis_size(("eig", "rep"))
    own_columns = seq_count // lax.axis_size("blk")
    parts = lax.all_to_all(parts, ("blk", "eig", "rep"), 0, 0, tiled=True)
    return jnp.sum(parts.reshape(-1, own_queries, own_columns), axis=0)


def solution(mesh):
    return jax.shard_map(
        on_device,
        mesh=mesh,
        in_specs=(
            P(("groups", "blk"), ("eig", "rep")),
            P(("groups", "blk"), ("eig", "rep")),
            P("blk", ("eig", "rep")),
            P(None, ("eig", "rep")),
            P("blk", None),
            P(("eig", "rep"), "groups"),
            P(("eig", "rep"), "groups"),
            P(("groups", "blk")),
            P("groups"),
        ),
        out_specs=P(("groups", "eig", "rep"), "blk"),
        check_vma=False,
    )
```

```python
import functools
import itertools

import jax
import jax.numpy as jnp
from jax import lax
from jax.experimental import pallas as pl
from jax.experimental.pallas import tpu as pltpu
from jax.sharding import PartitionSpec as P

R = 32
LANES = 128
BLOCK = 256
VMEM_LIMIT = 16 * 1024 * 1024
AXES = ("groups", "blk", "eig", "rep")


damping = 0.05


def contract_last(left_side, right_side, precision=None):
    return lax.dot_general(
        left_side,
        right_side,
        (((1,), (1,)), ((), ())),
        precision=precision,
        preferred_element_type=jnp.float32,
    )


def swap_sum(value, axis, send_as):
    size = lax.axis_size(axis)
    if size & (size - 1):
        return lax.psum(value, axis)
    step = 1
    while step < size:
        pairs = [(i, i ^ step) for i in range(size)]
        value = value + lax.ppermute(value.astype(send_as), axis, pairs).astype(jnp.float32)
        step *= 2
    return value


def by_distance(value, axis="blk"):
    size = lax.axis_size(axis)
    return [value] + [
        lax.ppermute(value, axis, [(i, i ^ k) for i in range(size)]) for k in range(1, size)
    ]


def held(value, *until):
    return lax.optimization_barrier((value, *until))[0]


def in_hbm(value):
    return pltpu.with_memory_space_constraint(value, pltpu.HBM)


def in_vmem(value):
    return pltpu.with_memory_space_constraint(value, pltpu.VMEM)


def pairing(partner):
    sizes = [lax.axis_size(axis) for axis in AXES]
    places = list(itertools.product(*map(range, sizes)))
    return [(number, places.index(partner(*place))) for number, place in enumerate(places)]


def halves_kernel(whole_ref, mine_ref, other_ref, copied):
    columns = mine_ref.shape[1]
    group = lax.axis_index("groups")
    copies = [
        pltpu.make_async_copy(
            whole_ref.at[:, pl.ds(pl.multiple_of(half * columns, LANES), columns)],
            half_ref,
            copied.at[place],
        )
        for place, (half, half_ref) in enumerate([(group, mine_ref), (1 - group, other_ref)])
    ]
    for copy in copies:
        copy.start()
    for copy in copies:
        copy.wait()


def take_halves(whole):
    rows, columns = whole.shape
    half = pltpu.VMEM((rows, columns // 2), whole.dtype)
    return pl.pallas_call(
        halves_kernel,
        in_specs=[pl.BlockSpec(memory_space=pl.ANY)],
        out_shape=[half, half],
        scratch_shapes=[pltpu.SemaphoreType.DMA((2,))],
    )(in_hbm(whole))


def parts_kernel(*refs):
    sources, sum_ref, copied = refs[:5], refs[5], refs[-1]
    held_refs = out_ref, out_query_ref, in_ref, in_query_ref, grads_ref = refs[6:-1]
    copies = [
        pltpu.make_async_copy(source, target, copied.at[place])
        for place, (source, target) in enumerate(zip(sources, held_refs))
    ]
    for copy in copies:
        copy.start()
    rows, width = in_ref.shape[0], out_ref.shape[0]
    copies[0].wait()
    copies[1].wait()
    sum_ref[rows : rows + width] = jnp.dot(
        out_ref[...], out_query_ref[...], preferred_element_type=jnp.float32
    )
    copies[2].wait()
    copies[3].wait()
    sum_ref[:rows] = jnp.dot(in_ref[...], in_query_ref[...], preferred_element_type=jnp.float32)
    copies[4].wait()

    @pl.loop(0, grads_ref.shape[0] // BLOCK)
    def _(step):
        start = pl.multiple_of(step * BLOCK, LANES)
        sum_ref[pl.ds(rows + width + start, BLOCK), :] = contract_last(
            grads_ref[pl.ds(start, BLOCK), :], out_ref[...]
        )


def small_parts(basis_in, query_in, basis_out, query_out, out_grads):
    high = basis_in.shape[0] + basis_out.shape[0] + out_grads.shape[0]
    sources = (basis_out, query_out, basis_in, query_in, out_grads)
    return pl.pallas_call(
        parts_kernel,
        in_specs=[pl.BlockSpec(memory_space=pl.ANY)] * len(sources),
        out_shape=jax.ShapeDtypeStruct((high, query_in.shape[1]), jnp.float32),
        scratch_shapes=[pltpu.VMEM(source.shape, source.dtype) for source in sources]
        + [pltpu.SemaphoreType.DMA((len(sources),))],
        compiler_params=pltpu.CompilerParams(vmem_limit_bytes=VMEM_LIMIT),
    )(*[in_hbm(source) for source in sources])


def weigh(query_count, packs, out_query, weights_ref):
    rows, pairs = packs[0].shape[0], out_query.shape[1]
    query_of = lax.broadcasted_iota(jnp.int32, (rows, pairs), 1) // R
    for slot, pack_ref in enumerate(packs):
        in_query = pack_ref[:, :pairs].astype(jnp.float32)
        inverse = 1.0 / (pack_ref[:, pairs:].astype(jnp.float32) + damping)
        for query in range(query_count):
            own = jnp.where(query_of == query, in_query, 0.0).astype(jnp.bfloat16)
            outer_sum = contract_last(own, out_query)
            weights_ref[slot // 2, pl.ds((2 * query + slot % 2) * rows, rows), :] = (
                outer_sum * inverse
            ).astype(jnp.bfloat16)


def project(acts_ref, start, pieces, group, first=0):
    columns = pl.ds(
        pl.multiple_of(group * (acts_ref.shape[1] // 2) + first, LANES), pieces[0].shape[1]
    )
    stacked = jnp.concatenate([piece[...] for piece in pieces], axis=0)
    return contract_last(acts_ref[pl.ds(start, BLOCK), columns], stacked)


def mix(start, projected, weights, grad_ref, onehot_ref):
    mixed = contract_last(grad_ref[pl.ds(start, BLOCK), :], weights)
    product = jnp.concatenate([projected] * (mixed.shape[1] // LANES), axis=1) * mixed
    high = product.astype(jnp.bfloat16)
    low = (product - high.astype(jnp.float32)).astype(jnp.bfloat16)
    onehot = onehot_ref[:, pl.ds(start, BLOCK)]
    return jnp.dot(onehot, high, preferred_element_type=jnp.float32) + jnp.dot(
        onehot, low, preferred_element_type=jnp.float32
    )


def blocks(tokens, body, initial):
    def step(index, carry):
        return body(pl.multiple_of(index * BLOCK, LANES), carry)

    return lax.fori_loop(0, tokens // BLOCK, step, initial)


def load_kernel(source_ref, acts_ref, copied):
    copies = [
        pltpu.make_async_copy(
            source_ref.at[pl.ds(start, BLOCK)], acts_ref.at[pl.ds(start, BLOCK)], copied.at[place]
        )
        for place, start in enumerate(range(0, acts_ref.shape[0], BLOCK))
    ]
    for copy in copies:
        copy.start()
    for copy in copies:
        copy.wait()


def weight_kernel(query_count, *refs):
    packs, (out_query_ref, weights_ref) = refs[:4], refs[4:]
    weigh(query_count, packs, out_query_ref[...], weights_ref)


def first_kernel(
    acts_ref, half_ref, mine_ref, other_half_ref, theirs_ref, weights_ref, grad_ref, onehot_ref,
    sums_ref,
):
    group = lax.axis_index("groups")

    def body(start, sums):
        total = project(acts_ref, start, (half_ref, mine_ref), group)
        total = total + project(acts_ref, start, (other_half_ref, theirs_ref), 1 - group)
        return sums + mix(start, total, weights_ref[0], grad_ref, onehot_ref)

    sums_ref[...] = blocks(acts_ref.shape[0], body, jnp.zeros(sums_ref.shape, jnp.float32))


def mine_kernel(acts_ref, mine_2_ref, mine_3_ref, total_ref):
    group = lax.axis_index("groups")

    def body(start, carry):
        total_ref[pl.ds(start, BLOCK), :] = project(
            acts_ref, start, (mine_2_ref, mine_3_ref), group
        )
        return carry

    blocks(acts_ref.shape[0], body, 0)


def last_kernel(
    query_count, acts_ref, theirs_2_ref, left_ref, right_ref, total_ref, weights_ref, grad_ref,
    onehot_ref, before_ref, out_ref,
):
    other = 1 - lax.axis_index("groups")
    cut = left_ref.shape[1]

    def body(start, sums):
        total = total_ref[pl.ds(start, BLOCK), :]
        total = total + project(
            acts_ref, start, (theirs_2_ref.at[:, :cut], left_ref), other
        )
        total = total + project(
            acts_ref, start, (theirs_2_ref.at[:, cut:], right_ref), other, cut
        )
        return sums + mix(start, total, weights_ref[1], grad_ref, onehot_ref)

    sums = blocks(acts_ref.shape[0], body, before_ref[...])
    width = sums.shape[1]
    query_of = lax.broadcasted_iota(jnp.int32, (query_count, width), 1) // (width // query_count)
    chosen = query_of == lax.broadcasted_iota(jnp.int32, (query_count, width), 0)
    scores = contract_last(chosen.astype(jnp.float32), sums, precision=lax.Precision.HIGHEST)
    columns = out_ref.shape[1]
    for place in range(out_ref.shape[0] // query_count):
        out_ref[pl.ds(place * query_count, query_count), :] = scores[
            :, place * columns : (place + 1) * columns
        ]


def call(kernel, out_shape, *operands, **options):
    return pl.pallas_call(
        kernel,
        out_shape=out_shape,
        compiler_params=pltpu.CompilerParams(vmem_limit_bytes=VMEM_LIMIT),
        cost_estimate=pl.CostEstimate(flops=1, bytes_accessed=1, transcendentals=0),
        **options,
    )(*operands)


def precondition(in_rows, eig_rows, out_query):
    row_count = in_rows.shape[0]
    basis_width = out_query.shape[0]
    query_count = out_query.shape[1] // R
    outer_sum = jnp.einsum(
        "jqr,iqr->qji",
        in_rows.reshape(row_count, query_count, R),
        out_query.reshape(basis_width, query_count, R),
        preferred_element_type=jnp.float32,
    )
    inverse = 1.0 / (eig_rows.astype(jnp.float32) + damping)
    return (outer_sum * inverse[None, :, :]).astype(jnp.bfloat16)


def plain_scores(acts, basis_in, pack, out_query, grad_proj, onehot):
    pack = lax.all_gather(pack, "blk", axis=0, tiled=True)
    piece = lax.all_gather(basis_in, "blk", axis=0, tiled=True)
    pairs = out_query.shape[1]
    weighted = precondition(pack[:, :pairs], pack[:, pairs:], out_query)
    projected = contract_last(acts, piece)
    per_token = jnp.stack(
        [jnp.sum(projected * contract_last(grad_proj, slab), axis=1) for slab in weighted]
    )
    return contract_last(per_token, onehot, precision=lax.Precision.HIGHEST)


def to_send(part, split):
    high = lax.reduce_precision(part[:split], 8, 7)
    low = part[:split] - high
    return jnp.concatenate([high, low, part[split:]], axis=0).astype(jnp.bfloat16)


def add_sent(part, other, split):
    high, low, rest = other[:split], other[split : 2 * split], other[2 * split :]
    first = part[:split] + high.astype(jnp.float32) + low.astype(jnp.float32)
    return jnp.concatenate([first, part[split:] + rest.astype(jnp.float32)], axis=0)


def stepped_scores(
    acts, out_grads, basis_in, basis_out, eigvals, query_out, query_in, onehot
):
    rows, width = basis_in.shape[0], basis_out.shape[0]
    tokens, seq_count = acts.shape[0], onehot.shape[0]
    query_count = query_in.shape[1] // R
    pair = [(0, 1), (1, 0)]
    place = lax.axis_index("blk")
    inner = (place == 1) | (place == 2)

    def along(value):
        return lax.ppermute(value, "blk", [(i, i ^ 1) for i in range(4)])

    def swapped(value):
        return lax.ppermute(value, "groups", pair)

    def across(value, at_ends):
        return lax.ppermute(
            value,
            AXES,
            pairing(lambda g, b, e, r: (g, 3 - b, e, r) if b in (1, 2) else at_ends(g, b, e, r)),
        )

    half, other_half = take_halves(basis_in)
    mine_1 = along(half)
    middle_3 = across(half, lambda g, b, e, r: (g, b, e, 1 - r))

    split = rows + width
    part = small_parts(held(basis_in, half), query_in, basis_out, query_out, out_grads)
    other = lax.ppermute(to_send(part, split), "rep", pair)
    part = add_sent(part, other, split)
    other = lax.ppermute(to_send(part, split), "eig", pair)
    middle_3 = held(middle_3, mine_1)
    from_pair = along(jnp.where(inner, middle_3, other_half))
    from_across = across(held(mine_1, middle_3), lambda g, b, e, r: (1 - g, b, e, r))
    part = add_sent(part, held(other, mine_1), split).astype(jnp.bfloat16)
    in_query, out_query, grad_proj = part[:rows], part[rows:split], part[split:]
    pack = jnp.concatenate([in_query, eigvals], axis=1)
    packs = by_distance(pack)
    acts = call(
        load_kernel,
        pltpu.VMEM(acts.shape, acts.dtype),
        in_hbm(held(acts, pack)),
        in_specs=[pl.BlockSpec(memory_space=pl.ANY)],
        scratch_shapes=[pltpu.SemaphoreType.DMA((tokens // BLOCK,))],
    )
    acts = in_vmem(acts)

    from_across = held(from_across, acts)
    mine_2 = jnp.where(inner, from_across, from_pair)
    theirs_2 = swapped(mine_2)
    mine_3 = along(mine_2)
    theirs_1 = jnp.where(inner, held(from_pair, mine_2), held(from_across, mine_2))
    weights = call(
        functools.partial(weight_kernel, query_count),
        jax.ShapeDtypeStruct((2, 2 * query_count * rows, width), jnp.bfloat16),
        *packs, held(out_query, mine_2),
    )
    fixed = (weights, grad_proj, onehot)
    sums = call(
        first_kernel,
        jax.ShapeDtypeStruct((seq_count, 2 * query_count * rows), jnp.float32),
        acts, half, mine_1, other_half, theirs_1, *fixed,
    )

    cut = mine_3.shape[1] // 2
    left_3 = along(held(theirs_2, sums)[:, :cut])
    right_3 = swapped(held(mine_3, sums)[:, cut:])
    total = call(mine_kernel, jax.ShapeDtypeStruct((tokens, LANES), jnp.float32), acts, mine_2, mine_3)
    places = lax.axis_size("blk")
    return call(
        functools.partial(last_kernel, query_count),
        jax.ShapeDtypeStruct((places * query_count, seq_count // places), jnp.float32),
        acts, theirs_2, left_3, right_3, total, *fixed, sums,
    )


def plain_path(acts, out_grads, basis_in, basis_out, eigvals, query_out, query_in, onehot):
    def whole_sum(part, send_as):
        return swap_sum(swap_sum(part, "rep", jnp.float32), "eig", send_as).astype(jnp.bfloat16)

    in_query = whole_sum(jnp.dot(basis_in, query_in, preferred_element_type=jnp.float32), jnp.float32)
    out_query = whole_sum(
        jnp.dot(basis_out, query_out, preferred_element_type=jnp.float32), jnp.float32
    )
    grad_proj = whole_sum(contract_last(out_grads, basis_out), jnp.bfloat16)
    pack = jnp.concatenate([in_query, eigvals], axis=1)
    scores = plain_scores(acts, basis_in, pack, out_query, grad_proj, onehot.astype(jnp.float32))
    queries, columns = scores.shape
    places = lax.axis_size("blk")
    parts = scores.reshape(queries, places, columns // places)
    return parts.transpose(1, 0, 2).reshape(places * queries, columns // places)


def on_device(acts, out_grads, basis_in, basis_out, eigvals, query_out, query_in, seq_ids, owner):
    rows, features = basis_in.shape
    pairs = query_in.shape[1]
    seq_count = owner.shape[0]
    labels = jnp.arange(seq_count, dtype=jnp.int32)
    column_of = jnp.sum(jnp.where(seq_ids[None, :] == labels[:, None], owner[:, None], 0), axis=0)
    onehot = (labels[:, None] == column_of[None, :]).astype(jnp.bfloat16)
    stepped = (
        all(lax.axis_size(axis) == size for axis, size in zip(AXES, (2, 4, 2, 2)))
        and 2 * rows == LANES
        and features % (4 * LANES) == 0
        and acts.shape[0] % BLOCK == 0
        and pairs == basis_out.shape[0] == LANES
    )
    way = stepped_scores if stepped else plain_path
    parts = way(acts, out_grads, basis_in, basis_out, eigvals, query_out, query_in, onehot)
    own_queries = pairs // R // lax.axis_size(("eig", "rep"))
    own_columns = seq_count // lax.axis_size("blk")
    parts = lax.all_to_all(parts, ("blk", "eig", "rep"), 0, 0, tiled=True)
    return jnp.sum(parts.reshape(-1, own_queries, own_columns), axis=0)


def solution(mesh):
    return jax.shard_map(
        on_device,
        mesh=mesh,
        in_specs=(
            P(("groups", "blk"), ("eig", "rep")),
            P(("groups", "blk"), ("eig", "rep")),
            P("blk", ("eig", "rep")),
            P(None, ("eig", "rep")),
            P("blk", None),
            P(("eig", "rep"), "groups"),
            P(("eig", "rep"), "groups"),
            P(("groups", "blk")),
            P("groups"),
        ),
        out_specs=P(("groups", "eig", "rep"), "blk"),
        check_vma=False,
    )
```

```python
import functools
import itertools

import jax
import jax.numpy as jnp
from jax import lax
from jax.experimental import pallas as pl
from jax.experimental.pallas import tpu as pltpu
from jax.sharding import PartitionSpec as P

R = 32
LANES = 128
BLOCK = 256
VMEM_LIMIT = 16 * 1024 * 1024
AXES = ("groups", "blk", "eig", "rep")


damping = 0.05


def contract_last(left_side, right_side, precision=None):
    return lax.dot_general(
        left_side,
        right_side,
        (((1,), (1,)), ((), ())),
        precision=precision,
        preferred_element_type=jnp.float32,
    )


def swap_sum(value, axis, send_as):
    size = lax.axis_size(axis)
    if size & (size - 1):
        return lax.psum(value, axis)
    step = 1
    while step < size:
        pairs = [(i, i ^ step) for i in range(size)]
        value = value + lax.ppermute(value.astype(send_as), axis, pairs).astype(jnp.float32)
        step *= 2
    return value


def by_distance(value, axis="blk"):
    size = lax.axis_size(axis)
    return [value] + [
        lax.ppermute(value, axis, [(i, i ^ k) for i in range(size)]) for k in range(1, size)
    ]


def held(value, *until):
    return lax.optimization_barrier((value, *until))[0]


def in_hbm(value):
    return pltpu.with_memory_space_constraint(value, pltpu.HBM)


def in_vmem(value):
    return pltpu.with_memory_space_constraint(value, pltpu.VMEM)


def pairing(partner):
    sizes = [lax.axis_size(axis) for axis in AXES]
    places = list(itertools.product(*map(range, sizes)))
    return [(number, places.index(partner(*place))) for number, place in enumerate(places)]


def halves_kernel(whole_ref, mine_ref, other_ref, copied):
    columns = mine_ref.shape[1]
    group = lax.axis_index("groups")
    copies = [
        pltpu.make_async_copy(
            whole_ref.at[:, pl.ds(pl.multiple_of(half * columns, LANES), columns)],
            half_ref,
            copied.at[place],
        )
        for place, (half, half_ref) in enumerate([(group, mine_ref), (1 - group, other_ref)])
    ]
    for copy in copies:
        copy.start()
    for copy in copies:
        copy.wait()


def take_halves(whole):
    rows, columns = whole.shape
    half = pltpu.VMEM((rows, columns // 2), whole.dtype)
    return pl.pallas_call(
        halves_kernel,
        in_specs=[pl.BlockSpec(memory_space=pl.ANY)],
        out_shape=[half, half],
        scratch_shapes=[pltpu.SemaphoreType.DMA((2,))],
    )(in_hbm(whole))


def parts_kernel(*refs):
    sources, sum_ref, copied = refs[:5], refs[5], refs[-1]
    held_refs = out_ref, out_query_ref, in_ref, in_query_ref, grads_ref = refs[6:-1]
    copies = [
        pltpu.make_async_copy(source, target, copied.at[place])
        for place, (source, target) in enumerate(zip(sources, held_refs))
    ]
    for copy in copies:
        copy.start()
    rows, width = in_ref.shape[0], out_ref.shape[0]
    copies[0].wait()
    copies[1].wait()
    sum_ref[rows : rows + width] = jnp.dot(
        out_ref[...], out_query_ref[...], preferred_element_type=jnp.float32
    )
    copies[2].wait()
    copies[3].wait()
    sum_ref[:rows] = jnp.dot(in_ref[...], in_query_ref[...], preferred_element_type=jnp.float32)
    copies[4].wait()

    @pl.loop(0, grads_ref.shape[0] // BLOCK)
    def _(step):
        start = pl.multiple_of(step * BLOCK, LANES)
        sum_ref[pl.ds(rows + width + start, BLOCK), :] = contract_last(
            grads_ref[pl.ds(start, BLOCK), :], out_ref[...]
        )


def small_parts(basis_in, query_in, basis_out, query_out, out_grads):
    high = basis_in.shape[0] + basis_out.shape[0] + out_grads.shape[0]
    sources = (basis_out, query_out, basis_in, query_in, out_grads)
    return pl.pallas_call(
        parts_kernel,
        in_specs=[pl.BlockSpec(memory_space=pl.ANY)] * len(sources),
        out_shape=jax.ShapeDtypeStruct((high, query_in.shape[1]), jnp.float32),
        scratch_shapes=[pltpu.VMEM(source.shape, source.dtype) for source in sources]
        + [pltpu.SemaphoreType.DMA((len(sources),))],
        compiler_params=pltpu.CompilerParams(vmem_limit_bytes=VMEM_LIMIT),
    )(*[in_hbm(source) for source in sources])


def weigh(query_count, packs, out_query, weights_ref):
    rows, pairs = packs[0].shape[0], out_query.shape[1]
    query_of = lax.broadcasted_iota(jnp.int32, (rows, pairs), 1) // R
    for slot, pack_ref in enumerate(packs):
        in_query = pack_ref[:, :pairs].astype(jnp.float32)
        inverse = 1.0 / (pack_ref[:, pairs:].astype(jnp.float32) + damping)
        for query in range(query_count):
            own = jnp.where(query_of == query, in_query, 0.0).astype(jnp.bfloat16)
            outer_sum = contract_last(own, out_query)
            weights_ref[slot // 2, pl.ds((2 * query + slot % 2) * rows, rows), :] = (
                outer_sum * inverse
            ).astype(jnp.bfloat16)


def project(acts_ref, start, pieces, group, first=0):
    columns = pl.ds(
        pl.multiple_of(group * (acts_ref.shape[1] // 2) + first, LANES), pieces[0].shape[1]
    )
    stacked = jnp.concatenate([piece[...] for piece in pieces], axis=0)
    return contract_last(acts_ref[pl.ds(start, BLOCK), columns], stacked)


def mixing(start, weights, grad_ref):
    return contract_last(grad_ref[pl.ds(start, BLOCK), :], weights)


def mix(start, projected, mixed, onehot_ref):
    product = jnp.concatenate([projected] * (mixed.shape[1] // LANES), axis=1) * mixed
    high = product.astype(jnp.bfloat16)
    low = (product - high.astype(jnp.float32)).astype(jnp.bfloat16)
    onehot = onehot_ref[:, pl.ds(start, BLOCK)]
    return jnp.dot(onehot, high, preferred_element_type=jnp.float32) + jnp.dot(
        onehot, low, preferred_element_type=jnp.float32
    )


def blocks(tokens, body, initial):
    def step(index, carry):
        return body(pl.multiple_of(index * BLOCK, LANES), carry)

    return lax.fori_loop(0, tokens // BLOCK, step, initial, unroll=True)


def weight_kernel(query_count, *refs):
    packs, (out_query_ref, weights_ref) = refs[:4], refs[4:]
    weigh(query_count, packs, out_query_ref[...], weights_ref)


def first_kernel(
    source_ref, half_ref, mine_ref, other_half_ref, theirs_ref, weights_ref, grad_ref, onehot_ref,
    sums_ref, acts_ref, copied,
):
    group = lax.axis_index("groups")
    copies = [
        pltpu.make_async_copy(
            source_ref.at[pl.ds(start, BLOCK)], acts_ref.at[pl.ds(start, BLOCK)], copied.at[place]
        )
        for place, start in enumerate(range(0, acts_ref.shape[0], BLOCK))
    ]
    for copy in copies:
        copy.start()
    sums = jnp.zeros(sums_ref.shape, jnp.float32)
    for place, copy in enumerate(copies):
        start = place * BLOCK
        mixed = mixing(start, weights_ref[0], grad_ref)
        copy.wait()
        total = project(acts_ref, start, (half_ref, mine_ref), group)
        total = total + project(acts_ref, start, (other_half_ref, theirs_ref), 1 - group)
        sums = sums + mix(start, total, mixed, onehot_ref)
    sums_ref[...] = sums


def mine_kernel(acts_ref, mine_2_ref, mine_3_ref, weights_ref, grad_ref, total_ref, mixed_ref):
    group = lax.axis_index("groups")

    def body(start, carry):
        total_ref[pl.ds(start, BLOCK), :] = project(
            acts_ref, start, (mine_2_ref, mine_3_ref), group
        )
        mixed_ref[pl.ds(start, BLOCK), :] = mixing(start, weights_ref[1], grad_ref)
        return carry

    blocks(acts_ref.shape[0], body, 0)


def last_kernel(
    query_count, acts_ref, theirs_2_ref, left_ref, right_ref, total_ref, mixed_ref, onehot_ref,
    before_ref, out_ref,
):
    other = 1 - lax.axis_index("groups")
    cut = left_ref.shape[1]

    def body(start, sums):
        total = total_ref[pl.ds(start, BLOCK), :]
        total = total + project(
            acts_ref, start, (theirs_2_ref.at[:, :cut], left_ref), other
        )
        total = total + project(
            acts_ref, start, (theirs_2_ref.at[:, cut:], right_ref), other, cut
        )
        return sums + mix(start, total, mixed_ref[pl.ds(start, BLOCK), :], onehot_ref)

    sums = blocks(acts_ref.shape[0], body, before_ref[...])
    width = sums.shape[1]
    query_of = lax.broadcasted_iota(jnp.int32, (query_count, width), 1) // (width // query_count)
    chosen = query_of == lax.broadcasted_iota(jnp.int32, (query_count, width), 0)
    scores = contract_last(chosen.astype(jnp.float32), sums, precision=lax.Precision.HIGHEST)
    columns = out_ref.shape[1]
    for place in range(out_ref.shape[0] // query_count):
        out_ref[pl.ds(place * query_count, query_count), :] = scores[
            :, place * columns : (place + 1) * columns
        ]


def call(kernel, out_shape, *operands, **options):
    return pl.pallas_call(
        kernel,
        out_shape=out_shape,
        compiler_params=pltpu.CompilerParams(vmem_limit_bytes=VMEM_LIMIT),
        cost_estimate=pl.CostEstimate(flops=1, bytes_accessed=1, transcendentals=0),
        **options,
    )(*operands)


def precondition(in_rows, eig_rows, out_query):
    row_count = in_rows.shape[0]
    basis_width = out_query.shape[0]
    query_count = out_query.shape[1] // R
    outer_sum = jnp.einsum(
        "jqr,iqr->qji",
        in_rows.reshape(row_count, query_count, R),
        out_query.reshape(basis_width, query_count, R),
        preferred_element_type=jnp.float32,
    )
    inverse = 1.0 / (eig_rows.astype(jnp.float32) + damping)
    return (outer_sum * inverse[None, :, :]).astype(jnp.bfloat16)


def plain_scores(acts, basis_in, pack, out_query, grad_proj, onehot):
    pack = lax.all_gather(pack, "blk", axis=0, tiled=True)
    piece = lax.all_gather(basis_in, "blk", axis=0, tiled=True)
    pairs = out_query.shape[1]
    weighted = precondition(pack[:, :pairs], pack[:, pairs:], out_query)
    projected = contract_last(acts, piece)
    per_token = jnp.stack(
        [jnp.sum(projected * contract_last(grad_proj, slab), axis=1) for slab in weighted]
    )
    return contract_last(per_token, onehot, precision=lax.Precision.HIGHEST)


def to_send(part, split):
    high = lax.reduce_precision(part[:split], 8, 7)
    low = part[:split] - high
    return jnp.concatenate([high, low, part[split:]], axis=0).astype(jnp.bfloat16)


def add_sent(part, other, split):
    high, low, rest = other[:split], other[split : 2 * split], other[2 * split :]
    first = part[:split] + high.astype(jnp.float32) + low.astype(jnp.float32)
    return jnp.concatenate([first, part[split:] + rest.astype(jnp.float32)], axis=0)


def stepped_scores(
    acts, out_grads, basis_in, basis_out, eigvals, query_out, query_in, onehot
):
    rows, width = basis_in.shape[0], basis_out.shape[0]
    tokens, seq_count = acts.shape[0], onehot.shape[0]
    query_count = query_in.shape[1] // R
    pair = [(0, 1), (1, 0)]
    place = lax.axis_index("blk")
    inner = (place == 1) | (place == 2)

    def along(value):
        return lax.ppermute(value, "blk", [(i, i ^ 1) for i in range(4)])

    def swapped(value):
        return lax.ppermute(value, "groups", pair)

    def across(value, at_ends):
        return lax.ppermute(
            value,
            AXES,
            pairing(lambda g, b, e, r: (g, 3 - b, e, r) if b in (1, 2) else at_ends(g, b, e, r)),
        )

    half, other_half = take_halves(basis_in)
    mine_1 = along(half)
    middle_3 = across(half, lambda g, b, e, r: (g, b, e, 1 - r))

    split = rows + width
    part = small_parts(held(basis_in, half), query_in, basis_out, query_out, out_grads)
    other = lax.ppermute(to_send(part, split), "rep", pair)
    part = add_sent(part, other, split)
    other = lax.ppermute(to_send(part, split), "eig", pair)
    middle_3 = held(middle_3, mine_1)
    from_pair = along(jnp.where(inner, middle_3, other_half))
    from_across = across(held(mine_1, middle_3), lambda g, b, e, r: (1 - g, b, e, r))
    part = add_sent(part, held(other, mine_1), split).astype(jnp.bfloat16)
    in_query, out_query, grad_proj = part[:rows], part[rows:split], part[split:]
    pack = jnp.concatenate([in_query, eigvals], axis=1)
    packs = by_distance(pack)
    mine_2 = jnp.where(inner, from_across, from_pair)
    theirs_2 = swapped(mine_2)
    mine_3 = along(mine_2)
    theirs_1 = jnp.where(inner, held(from_pair, mine_2), held(from_across, mine_2))
    weights = call(
        functools.partial(weight_kernel, query_count),
        jax.ShapeDtypeStruct((2, 2 * query_count * rows, width), jnp.bfloat16),
        *packs, held(out_query, mine_2),
    )
    mixed_width = 2 * query_count * rows
    sums, acts = call(
        first_kernel,
        [
            jax.ShapeDtypeStruct((seq_count, mixed_width), jnp.float32),
            pltpu.VMEM(acts.shape, acts.dtype),
        ],
        in_hbm(acts), half, mine_1, other_half, theirs_1, weights, grad_proj, onehot,
        in_specs=[pl.BlockSpec(memory_space=pl.ANY)]
        + [pl.BlockSpec(memory_space=pltpu.VMEM)] * 7,
        scratch_shapes=[pltpu.SemaphoreType.DMA((tokens // BLOCK,))],
    )
    acts = in_vmem(acts)

    cut = mine_3.shape[1] // 2
    left_3 = along(held(theirs_2, sums)[:, :cut])
    right_3 = swapped(held(mine_3, sums)[:, cut:])
    total, mixed = call(
        mine_kernel,
        [jax.ShapeDtypeStruct((tokens, size), jnp.float32) for size in (LANES, mixed_width)],
        acts, mine_2, mine_3, weights, grad_proj,
    )
    places = lax.axis_size("blk")
    return call(
        functools.partial(last_kernel, query_count),
        jax.ShapeDtypeStruct((places * query_count, seq_count // places), jnp.float32),
        acts, theirs_2, left_3, right_3, total, mixed, onehot, sums,
    )


def plain_path(acts, out_grads, basis_in, basis_out, eigvals, query_out, query_in, onehot):
    def whole_sum(part, send_as):
        return swap_sum(swap_sum(part, "rep", jnp.float32), "eig", send_as).astype(jnp.bfloat16)

    in_query = whole_sum(jnp.dot(basis_in, query_in, preferred_element_type=jnp.float32), jnp.float32)
    out_query = whole_sum(
        jnp.dot(basis_out, query_out, preferred_element_type=jnp.float32), jnp.float32
    )
    grad_proj = whole_sum(contract_last(out_grads, basis_out), jnp.bfloat16)
    pack = jnp.concatenate([in_query, eigvals], axis=1)
    scores = plain_scores(acts, basis_in, pack, out_query, grad_proj, onehot.astype(jnp.float32))
    queries, columns = scores.shape
    places = lax.axis_size("blk")
    parts = scores.reshape(queries, places, columns // places)
    return parts.transpose(1, 0, 2).reshape(places * queries, columns // places)


def on_device(acts, out_grads, basis_in, basis_out, eigvals, query_out, query_in, seq_ids, owner):
    rows, features = basis_in.shape
    pairs = query_in.shape[1]
    seq_count = owner.shape[0]
    labels = jnp.arange(seq_count, dtype=jnp.int32)
    column_of = jnp.sum(jnp.where(seq_ids[None, :] == labels[:, None], owner[:, None], 0), axis=0)
    onehot = (labels[:, None] == column_of[None, :]).astype(jnp.bfloat16)
    stepped = (
        all(lax.axis_size(axis) == size for axis, size in zip(AXES, (2, 4, 2, 2)))
        and 2 * rows == LANES
        and features % (4 * LANES) == 0
        and acts.shape[0] % BLOCK == 0
        and pairs == basis_out.shape[0] == LANES
    )
    way = stepped_scores if stepped else plain_path
    parts = way(acts, out_grads, basis_in, basis_out, eigvals, query_out, query_in, onehot)
    own_queries = pairs // R // lax.axis_size(("eig", "rep"))
    own_columns = seq_count // lax.axis_size("blk")
    parts = lax.all_to_all(parts, ("blk", "eig", "rep"), 0, 0, tiled=True)
    return jnp.sum(parts.reshape(-1, own_queries, own_columns), axis=0)


def solution(mesh):
    return jax.shard_map(
        on_device,
        mesh=mesh,
        in_specs=(
            P(("groups", "blk"), ("eig", "rep")),
            P(("groups", "blk"), ("eig", "rep")),
            P("blk", ("eig", "rep")),
            P(None, ("eig", "rep")),
            P("blk", None),
            P(("eig", "rep"), "groups"),
            P(("eig", "rep"), "groups"),
            P(("groups", "blk")),
            P("groups"),
        ),
        out_specs=P(("groups", "eig", "rep"), "blk"),
        check_vma=False,
    )
```

```python
import functools
import itertools

import jax
import jax.numpy as jnp
from jax import lax
from jax.experimental import pallas as pl
from jax.experimental.pallas import tpu as pltpu
from jax.sharding import PartitionSpec as P

R = 32
LANES = 128
BLOCK = 256
VMEM_LIMIT = 16 * 1024 * 1024
AXES = ("groups", "blk", "eig", "rep")


damping = 0.05


def contract_last(left_side, right_side, precision=None):
    return lax.dot_general(
        left_side,
        right_side,
        (((1,), (1,)), ((), ())),
        precision=precision,
        preferred_element_type=jnp.float32,
    )


def swap_sum(value, axis, send_as):
    size = lax.axis_size(axis)
    if size & (size - 1):
        return lax.psum(value, axis)
    step = 1
    while step < size:
        pairs = [(i, i ^ step) for i in range(size)]
        value = value + lax.ppermute(value.astype(send_as), axis, pairs).astype(jnp.float32)
        step *= 2
    return value


def by_distance(value, axis="blk"):
    size = lax.axis_size(axis)
    return [value] + [
        lax.ppermute(value, axis, [(i, i ^ k) for i in range(size)]) for k in range(1, size)
    ]


def held(value, *until):
    return lax.optimization_barrier((value, *until))[0]


def in_hbm(value):
    return pltpu.with_memory_space_constraint(value, pltpu.HBM)


def in_vmem(value):
    return pltpu.with_memory_space_constraint(value, pltpu.VMEM)


def pairing(partner):
    sizes = [lax.axis_size(axis) for axis in AXES]
    places = list(itertools.product(*map(range, sizes)))
    return [(number, places.index(partner(*place))) for number, place in enumerate(places)]


def chunks_kernel(whole_ref, *refs):
    chunk_refs, copied = refs[:4], refs[4]
    columns = chunk_refs[0].shape[1]
    group = lax.axis_index("groups")
    copies = []
    for place, chunk_ref in enumerate(chunk_refs):
        half = group if place < 2 else 1 - group
        begin = pl.multiple_of((2 * half + place % 2) * columns, LANES)
        source = whole_ref.at[:, pl.ds(begin, columns)]
        copies.append(pltpu.make_async_copy(source, chunk_ref, copied.at[place]))
    for copy in copies:
        copy.start()
    for copy in copies:
        copy.wait()


def take_chunks(whole):
    rows, columns = whole.shape
    return pl.pallas_call(
        chunks_kernel,
        in_specs=[pl.BlockSpec(memory_space=pl.ANY)],
        out_shape=[pltpu.VMEM((rows, columns // 4), whole.dtype)] * 4,
        scratch_shapes=[pltpu.SemaphoreType.DMA((4,))],
    )(in_hbm(whole))


def parts_kernel(*refs):
    sources, sum_ref, copied = refs[:5], refs[5], refs[-1]
    held_refs = out_ref, out_query_ref, in_ref, in_query_ref, grads_ref = refs[6:-1]
    copies = [
        pltpu.make_async_copy(source, target, copied.at[place])
        for place, (source, target) in enumerate(zip(sources, held_refs))
    ]
    for copy in copies:
        copy.start()
    rows, width = in_ref.shape[0], out_ref.shape[0]
    copies[0].wait()
    copies[1].wait()
    sum_ref[rows : rows + width] = jnp.dot(
        out_ref[...], out_query_ref[...], preferred_element_type=jnp.float32
    )
    copies[2].wait()
    copies[3].wait()
    sum_ref[:rows] = jnp.dot(in_ref[...], in_query_ref[...], preferred_element_type=jnp.float32)
    copies[4].wait()

    @pl.loop(0, grads_ref.shape[0] // BLOCK)
    def _(step):
        start = pl.multiple_of(step * BLOCK, LANES)
        sum_ref[pl.ds(rows + width + start, BLOCK), :] = contract_last(
            grads_ref[pl.ds(start, BLOCK), :], out_ref[...]
        )


def small_parts(basis_in, query_in, basis_out, query_out, out_grads):
    high = basis_in.shape[0] + basis_out.shape[0] + out_grads.shape[0]
    sources = (basis_out, query_out, basis_in, query_in, out_grads)
    return pl.pallas_call(
        parts_kernel,
        in_specs=[pl.BlockSpec(memory_space=pl.ANY)] * len(sources),
        out_shape=jax.ShapeDtypeStruct((high, query_in.shape[1]), jnp.float32),
        scratch_shapes=[pltpu.VMEM(source.shape, source.dtype) for source in sources]
        + [pltpu.SemaphoreType.DMA((len(sources),))],
        compiler_params=pltpu.CompilerParams(vmem_limit_bytes=VMEM_LIMIT),
    )(*[in_hbm(source) for source in sources])


def weigh(query_count, packs, out_query, weights_ref):
    rows, pairs = packs[0].shape[0], out_query.shape[1]
    query_of = lax.broadcasted_iota(jnp.int32, (rows, pairs), 1) // R
    for slot, pack_ref in enumerate(packs):
        in_query = pack_ref[:, :pairs].astype(jnp.float32)
        inverse = 1.0 / (pack_ref[:, pairs:].astype(jnp.float32) + damping)
        for query in range(query_count):
            own = jnp.where(query_of == query, in_query, 0.0).astype(jnp.bfloat16)
            outer_sum = contract_last(own, out_query)
            weights_ref[slot // 2, pl.ds((2 * query + slot % 2) * rows, rows), :] = (
                outer_sum * inverse
            ).astype(jnp.bfloat16)


def project(acts_ref, start, pieces, group, first=0):
    columns = pl.ds(
        pl.multiple_of(group * (acts_ref.shape[1] // 2) + first, LANES), pieces[0].shape[1]
    )
    stacked = jnp.concatenate([piece[...] for piece in pieces], axis=0)
    return contract_last(acts_ref[pl.ds(start, BLOCK), columns], stacked)


def mixing(start, weights, grad_ref):
    return contract_last(grad_ref[pl.ds(start, BLOCK), :], weights)


def mix(start, projected, mixed, onehot_ref):
    product = jnp.concatenate([projected] * (mixed.shape[1] // LANES), axis=1) * mixed
    high = product.astype(jnp.bfloat16)
    low = (product - high.astype(jnp.float32)).astype(jnp.bfloat16)
    onehot = onehot_ref[:, pl.ds(start, BLOCK)]
    return jnp.dot(onehot, high, preferred_element_type=jnp.float32) + jnp.dot(
        onehot, low, preferred_element_type=jnp.float32
    )


def blocks(tokens, body, initial):
    def step(index, carry):
        return body(pl.multiple_of(index * BLOCK, LANES), carry)

    return lax.fori_loop(0, tokens // BLOCK, step, initial, unroll=True)


def weight_kernel(query_count, *refs):
    packs, (out_query_ref, weights_ref) = refs[:4], refs[4:]
    weigh(query_count, packs, out_query_ref[...], weights_ref)


def load_kernel(source_ref, acts_ref, copied):
    copies = [
        pltpu.make_async_copy(
            source_ref.at[pl.ds(start, BLOCK)], acts_ref.at[pl.ds(start, BLOCK)], copied.at[place]
        )
        for place, start in enumerate(range(0, acts_ref.shape[0], BLOCK))
    ]
    for copy in copies:
        copy.start()
    for copy in copies:
        copy.wait()


def first_kernel(acts_ref, *refs):
    slots, (weights_ref, grad_ref, onehot_ref, sums_ref) = refs[:8], refs[8:]
    columns = slots[0].shape[1]
    group = lax.axis_index("groups")

    def body(start, sums):
        total = 0.0
        for place in range(4):
            half = group if place < 2 else 1 - group
            total = total + project(
                acts_ref, start, (slots[place], slots[4 + place]), half, place % 2 * columns
            )
        return sums + mix(start, total, mixing(start, weights_ref[0], grad_ref), onehot_ref)

    sums_ref[...] = blocks(acts_ref.shape[0], body, jnp.zeros(sums_ref.shape, jnp.float32))


def mine_kernel(acts_ref, mine_2_ref, mine_3_ref, weights_ref, grad_ref, total_ref, mixed_ref):
    group = lax.axis_index("groups")

    def body(start, carry):
        total_ref[pl.ds(start, BLOCK), :] = project(
            acts_ref, start, (mine_2_ref, mine_3_ref), group
        )
        mixed_ref[pl.ds(start, BLOCK), :] = mixing(start, weights_ref[1], grad_ref)
        return carry

    blocks(acts_ref.shape[0], body, 0)


def last_kernel(
    query_count, acts_ref, theirs_2_ref, left_ref, right_ref, total_ref, mixed_ref, onehot_ref,
    before_ref, out_ref,
):
    other = 1 - lax.axis_index("groups")
    cut = left_ref.shape[1]

    def body(start, sums):
        total = total_ref[pl.ds(start, BLOCK), :]
        total = total + project(
            acts_ref, start, (theirs_2_ref.at[:, :cut], left_ref), other
        )
        total = total + project(
            acts_ref, start, (theirs_2_ref.at[:, cut:], right_ref), other, cut
        )
        return sums + mix(start, total, mixed_ref[pl.ds(start, BLOCK), :], onehot_ref)

    sums = blocks(acts_ref.shape[0], body, before_ref[...])
    width = sums.shape[1]
    query_of = lax.broadcasted_iota(jnp.int32, (query_count, width), 1) // (width // query_count)
    chosen = query_of == lax.broadcasted_iota(jnp.int32, (query_count, width), 0)
    scores = contract_last(chosen.astype(jnp.float32), sums, precision=lax.Precision.HIGHEST)
    columns = out_ref.shape[1]
    for place in range(out_ref.shape[0] // query_count):
        out_ref[pl.ds(place * query_count, query_count), :] = scores[
            :, place * columns : (place + 1) * columns
        ]


def call(kernel, out_shape, *operands, **options):
    return pl.pallas_call(
        kernel,
        out_shape=out_shape,
        compiler_params=pltpu.CompilerParams(vmem_limit_bytes=VMEM_LIMIT),
        cost_estimate=pl.CostEstimate(flops=1, bytes_accessed=1, transcendentals=0),
        **options,
    )(*operands)


def precondition(in_rows, eig_rows, out_query):
    row_count = in_rows.shape[0]
    basis_width = out_query.shape[0]
    query_count = out_query.shape[1] // R
    outer_sum = jnp.einsum(
        "jqr,iqr->qji",
        in_rows.reshape(row_count, query_count, R),
        out_query.reshape(basis_width, query_count, R),
        preferred_element_type=jnp.float32,
    )
    inverse = 1.0 / (eig_rows.astype(jnp.float32) + damping)
    return (outer_sum * inverse[None, :, :]).astype(jnp.bfloat16)


def plain_scores(acts, basis_in, pack, out_query, grad_proj, onehot):
    pack = lax.all_gather(pack, "blk", axis=0, tiled=True)
    piece = lax.all_gather(basis_in, "blk", axis=0, tiled=True)
    pairs = out_query.shape[1]
    weighted = precondition(pack[:, :pairs], pack[:, pairs:], out_query)
    projected = contract_last(acts, piece)
    per_token = jnp.stack(
        [jnp.sum(projected * contract_last(grad_proj, slab), axis=1) for slab in weighted]
    )
    return contract_last(per_token, onehot, precision=lax.Precision.HIGHEST)


def to_send(part, split):
    high = lax.reduce_precision(part[:split], 8, 7)
    low = part[:split] - high
    return jnp.concatenate([high, low, part[split:]], axis=0).astype(jnp.bfloat16)


def add_sent(part, other, split):
    high, low, rest = other[:split], other[split : 2 * split], other[2 * split :]
    first = part[:split] + high.astype(jnp.float32) + low.astype(jnp.float32)
    return jnp.concatenate([first, part[split:] + rest.astype(jnp.float32)], axis=0)


def stepped_scores(
    acts, out_grads, basis_in, basis_out, eigvals, query_out, query_in, onehot
):
    rows, width = basis_in.shape[0], basis_out.shape[0]
    tokens, seq_count = acts.shape[0], onehot.shape[0]
    query_count = query_in.shape[1] // R
    pair = [(0, 1), (1, 0)]
    place = lax.axis_index("blk")
    inner = (place == 1) | (place == 2)

    def along(value):
        return lax.ppermute(value, "blk", [(i, i ^ 1) for i in range(4)])

    def swapped(value):
        return lax.ppermute(value, "groups", pair)

    def across(value, at_ends):
        return lax.ppermute(
            value,
            AXES,
            pairing(lambda g, b, e, r: (g, 3 - b, e, r) if b in (1, 2) else at_ends(g, b, e, r)),
        )

    chunks = take_chunks(basis_in)
    half, other_half = chunks[:2], chunks[2:]
    to_core = lambda g, b, e, r: (g, b, e, 1 - r)
    over_y = lambda g, b, e, r: (1 - g, b, e, r)
    mine_1, middle_3 = [], []
    for chunk in half:
        middle_3.append(across(chunk, to_core))
        mine_1.append(along(chunk))

    split = rows + width
    part = small_parts(held(basis_in, *half), query_in, basis_out, query_out, out_grads)
    other = lax.ppermute(to_send(part, split), "rep", pair)
    part = add_sent(part, held(other, *mine_1, *middle_3), split)
    sent = to_send(part, split)
    other = lax.ppermute(sent, "eig", pair)
    acts = call(
        load_kernel,
        pltpu.VMEM(acts.shape, acts.dtype),
        in_hbm(held(acts, sent)),
        in_specs=[pl.BlockSpec(memory_space=pl.ANY)],
        scratch_shapes=[pltpu.SemaphoreType.DMA((tokens // BLOCK,))],
    )
    acts = in_vmem(acts)

    mine_2, theirs_1 = [], []
    for first, middle, rest in zip(mine_1, middle_3, other_half):
        from_pair = along(jnp.where(inner, middle, held(rest, first)))
        from_across = across(held(first, middle), over_y)
        mine_2.append((from_across, from_pair))
    arrived = [chunk for both in mine_2 for chunk in both] + [acts]
    mine_2 = jnp.concatenate(
        [jnp.where(inner, held(here, *arrived), there) for here, there in mine_2], axis=1
    )
    theirs_1 = [
        jnp.where(inner, held(there, mine_2), held(here, mine_2))
        for here, there in zip(arrived[0:4:2], arrived[1:4:2])
    ]
    theirs_2 = swapped(mine_2)
    mine_3 = along(mine_2)

    part = add_sent(part, held(other, mine_2), split).astype(jnp.bfloat16)
    in_query, out_query, grad_proj = part[:rows], part[rows:split], part[split:]
    packs = by_distance(jnp.concatenate([in_query, eigvals], axis=1))
    weights = call(
        functools.partial(weight_kernel, query_count),
        jax.ShapeDtypeStruct((2, 2 * query_count * rows, width), jnp.bfloat16),
        *packs, out_query,
    )
    mixed_width = 2 * query_count * rows
    sums = call(
        first_kernel,
        jax.ShapeDtypeStruct((seq_count, mixed_width), jnp.float32),
        acts, *half, *other_half, *mine_1, *theirs_1, weights, grad_proj, onehot,
    )

    cut = mine_3.shape[1] // 2
    left_3 = along(held(theirs_2, sums)[:, :cut])
    right_3 = swapped(held(mine_3, sums)[:, cut:])
    total, mixed = call(
        mine_kernel,
        [jax.ShapeDtypeStruct((tokens, size), jnp.float32) for size in (LANES, mixed_width)],
        acts, mine_2, mine_3, weights, grad_proj,
    )
    places = lax.axis_size("blk")
    return call(
        functools.partial(last_kernel, query_count),
        jax.ShapeDtypeStruct((places * query_count, seq_count // places), jnp.float32),
        acts, theirs_2, left_3, right_3, total, mixed, onehot, sums,
    )


def plain_path(acts, out_grads, basis_in, basis_out, eigvals, query_out, query_in, onehot):
    def whole_sum(part, send_as):
        return swap_sum(swap_sum(part, "rep", jnp.float32), "eig", send_as).astype(jnp.bfloat16)

    in_query = whole_sum(jnp.dot(basis_in, query_in, preferred_element_type=jnp.float32), jnp.float32)
    out_query = whole_sum(
        jnp.dot(basis_out, query_out, preferred_element_type=jnp.float32), jnp.float32
    )
    grad_proj = whole_sum(contract_last(out_grads, basis_out), jnp.bfloat16)
    pack = jnp.concatenate([in_query, eigvals], axis=1)
    scores = plain_scores(acts, basis_in, pack, out_query, grad_proj, onehot.astype(jnp.float32))
    queries, columns = scores.shape
    places = lax.axis_size("blk")
    parts = scores.reshape(queries, places, columns // places)
    return parts.transpose(1, 0, 2).reshape(places * queries, columns // places)


def on_device(acts, out_grads, basis_in, basis_out, eigvals, query_out, query_in, seq_ids, owner):
    rows, features = basis_in.shape
    pairs = query_in.shape[1]
    seq_count = owner.shape[0]
    labels = jnp.arange(seq_count, dtype=jnp.int32)
    column_of = jnp.sum(jnp.where(seq_ids[None, :] == labels[:, None], owner[:, None], 0), axis=0)
    onehot = (labels[:, None] == column_of[None, :]).astype(jnp.bfloat16)
    stepped = (
        all(lax.axis_size(axis) == size for axis, size in zip(AXES, (2, 4, 2, 2)))
        and 2 * rows == LANES
        and features % (4 * LANES) == 0
        and acts.shape[0] % BLOCK == 0
        and pairs == basis_out.shape[0] == LANES
    )
    way = stepped_scores if stepped else plain_path
    parts = way(acts, out_grads, basis_in, basis_out, eigvals, query_out, query_in, onehot)
    own_queries = pairs // R // lax.axis_size(("eig", "rep"))
    own_columns = seq_count // lax.axis_size("blk")
    parts = lax.all_to_all(parts, ("blk", "eig", "rep"), 0, 0, tiled=True)
    return jnp.sum(parts.reshape(-1, own_queries, own_columns), axis=0)


def solution(mesh):
    return jax.shard_map(
        on_device,
        mesh=mesh,
        in_specs=(
            P(("groups", "blk"), ("eig", "rep")),
            P(("groups", "blk"), ("eig", "rep")),
            P("blk", ("eig", "rep")),
            P(None, ("eig", "rep")),
            P("blk", None),
            P(("eig", "rep"), "groups"),
            P(("eig", "rep"), "groups"),
            P(("groups", "blk")),
            P("groups"),
        ),
        out_specs=P(("groups", "eig", "rep"), "blk"),
        check_vma=False,
    )
```

```python
import functools
import itertools

import jax
import jax.numpy as jnp
from jax import lax
from jax.experimental import pallas as pl
from jax.experimental.pallas import tpu as pltpu
from jax.sharding import PartitionSpec as P

R = 32
LANES = 128
BLOCK = 256
VMEM_LIMIT = 16 * 1024 * 1024
AXES = ("groups", "blk", "eig", "rep")


damping = 0.05


def contract_last(left_side, right_side, precision=None):
    return lax.dot_general(
        left_side,
        right_side,
        (((1,), (1,)), ((), ())),
        precision=precision,
        preferred_element_type=jnp.float32,
    )


def swap_sum(value, axis):
    size = lax.axis_size(axis)
    if size & (size - 1):
        return lax.psum(value, axis)
    step = 1
    while step < size:
        pairs = [(i, i ^ step) for i in range(size)]
        value = value + lax.ppermute(value, axis, pairs)
        step *= 2
    return value


def by_distance(value, axis="blk"):
    size = lax.axis_size(axis)
    return [value] + [
        lax.ppermute(value, axis, [(i, i ^ k) for i in range(size)]) for k in range(1, size)
    ]


def held(value, *until):
    return lax.optimization_barrier((value, *until))[0]


def in_hbm(value):
    return pltpu.with_memory_space_constraint(value, pltpu.HBM)


def in_vmem(value):
    return pltpu.with_memory_space_constraint(value, pltpu.VMEM)


def pairing(partner):
    sizes = [lax.axis_size(axis) for axis in AXES]
    places = list(itertools.product(*map(range, sizes)))
    return [(number, places.index(partner(*place))) for number, place in enumerate(places)]


def chunks_kernel(whole_ref, *refs):
    chunk_refs, copied = refs[:4], refs[4]
    columns = chunk_refs[0].shape[1]
    group = lax.axis_index("groups")
    copies = []
    for place, chunk_ref in enumerate(chunk_refs):
        half = group if place < 2 else 1 - group
        begin = pl.multiple_of((2 * half + place % 2) * columns, LANES)
        source = whole_ref.at[:, pl.ds(begin, columns)]
        copies.append(pltpu.make_async_copy(source, chunk_ref, copied.at[place]))
    for copy in copies:
        copy.start()
    for copy in copies:
        copy.wait()


def take_chunks(whole):
    rows, columns = whole.shape
    return pl.pallas_call(
        chunks_kernel,
        in_specs=[pl.BlockSpec(memory_space=pl.ANY)],
        out_shape=[pltpu.VMEM((rows, columns // 4), whole.dtype)] * 4,
        scratch_shapes=[pltpu.SemaphoreType.DMA((4,))],
    )(in_hbm(whole))


def parts_kernel(*refs):
    sources, keep_ref, send_ref, copied = refs[:5], refs[5], refs[6], refs[-1]
    held_refs = out_ref, out_query_ref, in_ref, in_query_ref, grads_ref = refs[7:-2]
    sum_ref = refs[-2]
    copies = [
        pltpu.make_async_copy(source, target, copied.at[place])
        for place, (source, target) in enumerate(zip(sources, held_refs))
    ]
    for copy in copies:
        copy.start()
    rows, width = in_ref.shape[0], out_ref.shape[0]
    copies[0].wait()
    copies[1].wait()
    sum_ref[rows : rows + width] = jnp.dot(
        out_ref[...], out_query_ref[...], preferred_element_type=jnp.float32
    )
    copies[2].wait()
    copies[3].wait()
    sum_ref[:rows] = jnp.dot(in_ref[...], in_query_ref[...], preferred_element_type=jnp.float32)
    copies[4].wait()

    @pl.loop(0, grads_ref.shape[0] // BLOCK)
    def _(step):
        start = pl.multiple_of(step * BLOCK, LANES)
        sum_ref[pl.ds(rows + width + start, BLOCK), :] = contract_last(
            grads_ref[pl.ds(start, BLOCK), :], out_ref[...]
        )

    core, split = lax.axis_index("rep"), rows + width
    half = grads_ref.shape[0] // 2
    for part_ref, whose in ((keep_ref, core), (send_ref, 1 - core)):
        part_ref[:split] = sum_ref[:split]
        start = pl.multiple_of(split + whose * half, 8)
        part_ref[split:] = sum_ref[pl.ds(start, half), :]


def small_parts(basis_in, query_in, basis_out, query_out, out_grads):
    split, tokens, pairs = basis_in.shape[0] + basis_out.shape[0], out_grads.shape[0], query_in.shape[1]
    high = split + tokens
    sources = (basis_out, query_out, basis_in, query_in, out_grads)
    half = jax.ShapeDtypeStruct((split + tokens // 2, pairs), jnp.float32)
    return pl.pallas_call(
        parts_kernel,
        in_specs=[pl.BlockSpec(memory_space=pl.ANY)] * len(sources),
        out_shape=[half, half],
        scratch_shapes=[pltpu.VMEM(source.shape, source.dtype) for source in sources]
        + [pltpu.VMEM((high, pairs), jnp.float32), pltpu.SemaphoreType.DMA((len(sources),))],
        compiler_params=pltpu.CompilerParams(vmem_limit_bytes=VMEM_LIMIT),
    )(*[in_hbm(source) for source in sources])


def weigh(query_count, packs, out_query, weights_ref):
    rows, pairs = packs[0].shape[0], out_query.shape[1]
    query_of = lax.broadcasted_iota(jnp.int32, (rows, pairs), 1) // R
    for slot, pack_ref in enumerate(packs):
        in_query = pack_ref[:, :pairs].astype(jnp.float32)
        inverse = 1.0 / (pack_ref[:, pairs:].astype(jnp.float32) + damping)
        for query in range(query_count):
            own = jnp.where(query_of == query, in_query, 0.0).astype(jnp.bfloat16)
            outer_sum = contract_last(own, out_query)
            weights_ref[slot // 2, pl.ds((2 * query + slot % 2) * rows, rows), :] = (
                outer_sum * inverse
            ).astype(jnp.bfloat16)


def project(acts_ref, start, pieces, group, first=0):
    columns = pl.ds(
        pl.multiple_of(group * (acts_ref.shape[1] // 2) + first, LANES), pieces[0].shape[1]
    )
    stacked = jnp.concatenate([piece[...] for piece in pieces], axis=0)
    return contract_last(acts_ref[pl.ds(start, BLOCK), columns], stacked)


def mixing(start, weights, grad_ref):
    return contract_last(grad_ref[pl.ds(start, BLOCK), :], weights)


def mix(start, projected, mixed, onehot_ref):
    product = jnp.concatenate([projected] * (mixed.shape[1] // LANES), axis=1) * mixed
    high = product.astype(jnp.bfloat16)
    low = (product - high.astype(jnp.float32)).astype(jnp.bfloat16)
    onehot = onehot_ref[:, pl.ds(start, BLOCK)]
    return jnp.dot(onehot, high, preferred_element_type=jnp.float32) + jnp.dot(
        onehot, low, preferred_element_type=jnp.float32
    )


def blocks(tokens, body, initial):
    def step(index, carry):
        return body(pl.multiple_of(index * BLOCK, LANES), carry)

    return lax.fori_loop(0, tokens // BLOCK, step, initial, unroll=True)


def weight_kernel(query_count, *refs):
    packs, (out_query_ref, weights_ref) = refs[:4], refs[4:]
    weigh(query_count, packs, out_query_ref[...], weights_ref)


def first_kernel(source_ref, *refs):
    slots, (total_ref, acts_ref, copied) = refs[:8], refs[8:]
    columns = slots[0].shape[1]
    group = lax.axis_index("groups")
    steps = acts_ref.shape[0] // BLOCK
    parts = 2

    def copies(step):
        size = BLOCK // parts
        places = [pl.ds(step * BLOCK + part * size, size) for part in range(parts)]
        return [
            pltpu.make_async_copy(source_ref.at[place], acts_ref.at[place], copied.at[step, part])
            for part, place in enumerate(places)
        ]

    for copy in copies(0):
        copy.start()
    for step in range(steps):
        for copy in copies(step):
            copy.wait()
        if step + 1 < steps:
            for copy in copies(step + 1):
                copy.start()
        start = step * BLOCK
        total = 0.0
        for place in range(4):
            half = group if place < 2 else 1 - group
            total = total + project(
                acts_ref, start, (slots[place], slots[4 + place]), half, place % 2 * columns
            )
        total_ref[pl.ds(start, BLOCK), :] = total


def mine_kernel(
    acts_ref, mine_2_ref, mine_3_ref, first_ref, weights_ref, grad_ref, onehot_ref,
    total_ref, mixed_ref, sums_ref,
):
    group = lax.axis_index("groups")

    def body(start, sums):
        rows = pl.ds(start, BLOCK)
        total_ref[rows, :] = project(acts_ref, start, (mine_2_ref, mine_3_ref), group)
        mixed_ref[rows, :] = mixing(start, weights_ref[1], grad_ref)
        mixed = mixing(start, weights_ref[0], grad_ref)
        return sums + mix(start, first_ref[rows, :], mixed, onehot_ref)

    sums_ref[...] = blocks(acts_ref.shape[0], body, jnp.zeros(sums_ref.shape, jnp.float32))


def last_kernel(
    query_count, acts_ref, theirs_2_ref, left_ref, right_ref, total_ref, mixed_ref, onehot_ref,
    before_ref, out_ref,
):
    other = 1 - lax.axis_index("groups")
    cut = left_ref.shape[1]

    def body(start, sums):
        total = total_ref[pl.ds(start, BLOCK), :]
        total = total + project(
            acts_ref, start, (theirs_2_ref.at[:, :cut], left_ref), other
        )
        total = total + project(
            acts_ref, start, (theirs_2_ref.at[:, cut:], right_ref), other, cut
        )
        return sums + mix(start, total, mixed_ref[pl.ds(start, BLOCK), :], onehot_ref)

    sums = blocks(acts_ref.shape[0], body, before_ref[...])
    width = sums.shape[1]
    query_of = lax.broadcasted_iota(jnp.int32, (query_count, width), 1) // (width // query_count)
    chosen = query_of == lax.broadcasted_iota(jnp.int32, (query_count, width), 0)
    scores = contract_last(chosen.astype(jnp.float32), sums, precision=lax.Precision.HIGHEST)
    columns = out_ref.shape[1]
    for place in range(out_ref.shape[0] // query_count):
        out_ref[pl.ds(place * query_count, query_count), :] = scores[
            :, place * columns : (place + 1) * columns
        ]


def call(kernel, out_shape, *operands, **options):
    return pl.pallas_call(
        kernel,
        out_shape=out_shape,
        compiler_params=pltpu.CompilerParams(vmem_limit_bytes=VMEM_LIMIT),
        cost_estimate=pl.CostEstimate(flops=1, bytes_accessed=1, transcendentals=0),
        **options,
    )(*operands)


def precondition(in_rows, eig_rows, out_query):
    row_count = in_rows.shape[0]
    basis_width = out_query.shape[0]
    query_count = out_query.shape[1] // R
    outer_sum = jnp.einsum(
        "jqr,iqr->qji",
        in_rows.reshape(row_count, query_count, R),
        out_query.reshape(basis_width, query_count, R),
        preferred_element_type=jnp.float32,
    )
    inverse = 1.0 / (eig_rows.astype(jnp.float32) + damping)
    return (outer_sum * inverse[None, :, :]).astype(jnp.bfloat16)


def plain_scores(acts, basis_in, pack, out_query, grad_proj, onehot):
    pack = lax.all_gather(pack, "blk", axis=0, tiled=True)
    piece = lax.all_gather(basis_in, "blk", axis=0, tiled=True)
    pairs = out_query.shape[1]
    weighted = precondition(pack[:, :pairs], pack[:, pairs:], out_query)
    projected = contract_last(acts, piece)
    per_token = jnp.stack(
        [jnp.sum(projected * contract_last(grad_proj, slab), axis=1) for slab in weighted]
    )
    return contract_last(per_token, onehot, precision=lax.Precision.HIGHEST)


def stepped_scores(
    acts, out_grads, basis_in, basis_out, eigvals, query_out, query_in, onehot
):
    rows, width = basis_in.shape[0], basis_out.shape[0]
    tokens, seq_count = acts.shape[0], onehot.shape[0]
    query_count = query_in.shape[1] // R
    pair = [(0, 1), (1, 0)]
    place = lax.axis_index("blk")
    inner = (place == 1) | (place == 2)

    def along(value):
        return lax.ppermute(value, "blk", [(i, i ^ 1) for i in range(4)])

    def swapped(value):
        return lax.ppermute(value, "groups", pair)

    def across(value, at_ends):
        return lax.ppermute(
            value,
            AXES,
            pairing(lambda g, b, e, r: (g, 3 - b, e, r) if b in (1, 2) else at_ends(g, b, e, r)),
        )

    chunks = take_chunks(basis_in)
    half, other_half = chunks[:2], chunks[2:]
    to_core = lambda g, b, e, r: (g, b, e, 1 - r)
    over_y = lambda g, b, e, r: (1 - g, b, e, r)
    mine_1, middle_3 = [], []
    for chunk in half:
        middle_3.append(across(chunk, to_core))
        mine_1.append(along(chunk))

    split = rows + width
    keep, send = small_parts(held(basis_in, *half), query_in, basis_out, query_out, out_grads)
    other = lax.ppermute(send, "rep", pair)
    keep = keep + held(other, *mine_1, *middle_3)
    small, grad_half = keep[:split], keep[split:]
    small_other = lax.ppermute(small, "eig", pair)
    grad_other = lax.ppermute(grad_half, "eig", pair)

    arrived = []
    for after, first, middle, rest in zip((half[0], keep), mine_1, middle_3, other_half):
        from_pair = along(jnp.where(inner, middle, held(rest, first, after)))
        from_across = across(held(first, middle, after), over_y)
        arrived.append((from_pair, from_across))

    small = (small + held(small_other, *arrived[0])).astype(jnp.bfloat16)
    in_query, out_query = small[:rows], small[rows:]
    packs = by_distance(jnp.concatenate([in_query, eigvals], axis=1))

    ready = [chunk for both in arrived for chunk in both] + packs[1:]
    mine_2 = jnp.concatenate(
        [jnp.where(inner, held(there, *ready), here) for here, there in arrived], axis=1
    )
    theirs_1 = [
        jnp.where(inner, held(here, mine_2), held(there, mine_2)) for here, there in arrived
    ]
    theirs_2 = swapped(mine_2)
    mine_3 = along(mine_2)

    grad_half = (grad_half + held(grad_other, mine_2)).astype(jnp.bfloat16)
    grad_other = lax.ppermute(grad_half, "rep", pair)
    of_first = lax.axis_index("rep") == 0
    grad_proj = jnp.concatenate(
        [
            jnp.where(of_first, grad_half, grad_other),
            jnp.where(of_first, grad_other, grad_half),
        ],
        axis=0,
    )
    total_shape = jax.ShapeDtypeStruct((tokens, LANES), jnp.float32)
    first_total, acts = call(
        first_kernel,
        [total_shape, pltpu.VMEM(acts.shape, acts.dtype)],
        in_hbm(held(acts, grad_half)), *half, *other_half, *mine_1, *theirs_1,
        in_specs=[pl.BlockSpec(memory_space=pl.ANY)]
        + [pl.BlockSpec(memory_space=pltpu.VMEM)] * 8,
        scratch_shapes=[pltpu.SemaphoreType.DMA((tokens // BLOCK, 2))],
    )
    acts = in_vmem(acts)

    cut = mine_3.shape[1] // 2
    left_3 = along(held(theirs_2, first_total)[:, :cut])
    right_3 = swapped(held(mine_3, first_total)[:, cut:])
    mixed_width = 2 * query_count * rows
    weights = call(
        functools.partial(weight_kernel, query_count),
        jax.ShapeDtypeStruct((2, mixed_width, width), jnp.bfloat16),
        *packs, out_query,
    )
    total, mixed, sums = call(
        mine_kernel,
        [
            total_shape,
            jax.ShapeDtypeStruct((tokens, mixed_width), jnp.float32),
            jax.ShapeDtypeStruct((seq_count, mixed_width), jnp.float32),
        ],
        acts, mine_2, mine_3, first_total, weights, grad_proj, onehot,
    )
    places = lax.axis_size("blk")
    return call(
        functools.partial(last_kernel, query_count),
        jax.ShapeDtypeStruct((places * query_count, seq_count // places), jnp.float32),
        acts, theirs_2, left_3, right_3, total, mixed, onehot, sums,
    )


def plain_path(acts, out_grads, basis_in, basis_out, eigvals, query_out, query_in, onehot):
    def whole_sum(part):
        return swap_sum(swap_sum(part, "rep"), "eig").astype(jnp.bfloat16)

    in_query = whole_sum(jnp.dot(basis_in, query_in, preferred_element_type=jnp.float32))
    out_query = whole_sum(jnp.dot(basis_out, query_out, preferred_element_type=jnp.float32))
    grad_proj = whole_sum(contract_last(out_grads, basis_out))
    pack = jnp.concatenate([in_query, eigvals], axis=1)
    scores = plain_scores(acts, basis_in, pack, out_query, grad_proj, onehot.astype(jnp.float32))
    queries, columns = scores.shape
    places = lax.axis_size("blk")
    parts = scores.reshape(queries, places, columns // places)
    return parts.transpose(1, 0, 2).reshape(places * queries, columns // places)


def on_device(acts, out_grads, basis_in, basis_out, eigvals, query_out, query_in, seq_ids, owner):
    rows, features = basis_in.shape
    pairs = query_in.shape[1]
    seq_count = owner.shape[0]
    labels = jnp.arange(seq_count, dtype=jnp.int32)
    column_of = jnp.sum(jnp.where(seq_ids[None, :] == labels[:, None], owner[:, None], 0), axis=0)
    onehot = (labels[:, None] == column_of[None, :]).astype(jnp.bfloat16)
    stepped = (
        all(lax.axis_size(axis) == size for axis, size in zip(AXES, (2, 4, 2, 2)))
        and 2 * rows == LANES
        and (rows + basis_out.shape[0]) % 16 == acts.shape[0] % 32 == 0
        and features % (4 * LANES) == 0
        and acts.shape[0] % BLOCK == 0
        and pairs == basis_out.shape[0] == LANES
    )
    way = stepped_scores if stepped else plain_path
    parts = way(acts, out_grads, basis_in, basis_out, eigvals, query_out, query_in, onehot)
    own_queries = pairs // R // lax.axis_size(("eig", "rep"))
    own_columns = seq_count // lax.axis_size("blk")
    parts = lax.all_to_all(parts, ("blk", "eig", "rep"), 0, 0, tiled=True)
    return jnp.sum(parts.reshape(-1, own_queries, own_columns), axis=0)


def solution(mesh):
    return jax.shard_map(
        on_device,
        mesh=mesh,
        in_specs=(
            P(("groups", "blk"), ("eig", "rep")),
            P(("groups", "blk"), ("eig", "rep")),
            P("blk", ("eig", "rep")),
            P(None, ("eig", "rep")),
            P("blk", None),
            P(("eig", "rep"), "groups"),
            P(("eig", "rep"), "groups"),
            P(("groups", "blk")),
            P("groups"),
        ),
        out_specs=P(("groups", "eig", "rep"), "blk"),
        check_vma=False,
    )
```

```python
import functools
import itertools

import jax
import jax.numpy as jnp
from jax import lax
from jax.experimental import pallas as pl
from jax.experimental.pallas import tpu as pltpu
from jax.sharding import PartitionSpec as P

R = 32
LANES = 128
BLOCK = 256
VMEM_LIMIT = 16 * 1024 * 1024
AXES = ("groups", "blk", "eig", "rep")


damping = 0.05


def contract_last(left_side, right_side, precision=None):
    return lax.dot_general(
        left_side,
        right_side,
        (((1,), (1,)), ((), ())),
        precision=precision,
        preferred_element_type=jnp.float32,
    )


def swap_sum(value, axis):
    size = lax.axis_size(axis)
    if size & (size - 1):
        return lax.psum(value, axis)
    step = 1
    while step < size:
        pairs = [(i, i ^ step) for i in range(size)]
        value = value + lax.ppermute(value, axis, pairs)
        step *= 2
    return value


def by_distance(value, axis="blk"):
    size = lax.axis_size(axis)
    return [value] + [
        lax.ppermute(value, axis, [(i, i ^ k) for i in range(size)]) for k in range(1, size)
    ]


def held(value, *until):
    return lax.optimization_barrier((value, *until))[0]


def in_hbm(value):
    return pltpu.with_memory_space_constraint(value, pltpu.HBM)


def in_vmem(value):
    return pltpu.with_memory_space_constraint(value, pltpu.VMEM)


def pairing(partner):
    sizes = [lax.axis_size(axis) for axis in AXES]
    places = list(itertools.product(*map(range, sizes)))
    return [(number, places.index(partner(*place))) for number, place in enumerate(places)]


def chunks_kernel(whole_ref, *refs):
    chunk_refs, copied = refs[:4], refs[4]
    columns = chunk_refs[0].shape[1]
    group = lax.axis_index("groups")
    copies = []
    for place, chunk_ref in enumerate(chunk_refs):
        half = group if place < 2 else 1 - group
        begin = pl.multiple_of((2 * half + place % 2) * columns, LANES)
        source = whole_ref.at[:, pl.ds(begin, columns)]
        copies.append(pltpu.make_async_copy(source, chunk_ref, copied.at[place]))
    for copy in copies:
        copy.start()
    for copy in copies:
        copy.wait()


def take_chunks(whole):
    rows, columns = whole.shape
    return pl.pallas_call(
        chunks_kernel,
        in_specs=[pl.BlockSpec(memory_space=pl.ANY)],
        out_shape=[pltpu.VMEM((rows, columns // 4), whole.dtype)] * 4,
        scratch_shapes=[pltpu.SemaphoreType.DMA((4,))],
    )(in_hbm(whole))


def cut_copies(source, target, copied, parts):
    size = source.shape[0] // parts
    places = [pl.ds(part * size, size) for part in range(parts)]
    return [
        pltpu.make_async_copy(source.at[place], target.at[place], copied.at[part])
        for part, place in enumerate(places)
    ]


def parts_kernel(*refs):
    sources, keep_ref, send_ref, copied = refs[:5], refs[5], refs[6], refs[-1]
    held_refs = out_ref, out_query_ref, in_ref, in_query_ref, grads_ref = refs[7:-2]
    sum_ref = refs[-2]
    copies = [
        cut_copies(source, target, copied.at[place], parts)
        for place, (source, target, parts) in enumerate(zip(sources, held_refs, (1, 1, 2, 4, 8)))
    ]
    for group in copies:
        for copy in group:
            copy.start()

    def wait(*places):
        for place in places:
            for copy in copies[place]:
                copy.wait()

    rows, width = in_ref.shape[0], out_ref.shape[0]
    wait(0, 1)
    sum_ref[rows : rows + width] = jnp.dot(
        out_ref[...], out_query_ref[...], preferred_element_type=jnp.float32
    )
    wait(2, 3)
    sum_ref[:rows] = jnp.dot(in_ref[...], in_query_ref[...], preferred_element_type=jnp.float32)
    wait(4)

    @pl.loop(0, grads_ref.shape[0] // BLOCK)
    def _(step):
        start = pl.multiple_of(step * BLOCK, LANES)
        sum_ref[pl.ds(rows + width + start, BLOCK), :] = contract_last(
            grads_ref[pl.ds(start, BLOCK), :], out_ref[...]
        )

    core, split = lax.axis_index("rep"), rows + width
    half = grads_ref.shape[0] // 2
    for part_ref, whose in ((keep_ref, core), (send_ref, 1 - core)):
        part_ref[:split] = sum_ref[:split]
        start = pl.multiple_of(split + whose * half, 8)
        part_ref[split:] = sum_ref[pl.ds(start, half), :]


def small_parts(basis_in, query_in, basis_out, query_out, out_grads):
    split, tokens, pairs = basis_in.shape[0] + basis_out.shape[0], out_grads.shape[0], query_in.shape[1]
    high = split + tokens
    sources = (basis_out, query_out, basis_in, query_in, out_grads)
    half = jax.ShapeDtypeStruct((split + tokens // 2, pairs), jnp.float32)
    return pl.pallas_call(
        parts_kernel,
        in_specs=[pl.BlockSpec(memory_space=pl.ANY)] * len(sources),
        out_shape=[half, half],
        scratch_shapes=[pltpu.VMEM(source.shape, source.dtype) for source in sources]
        + [pltpu.VMEM((high, pairs), jnp.float32), pltpu.SemaphoreType.DMA((len(sources), 8))],
        compiler_params=pltpu.CompilerParams(vmem_limit_bytes=VMEM_LIMIT),
    )(*[in_hbm(source) for source in sources])


def weigh(query_count, packs, out_query, weights_ref):
    rows, pairs = packs[0].shape[0], out_query.shape[1]
    query_of = lax.broadcasted_iota(jnp.int32, (rows, pairs), 1) // R
    for slot, pack_ref in enumerate(packs):
        in_query = pack_ref[:, :pairs].astype(jnp.float32)
        inverse = 1.0 / (pack_ref[:, pairs:].astype(jnp.float32) + damping)
        for query in range(query_count):
            own = jnp.where(query_of == query, in_query, 0.0).astype(jnp.bfloat16)
            outer_sum = contract_last(own, out_query)
            weights_ref[slot // 2, pl.ds((2 * query + slot % 2) * rows, rows), :] = (
                outer_sum * inverse
            ).astype(jnp.bfloat16)


def project(acts_ref, start, pieces, group, first=0):
    columns = pl.ds(
        pl.multiple_of(group * (acts_ref.shape[1] // 2) + first, LANES), pieces[0].shape[1]
    )
    stacked = jnp.concatenate([piece[...] for piece in pieces], axis=0)
    return contract_last(acts_ref[pl.ds(start, BLOCK), columns], stacked)


def mixing(start, weights, grad_ref):
    return contract_last(grad_ref[pl.ds(start, BLOCK), :], weights)


def mix(start, projected, mixed, onehot_ref):
    product = jnp.concatenate([projected] * (mixed.shape[1] // LANES), axis=1) * mixed
    high = product.astype(jnp.bfloat16)
    low = (product - high.astype(jnp.float32)).astype(jnp.bfloat16)
    onehot = onehot_ref[:, pl.ds(start, BLOCK)]
    return jnp.dot(onehot, high, preferred_element_type=jnp.float32) + jnp.dot(
        onehot, low, preferred_element_type=jnp.float32
    )


def blocks(tokens, body, initial):
    def step(index, carry):
        return body(pl.multiple_of(index * BLOCK, LANES), carry)

    return lax.fori_loop(0, tokens // BLOCK, step, initial, unroll=True)


def weight_kernel(query_count, *refs):
    packs, (out_query_ref, weights_ref) = refs[:4], refs[4:]
    weigh(query_count, packs, out_query_ref[...], weights_ref)


def first_kernel(source_ref, *refs):
    slots, (total_ref, acts_ref, copied) = refs[:8], refs[8:]
    columns = slots[0].shape[1]
    group = lax.axis_index("groups")
    steps = acts_ref.shape[0] // BLOCK
    parts = 8

    def copies(step):
        size = BLOCK // parts
        places = [pl.ds(step * BLOCK + part * size, size) for part in range(parts)]
        return [
            pltpu.make_async_copy(source_ref.at[place], acts_ref.at[place], copied.at[step, part])
            for part, place in enumerate(places)
        ]

    for copy in copies(0):
        copy.start()
    for step in range(steps):
        for copy in copies(step):
            copy.wait()
        if step + 1 < steps:
            for copy in copies(step + 1):
                copy.start()
        start = step * BLOCK
        total = 0.0
        for place in range(4):
            half = group if place < 2 else 1 - group
            total = total + project(
                acts_ref, start, (slots[place], slots[4 + place]), half, place % 2 * columns
            )
        total_ref[pl.ds(start, BLOCK), :] = total


def mine_kernel(
    acts_ref, mine_2_ref, mine_3_ref, first_ref, weights_ref, grad_ref, onehot_ref,
    total_ref, mixed_ref, sums_ref,
):
    group = lax.axis_index("groups")

    def body(start, sums):
        rows = pl.ds(start, BLOCK)
        total_ref[rows, :] = project(acts_ref, start, (mine_2_ref, mine_3_ref), group)
        mixed_ref[rows, :] = mixing(start, weights_ref[1], grad_ref)
        mixed = mixing(start, weights_ref[0], grad_ref)
        return sums + mix(start, first_ref[rows, :], mixed, onehot_ref)

    sums_ref[...] = blocks(acts_ref.shape[0], body, jnp.zeros(sums_ref.shape, jnp.float32))


def last_kernel(
    query_count, acts_ref, theirs_2_ref, left_ref, right_ref, total_ref, mixed_ref, onehot_ref,
    before_ref, out_ref,
):
    other = 1 - lax.axis_index("groups")
    cut = left_ref.shape[1]

    def body(start, sums):
        total = total_ref[pl.ds(start, BLOCK), :]
        total = total + project(
            acts_ref, start, (theirs_2_ref.at[:, :cut], left_ref), other
        )
        total = total + project(
            acts_ref, start, (theirs_2_ref.at[:, cut:], right_ref), other, cut
        )
        return sums + mix(start, total, mixed_ref[pl.ds(start, BLOCK), :], onehot_ref)

    sums = blocks(acts_ref.shape[0], body, before_ref[...])
    width = sums.shape[1]
    query_of = lax.broadcasted_iota(jnp.int32, (query_count, width), 1) // (width // query_count)
    chosen = query_of == lax.broadcasted_iota(jnp.int32, (query_count, width), 0)
    scores = contract_last(chosen.astype(jnp.float32), sums, precision=lax.Precision.HIGHEST)
    columns = out_ref.shape[1]
    for place in range(out_ref.shape[0] // query_count):
        out_ref[pl.ds(place * query_count, query_count), :] = scores[
            :, place * columns : (place + 1) * columns
        ]


def call(kernel, out_shape, *operands, **options):
    return pl.pallas_call(
        kernel,
        out_shape=out_shape,
        compiler_params=pltpu.CompilerParams(vmem_limit_bytes=VMEM_LIMIT),
        cost_estimate=pl.CostEstimate(flops=1, bytes_accessed=1, transcendentals=0),
        **options,
    )(*operands)


def precondition(in_rows, eig_rows, out_query):
    row_count = in_rows.shape[0]
    basis_width = out_query.shape[0]
    query_count = out_query.shape[1] // R
    outer_sum = jnp.einsum(
        "jqr,iqr->qji",
        in_rows.reshape(row_count, query_count, R),
        out_query.reshape(basis_width, query_count, R),
        preferred_element_type=jnp.float32,
    )
    inverse = 1.0 / (eig_rows.astype(jnp.float32) + damping)
    return (outer_sum * inverse[None, :, :]).astype(jnp.bfloat16)


def plain_scores(acts, basis_in, pack, out_query, grad_proj, onehot):
    pack = lax.all_gather(pack, "blk", axis=0, tiled=True)
    piece = lax.all_gather(basis_in, "blk", axis=0, tiled=True)
    pairs = out_query.shape[1]
    weighted = precondition(pack[:, :pairs], pack[:, pairs:], out_query)
    projected = contract_last(acts, piece)
    per_token = jnp.stack(
        [jnp.sum(projected * contract_last(grad_proj, slab), axis=1) for slab in weighted]
    )
    return contract_last(per_token, onehot, precision=lax.Precision.HIGHEST)


def stepped_scores(
    acts, out_grads, basis_in, basis_out, eigvals, query_out, query_in, onehot
):
    rows, width = basis_in.shape[0], basis_out.shape[0]
    tokens, seq_count = acts.shape[0], onehot.shape[0]
    query_count = query_in.shape[1] // R
    pair = [(0, 1), (1, 0)]
    place = lax.axis_index("blk")
    inner = (place == 1) | (place == 2)

    def along(value):
        return lax.ppermute(value, "blk", [(i, i ^ 1) for i in range(4)])

    def swapped(value):
        return lax.ppermute(value, "groups", pair)

    def across(value, at_ends):
        return lax.ppermute(
            value,
            AXES,
            pairing(lambda g, b, e, r: (g, 3 - b, e, r) if b in (1, 2) else at_ends(g, b, e, r)),
        )

    chunks = take_chunks(basis_in)
    half, other_half = chunks[:2], chunks[2:]
    to_core = lambda g, b, e, r: (g, b, e, 1 - r)
    over_y = lambda g, b, e, r: (1 - g, b, e, r)
    mine_1, middle_3 = [], []
    for chunk in half:
        middle_3.append(across(chunk, to_core))
        mine_1.append(along(chunk))

    split = rows + width
    keep, send = small_parts(held(basis_in, *half), query_in, basis_out, query_out, out_grads)
    other = lax.ppermute(send, "rep", pair)
    keep = keep + held(other, *mine_1, *middle_3)
    other = lax.ppermute(keep, "eig", pair)

    arrived = []
    for after, first, middle, rest in zip((half[0], keep), mine_1, middle_3, other_half):
        from_pair = along(jnp.where(inner, middle, held(rest, first, after)))
        from_across = across(held(first, middle, after), over_y)
        arrived.append((from_pair, from_across))

    ready = [chunk for both in arrived for chunk in both]
    mine_2 = jnp.concatenate(
        [jnp.where(inner, held(there, *ready), here) for here, there in arrived], axis=1
    )
    theirs_1 = [
        jnp.where(inner, held(here, mine_2), held(there, mine_2)) for here, there in arrived
    ]
    theirs_2 = swapped(mine_2)
    mine_3 = along(mine_2)

    small = (keep + held(other, mine_2)).astype(jnp.bfloat16)
    in_query, out_query, grad_half = small[:rows], small[rows:split], small[split:]
    packs = by_distance(jnp.concatenate([in_query, eigvals], axis=1))
    grad_other = lax.ppermute(grad_half, "rep", pair)
    of_first = lax.axis_index("rep") == 0
    grad_proj = jnp.concatenate(
        [
            jnp.where(of_first, grad_half, grad_other),
            jnp.where(of_first, grad_other, grad_half),
        ],
        axis=0,
    )
    total_shape = jax.ShapeDtypeStruct((tokens, LANES), jnp.float32)
    first_total, acts = call(
        first_kernel,
        [total_shape, pltpu.VMEM(acts.shape, acts.dtype)],
        in_hbm(held(acts, grad_half)), *half, *other_half, *mine_1, *theirs_1,
        in_specs=[pl.BlockSpec(memory_space=pl.ANY)]
        + [pl.BlockSpec(memory_space=pltpu.VMEM)] * 8,
        scratch_shapes=[pltpu.SemaphoreType.DMA((tokens // BLOCK, 8))],
    )
    acts = in_vmem(acts)

    cut = mine_3.shape[1] // 2
    left_3 = along(held(theirs_2, first_total, *packs[1:])[:, :cut])
    right_3 = swapped(held(mine_3, first_total, *packs[1:])[:, cut:])
    mixed_width = 2 * query_count * rows
    weights = call(
        functools.partial(weight_kernel, query_count),
        jax.ShapeDtypeStruct((2, mixed_width, width), jnp.bfloat16),
        *packs, out_query,
    )
    total, mixed, sums = call(
        mine_kernel,
        [
            total_shape,
            jax.ShapeDtypeStruct((tokens, mixed_width), jnp.float32),
            jax.ShapeDtypeStruct((seq_count, mixed_width), jnp.float32),
        ],
        acts, mine_2, mine_3, first_total, weights, grad_proj, onehot,
    )
    places = lax.axis_size("blk")
    return call(
        functools.partial(last_kernel, query_count),
        jax.ShapeDtypeStruct((places * query_count, seq_count // places), jnp.float32),
        acts, theirs_2, left_3, right_3, total, mixed, onehot, sums,
    )


def plain_path(acts, out_grads, basis_in, basis_out, eigvals, query_out, query_in, onehot):
    def whole_sum(part):
        return swap_sum(swap_sum(part, "rep"), "eig").astype(jnp.bfloat16)

    in_query = whole_sum(jnp.dot(basis_in, query_in, preferred_element_type=jnp.float32))
    out_query = whole_sum(jnp.dot(basis_out, query_out, preferred_element_type=jnp.float32))
    grad_proj = whole_sum(contract_last(out_grads, basis_out))
    pack = jnp.concatenate([in_query, eigvals], axis=1)
    scores = plain_scores(acts, basis_in, pack, out_query, grad_proj, onehot.astype(jnp.float32))
    queries, columns = scores.shape
    places = lax.axis_size("blk")
    parts = scores.reshape(queries, places, columns // places)
    return parts.transpose(1, 0, 2).reshape(places * queries, columns // places)


def on_device(acts, out_grads, basis_in, basis_out, eigvals, query_out, query_in, seq_ids, owner):
    rows, features = basis_in.shape
    pairs = query_in.shape[1]
    seq_count = owner.shape[0]
    labels = jnp.arange(seq_count, dtype=jnp.int32)
    column_of = jnp.sum(jnp.where(seq_ids[None, :] == labels[:, None], owner[:, None], 0), axis=0)
    onehot = (labels[:, None] == column_of[None, :]).astype(jnp.bfloat16)
    stepped = (
        all(lax.axis_size(axis) == size for axis, size in zip(AXES, (2, 4, 2, 2)))
        and 2 * rows == LANES
        and (rows + basis_out.shape[0]) % 16 == acts.shape[0] % 32 == 0
        and features % (4 * LANES) == 0
        and acts.shape[0] % BLOCK == 0
        and pairs == basis_out.shape[0] == LANES
    )
    way = stepped_scores if stepped else plain_path
    parts = way(acts, out_grads, basis_in, basis_out, eigvals, query_out, query_in, onehot)
    own_queries = pairs // R // lax.axis_size(("eig", "rep"))
    own_columns = seq_count // lax.axis_size("blk")
    parts = lax.all_to_all(parts, ("blk", "eig", "rep"), 0, 0, tiled=True)
    return jnp.sum(parts.reshape(-1, own_queries, own_columns), axis=0)


def solution(mesh):
    return jax.shard_map(
        on_device,
        mesh=mesh,
        in_specs=(
            P(("groups", "blk"), ("eig", "rep")),
            P(("groups", "blk"), ("eig", "rep")),
            P("blk", ("eig", "rep")),
            P(None, ("eig", "rep")),
            P("blk", None),
            P(("eig", "rep"), "groups"),
            P(("eig", "rep"), "groups"),
            P(("groups", "blk")),
            P("groups"),
        ),
        out_specs=P(("groups", "eig", "rep"), "blk"),
        check_vma=False,
    )
```

```python
import functools
import itertools

import jax
import jax.numpy as jnp
from jax import lax
from jax.experimental import pallas as pl
from jax.experimental.pallas import tpu as pltpu
from jax.sharding import PartitionSpec as P

R = 32
LANES = 128
BLOCK = 256
VMEM_LIMIT = 16 * 1024 * 1024
AXES = ("groups", "blk", "eig", "rep")


damping = 0.05


def contract_last(left_side, right_side, precision=None):
    return lax.dot_general(
        left_side,
        right_side,
        (((1,), (1,)), ((), ())),
        precision=precision,
        preferred_element_type=jnp.float32,
    )


def swap_sum(value, axis):
    size = lax.axis_size(axis)
    if size & (size - 1):
        return lax.psum(value, axis)
    step = 1
    while step < size:
        pairs = [(i, i ^ step) for i in range(size)]
        value = value + lax.ppermute(value, axis, pairs)
        step *= 2
    return value


def by_distance(value, axis="blk"):
    size = lax.axis_size(axis)
    return [value] + [
        lax.ppermute(value, axis, [(i, i ^ k) for i in range(size)]) for k in range(1, size)
    ]


def held(value, *until):
    return lax.optimization_barrier((value, *until))[0]


def in_hbm(value):
    return pltpu.with_memory_space_constraint(value, pltpu.HBM)


def in_vmem(value):
    return pltpu.with_memory_space_constraint(value, pltpu.VMEM)


def pairing(partner):
    sizes = [lax.axis_size(axis) for axis in AXES]
    places = list(itertools.product(*map(range, sizes)))
    return [(number, places.index(partner(*place))) for number, place in enumerate(places)]


def chunks_kernel(whole_ref, *refs):
    chunk_refs, copied = refs[:4], refs[4]
    columns = chunk_refs[0].shape[1]
    group = lax.axis_index("groups")
    copies = []
    for place, chunk_ref in enumerate(chunk_refs):
        half = group if place < 2 else 1 - group
        begin = pl.multiple_of((2 * half + place % 2) * columns, LANES)
        source = whole_ref.at[:, pl.ds(begin, columns)]
        copies.append(pltpu.make_async_copy(source, chunk_ref, copied.at[place]))
    for copy in copies:
        copy.start()
    for copy in copies:
        copy.wait()


def take_chunks(whole):
    rows, columns = whole.shape
    return pl.pallas_call(
        chunks_kernel,
        in_specs=[pl.BlockSpec(memory_space=pl.ANY)],
        out_shape=[pltpu.VMEM((rows, columns // 4), whole.dtype)] * 4,
        scratch_shapes=[pltpu.SemaphoreType.DMA((4,))],
    )(in_hbm(whole))


def cut_copies(source, target, copied, parts):
    size = source.shape[0] // parts
    places = [pl.ds(part * size, size) for part in range(parts)]
    return [
        pltpu.make_async_copy(source.at[place], target.at[place], copied.at[part])
        for part, place in enumerate(places)
    ]


def parts_kernel(*refs):
    sources, keep_ref, send_ref, copied = refs[:5], refs[5], refs[6], refs[-1]
    held_refs = out_ref, out_query_ref, in_ref, in_query_ref, grads_ref = refs[7:-2]
    sum_ref = refs[-2]
    copies = [
        cut_copies(source, target, copied.at[place], parts)
        for place, (source, target, parts) in enumerate(zip(sources, held_refs, (1, 1, 2, 4, 4)))
    ]
    for group in copies:
        for copy in group:
            copy.start()

    def wait(*places):
        for place in places:
            for copy in copies[place]:
                copy.wait()

    rows, width = in_ref.shape[0], out_ref.shape[0]
    wait(0, 1)
    sum_ref[rows : rows + width] = jnp.dot(
        out_ref[...], out_query_ref[...], preferred_element_type=jnp.float32
    )
    wait(2, 3)
    sum_ref[:rows] = jnp.dot(in_ref[...], in_query_ref[...], preferred_element_type=jnp.float32)
    blocks_copied = copies[4]
    size = grads_ref.shape[0] // len(blocks_copied)

    @pl.loop(0, len(blocks_copied))
    def _(step):
        start = pl.multiple_of(step * size, 16)
        place = pl.ds(start, size)
        pltpu.make_async_copy(
            sources[4].at[place], grads_ref.at[place], copied.at[4, step]
        ).wait()
        sum_ref[pl.ds(rows + width + start, size), :] = contract_last(
            grads_ref[place, :], out_ref[...]
        )

    core, split = lax.axis_index("rep"), rows + width
    half = grads_ref.shape[0] // 2
    for part_ref, whose in ((keep_ref, core), (send_ref, 1 - core)):
        part_ref[:split] = sum_ref[:split]
        start = pl.multiple_of(split + whose * half, 8)
        part_ref[split:] = sum_ref[pl.ds(start, half), :]


def small_parts(basis_in, query_in, basis_out, query_out, out_grads):
    split, tokens, pairs = basis_in.shape[0] + basis_out.shape[0], out_grads.shape[0], query_in.shape[1]
    high = split + tokens
    sources = (basis_out, query_out, basis_in, query_in, out_grads)
    half = jax.ShapeDtypeStruct((split + tokens // 2, pairs), jnp.float32)
    return pl.pallas_call(
        parts_kernel,
        in_specs=[pl.BlockSpec(memory_space=pl.ANY)] * len(sources),
        out_shape=[half, half],
        scratch_shapes=[pltpu.VMEM(source.shape, source.dtype) for source in sources]
        + [pltpu.VMEM((high, pairs), jnp.float32), pltpu.SemaphoreType.DMA((len(sources), 8))],
        compiler_params=pltpu.CompilerParams(vmem_limit_bytes=VMEM_LIMIT),
    )(*[in_hbm(source) for source in sources])


def weigh(query_count, packs, out_query, weights_ref):
    rows, pairs = packs[0].shape[0], out_query.shape[1]
    query_of = lax.broadcasted_iota(jnp.int32, (rows, pairs), 1) // R
    for slot, pack_ref in enumerate(packs):
        in_query = pack_ref[:, :pairs].astype(jnp.float32)
        inverse = 1.0 / (pack_ref[:, pairs:].astype(jnp.float32) + damping)
        for query in range(query_count):
            own = jnp.where(query_of == query, in_query, 0.0).astype(jnp.bfloat16)
            outer_sum = contract_last(own, out_query)
            weights_ref[slot // 2, pl.ds((2 * query + slot % 2) * rows, rows), :] = (
                outer_sum * inverse
            ).astype(jnp.bfloat16)


def project(acts_ref, start, pieces, group, first=0):
    columns = pl.ds(
        pl.multiple_of(group * (acts_ref.shape[1] // 2) + first, LANES), pieces[0].shape[1]
    )
    stacked = jnp.concatenate([piece[...] for piece in pieces], axis=0)
    return contract_last(acts_ref[pl.ds(start, BLOCK), columns], stacked)


def mixing(start, weights, grad_ref):
    return contract_last(grad_ref[pl.ds(start, BLOCK), :], weights)


def mix(start, projected, mixed, onehot_ref):
    product = jnp.concatenate([projected] * (mixed.shape[1] // LANES), axis=1) * mixed
    high = product.astype(jnp.bfloat16)
    low = (product - high.astype(jnp.float32)).astype(jnp.bfloat16)
    onehot = onehot_ref[:, pl.ds(start, BLOCK)]
    return jnp.dot(onehot, high, preferred_element_type=jnp.float32) + jnp.dot(
        onehot, low, preferred_element_type=jnp.float32
    )


def blocks(tokens, body, initial):
    def step(index, carry):
        return body(pl.multiple_of(index * BLOCK, LANES), carry)

    return lax.fori_loop(0, tokens // BLOCK, step, initial, unroll=True)


def weight_kernel(query_count, *refs):
    packs, (out_query_ref, weights_ref) = refs[:4], refs[4:]
    weigh(query_count, packs, out_query_ref[...], weights_ref)


def first_kernel(source_ref, *refs):
    slots, (total_ref, acts_ref, copied) = refs[:8], refs[8:]
    columns = slots[0].shape[1]
    group = lax.axis_index("groups")
    steps = acts_ref.shape[0] // BLOCK
    parts = 8

    def copies(step):
        size = BLOCK // parts
        begin = pl.multiple_of(step * BLOCK, BLOCK)
        places = [pl.ds(begin + part * size, size) for part in range(parts)]
        return [
            pltpu.make_async_copy(source_ref.at[place], acts_ref.at[place], copied.at[step, part])
            for part, place in enumerate(places)
        ]

    for copy in copies(0):
        copy.start()

    @pl.loop(0, steps)
    def _(step):
        for copy in copies(step):
            copy.wait()

        @pl.when(step + 1 < steps)
        def _():
            for copy in copies(step + 1):
                copy.start()

        start = pl.multiple_of(step * BLOCK, LANES)
        total = 0.0
        for place in range(4):
            half = group if place < 2 else 1 - group
            total = total + project(
                acts_ref, start, (slots[place], slots[4 + place]), half, place % 2 * columns
            )
        total_ref[pl.ds(start, BLOCK), :] = total


def mine_kernel(
    acts_ref, mine_2_ref, mine_3_ref, first_ref, weights_ref, grad_ref, onehot_ref,
    total_ref, mixed_ref, sums_ref,
):
    group = lax.axis_index("groups")

    def body(start, sums):
        rows = pl.ds(start, BLOCK)
        total_ref[rows, :] = project(acts_ref, start, (mine_2_ref, mine_3_ref), group)
        mixed_ref[rows, :] = mixing(start, weights_ref[1], grad_ref)
        mixed = mixing(start, weights_ref[0], grad_ref)
        return sums + mix(start, first_ref[rows, :], mixed, onehot_ref)

    sums_ref[...] = blocks(acts_ref.shape[0], body, jnp.zeros(sums_ref.shape, jnp.float32))


def last_kernel(
    query_count, acts_ref, theirs_2_ref, left_ref, right_ref, total_ref, mixed_ref, onehot_ref,
    before_ref, out_ref,
):
    other = 1 - lax.axis_index("groups")
    cut = left_ref.shape[1]

    def body(start, sums):
        total = total_ref[pl.ds(start, BLOCK), :]
        total = total + project(
            acts_ref, start, (theirs_2_ref.at[:, :cut], left_ref), other
        )
        total = total + project(
            acts_ref, start, (theirs_2_ref.at[:, cut:], right_ref), other, cut
        )
        return sums + mix(start, total, mixed_ref[pl.ds(start, BLOCK), :], onehot_ref)

    sums = blocks(acts_ref.shape[0], body, before_ref[...])
    width = sums.shape[1]
    query_of = lax.broadcasted_iota(jnp.int32, (query_count, width), 1) // (width // query_count)
    chosen = query_of == lax.broadcasted_iota(jnp.int32, (query_count, width), 0)
    scores = contract_last(chosen.astype(jnp.float32), sums, precision=lax.Precision.HIGHEST)
    columns = out_ref.shape[1]
    for place in range(out_ref.shape[0] // query_count):
        out_ref[pl.ds(place * query_count, query_count), :] = scores[
            :, place * columns : (place + 1) * columns
        ]


def call(kernel, out_shape, *operands, **options):
    return pl.pallas_call(
        kernel,
        out_shape=out_shape,
        compiler_params=pltpu.CompilerParams(vmem_limit_bytes=VMEM_LIMIT),
        cost_estimate=pl.CostEstimate(flops=1, bytes_accessed=1, transcendentals=0),
        **options,
    )(*operands)


def precondition(in_rows, eig_rows, out_query):
    row_count = in_rows.shape[0]
    basis_width = out_query.shape[0]
    query_count = out_query.shape[1] // R
    outer_sum = jnp.einsum(
        "jqr,iqr->qji",
        in_rows.reshape(row_count, query_count, R),
        out_query.reshape(basis_width, query_count, R),
        preferred_element_type=jnp.float32,
    )
    inverse = 1.0 / (eig_rows.astype(jnp.float32) + damping)
    return (outer_sum * inverse[None, :, :]).astype(jnp.bfloat16)


def plain_scores(acts, basis_in, pack, out_query, grad_proj, onehot):
    pack = lax.all_gather(pack, "blk", axis=0, tiled=True)
    piece = lax.all_gather(basis_in, "blk", axis=0, tiled=True)
    pairs = out_query.shape[1]
    weighted = precondition(pack[:, :pairs], pack[:, pairs:], out_query)
    projected = contract_last(acts, piece)
    per_token = jnp.stack(
        [jnp.sum(projected * contract_last(grad_proj, slab), axis=1) for slab in weighted]
    )
    return contract_last(per_token, onehot, precision=lax.Precision.HIGHEST)


def stepped_scores(
    acts, out_grads, basis_in, basis_out, eigvals, query_out, query_in, onehot
):
    rows, width = basis_in.shape[0], basis_out.shape[0]
    tokens, seq_count = acts.shape[0], onehot.shape[0]
    query_count = query_in.shape[1] // R
    pair = [(0, 1), (1, 0)]
    place = lax.axis_index("blk")
    inner = (place == 1) | (place == 2)

    def along(value):
        return lax.ppermute(value, "blk", [(i, i ^ 1) for i in range(4)])

    def swapped(value):
        return lax.ppermute(value, "groups", pair)

    def across(value, at_ends):
        return lax.ppermute(
            value,
            AXES,
            pairing(lambda g, b, e, r: (g, 3 - b, e, r) if b in (1, 2) else at_ends(g, b, e, r)),
        )

    chunks = take_chunks(basis_in)
    half, other_half = chunks[:2], chunks[2:]
    to_core = lambda g, b, e, r: (g, b, e, 1 - r)
    over_y = lambda g, b, e, r: (1 - g, b, e, r)
    mine_1, middle_3 = [], []
    for chunk in half:
        middle_3.append(across(chunk, to_core))
        mine_1.append(along(chunk))

    split = rows + width
    keep, send = small_parts(held(basis_in, *half), query_in, basis_out, query_out, out_grads)
    other = lax.ppermute(send, "rep", pair)
    keep = keep + held(other, mine_1[0], middle_3[0])
    other = lax.ppermute(keep, "eig", pair)

    arrived = []
    for first, middle, rest in zip(mine_1, middle_3, other_half):
        from_pair = along(jnp.where(inner, middle, held(rest, first, keep)))
        from_across = across(held(first, middle, keep), over_y)
        arrived.append((from_pair, from_across))

    small = (keep + held(other, *arrived[0])).astype(jnp.bfloat16)
    ready = [chunk for both in arrived for chunk in both] + [small]
    mine_2 = jnp.concatenate(
        [jnp.where(inner, held(there, *ready), here) for here, there in arrived], axis=1
    )
    theirs_1 = [
        jnp.where(inner, held(here, mine_2), held(there, mine_2)) for here, there in arrived
    ]
    theirs_2 = swapped(mine_2)
    mine_3 = along(mine_2)

    in_query, out_query, grad_half = small[:rows], small[rows:split], small[split:]
    packs = by_distance(jnp.concatenate([in_query, eigvals], axis=1))
    grad_other = lax.ppermute(grad_half, "rep", pair)
    of_first = lax.axis_index("rep") == 0
    grad_proj = jnp.concatenate(
        [
            jnp.where(of_first, grad_half, grad_other),
            jnp.where(of_first, grad_other, grad_half),
        ],
        axis=0,
    )
    total_shape = jax.ShapeDtypeStruct((tokens, LANES), jnp.float32)
    first_total, acts = call(
        first_kernel,
        [total_shape, pltpu.VMEM(acts.shape, acts.dtype)],
        in_hbm(held(acts, grad_half)), *half, *other_half, *mine_1, *theirs_1,
        in_specs=[pl.BlockSpec(memory_space=pl.ANY)]
        + [pl.BlockSpec(memory_space=pltpu.VMEM)] * 8,
        scratch_shapes=[pltpu.SemaphoreType.DMA((tokens // BLOCK, 8))],
    )
    acts = in_vmem(acts)

    cut = mine_3.shape[1] // 2
    left_3 = along(held(theirs_2, first_total, *packs[1:])[:, :cut])
    right_3 = swapped(held(mine_3, first_total, *packs[1:])[:, cut:])
    mixed_width = 2 * query_count * rows
    weights = call(
        functools.partial(weight_kernel, query_count),
        jax.ShapeDtypeStruct((2, mixed_width, width), jnp.bfloat16),
        *packs, out_query,
    )
    total, mixed, sums = call(
        mine_kernel,
        [
            total_shape,
            jax.ShapeDtypeStruct((tokens, mixed_width), jnp.float32),
            jax.ShapeDtypeStruct((seq_count, mixed_width), jnp.float32),
        ],
        acts, mine_2, mine_3, first_total, weights, grad_proj, onehot,
    )
    places = lax.axis_size("blk")
    return call(
        functools.partial(last_kernel, query_count),
        jax.ShapeDtypeStruct((places * query_count, seq_count // places), jnp.float32),
        acts, theirs_2, left_3, right_3, total, mixed, onehot, sums,
    )


def plain_path(acts, out_grads, basis_in, basis_out, eigvals, query_out, query_in, onehot):
    def whole_sum(part):
        return swap_sum(swap_sum(part, "rep"), "eig").astype(jnp.bfloat16)

    in_query = whole_sum(jnp.dot(basis_in, query_in, preferred_element_type=jnp.float32))
    out_query = whole_sum(jnp.dot(basis_out, query_out, preferred_element_type=jnp.float32))
    grad_proj = whole_sum(contract_last(out_grads, basis_out))
    pack = jnp.concatenate([in_query, eigvals], axis=1)
    scores = plain_scores(acts, basis_in, pack, out_query, grad_proj, onehot.astype(jnp.float32))
    queries, columns = scores.shape
    places = lax.axis_size("blk")
    parts = scores.reshape(queries, places, columns // places)
    return parts.transpose(1, 0, 2).reshape(places * queries, columns // places)


def on_device(acts, out_grads, basis_in, basis_out, eigvals, query_out, query_in, seq_ids, owner):
    rows, features = basis_in.shape
    pairs = query_in.shape[1]
    seq_count = owner.shape[0]
    labels = jnp.arange(seq_count, dtype=jnp.int32)
    column_of = jnp.sum(jnp.where(seq_ids[None, :] == labels[:, None], owner[:, None], 0), axis=0)
    onehot = (labels[:, None] == column_of[None, :]).astype(jnp.bfloat16)
    stepped = (
        all(lax.axis_size(axis) == size for axis, size in zip(AXES, (2, 4, 2, 2)))
        and 2 * rows == LANES
        and (rows + basis_out.shape[0]) % 16 == acts.shape[0] % 32 == 0
        and features % (4 * LANES) == 0
        and acts.shape[0] % BLOCK == 0
        and pairs == basis_out.shape[0] == LANES
    )
    way = stepped_scores if stepped else plain_path
    parts = way(acts, out_grads, basis_in, basis_out, eigvals, query_out, query_in, onehot)
    own_queries = pairs // R // lax.axis_size(("eig", "rep"))
    own_columns = seq_count // lax.axis_size("blk")
    parts = lax.all_to_all(parts, ("blk", "eig", "rep"), 0, 0, tiled=True)
    return jnp.sum(parts.reshape(-1, own_queries, own_columns), axis=0)


def solution(mesh):
    return jax.shard_map(
        on_device,
        mesh=mesh,
        in_specs=(
            P(("groups", "blk"), ("eig", "rep")),
            P(("groups", "blk"), ("eig", "rep")),
            P("blk", ("eig", "rep")),
            P(None, ("eig", "rep")),
            P("blk", None),
            P(("eig", "rep"), "groups"),
            P(("eig", "rep"), "groups"),
            P(("groups", "blk")),
            P("groups"),
        ),
        out_specs=P(("groups", "eig", "rep"), "blk"),
        check_vma=False,
    )
```

```python
import functools
import itertools

import jax
import jax.numpy as jnp
from jax import lax
from jax.experimental import pallas as pl
from jax.experimental.pallas import tpu as pltpu
from jax.sharding import PartitionSpec as P

R = 32
LANES = 128
BLOCK = 256
VMEM_LIMIT = 16 * 1024 * 1024
AXES = ("groups", "blk", "eig", "rep")


damping = 0.05


def contract_last(left_side, right_side, precision=None):
    return lax.dot_general(
        left_side,
        right_side,
        (((1,), (1,)), ((), ())),
        precision=precision,
        preferred_element_type=jnp.float32,
    )


def swap_sum(value, axis):
    size = lax.axis_size(axis)
    if size & (size - 1):
        return lax.psum(value, axis)
    step = 1
    while step < size:
        pairs = [(i, i ^ step) for i in range(size)]
        value = value + lax.ppermute(value, axis, pairs)
        step *= 2
    return value


def by_distance(value, axis="blk"):
    size = lax.axis_size(axis)
    return [value] + [
        lax.ppermute(value, axis, [(i, i ^ k) for i in range(size)]) for k in range(1, size)
    ]


def held(value, *until):
    return lax.optimization_barrier((value, *until))[0]


def in_hbm(value):
    return pltpu.with_memory_space_constraint(value, pltpu.HBM)


def in_vmem(value):
    return pltpu.with_memory_space_constraint(value, pltpu.VMEM)


def pairing(partner):
    sizes = [lax.axis_size(axis) for axis in AXES]
    places = list(itertools.product(*map(range, sizes)))
    return [(number, places.index(partner(*place))) for number, place in enumerate(places)]


def chunks_kernel(whole_ref, *refs):
    chunk_refs, copied = refs[:4], refs[4]
    columns = chunk_refs[0].shape[1]
    group = lax.axis_index("groups")
    copies = []
    for place, chunk_ref in enumerate(chunk_refs):
        half = group if place < 2 else 1 - group
        begin = pl.multiple_of((2 * half + place % 2) * columns, LANES)
        source = whole_ref.at[:, pl.ds(begin, columns)]
        copies.append(pltpu.make_async_copy(source, chunk_ref, copied.at[place]))
    for copy in copies:
        copy.start()
    for copy in copies:
        copy.wait()


def take_chunks(whole):
    rows, columns = whole.shape
    return pl.pallas_call(
        chunks_kernel,
        in_specs=[pl.BlockSpec(memory_space=pl.ANY)],
        out_shape=[pltpu.VMEM((rows, columns // 4), whole.dtype)] * 4,
        scratch_shapes=[pltpu.SemaphoreType.DMA((4,))],
    )(in_hbm(whole))


def cut_copies(source, target, copied, parts):
    size = source.shape[0] // parts
    places = [pl.ds(part * size, size) for part in range(parts)]
    return [
        pltpu.make_async_copy(source.at[place], target.at[place], copied.at[part])
        for part, place in enumerate(places)
    ]


def parts_kernel(*refs):
    sources, keep_ref, send_ref, copied = refs[:5], refs[5], refs[6], refs[-1]
    held_refs = out_ref, out_query_ref, in_ref, in_query_ref, grads_ref = refs[7:-2]
    sum_ref = refs[-2]
    copies = [
        cut_copies(source, target, copied.at[place], parts)
        for place, (source, target, parts) in enumerate(zip(sources, held_refs, (1, 1, 2, 4, 4)))
    ]
    for group in copies:
        for copy in group:
            copy.start()

    def wait(*places):
        for place in places:
            for copy in copies[place]:
                copy.wait()

    rows, width = in_ref.shape[0], out_ref.shape[0]
    wait(0, 1)
    sum_ref[rows : rows + width] = jnp.dot(
        out_ref[...], out_query_ref[...], preferred_element_type=jnp.float32
    )
    wait(2, 3)
    sum_ref[:rows] = jnp.dot(in_ref[...], in_query_ref[...], preferred_element_type=jnp.float32)
    blocks_copied = copies[4]
    size = grads_ref.shape[0] // len(blocks_copied)

    @pl.loop(0, len(blocks_copied))
    def _(step):
        start = pl.multiple_of(step * size, 16)
        place = pl.ds(start, size)
        pltpu.make_async_copy(
            sources[4].at[place], grads_ref.at[place], copied.at[4, step]
        ).wait()
        sum_ref[pl.ds(rows + width + start, size), :] = contract_last(
            grads_ref[place, :], out_ref[...]
        )

    core, split = lax.axis_index("rep"), rows + width
    half = grads_ref.shape[0] // 2
    for part_ref, whose in ((keep_ref, core), (send_ref, 1 - core)):
        part_ref[:split] = sum_ref[:split]
        start = pl.multiple_of(split + whose * half, 8)
        part_ref[split:] = sum_ref[pl.ds(start, half), :]


def small_parts(basis_in, query_in, basis_out, query_out, out_grads):
    split, tokens, pairs = basis_in.shape[0] + basis_out.shape[0], out_grads.shape[0], query_in.shape[1]
    high = split + tokens
    sources = (basis_out, query_out, basis_in, query_in, out_grads)
    half = jax.ShapeDtypeStruct((split + tokens // 2, pairs), jnp.float32)
    return pl.pallas_call(
        parts_kernel,
        in_specs=[pl.BlockSpec(memory_space=pl.ANY)] * len(sources),
        out_shape=[half, half],
        scratch_shapes=[pltpu.VMEM(source.shape, source.dtype) for source in sources]
        + [pltpu.VMEM((high, pairs), jnp.float32), pltpu.SemaphoreType.DMA((len(sources), 8))],
        compiler_params=pltpu.CompilerParams(vmem_limit_bytes=VMEM_LIMIT),
    )(*[in_hbm(source) for source in sources])


def weigh(query_count, packs, out_query, weights_ref):
    rows, pairs = packs[0].shape[0], out_query.shape[1]
    query_of = lax.broadcasted_iota(jnp.int32, (rows, pairs), 1) // R
    for slot, pack_ref in enumerate(packs):
        in_query = pack_ref[:, :pairs].astype(jnp.float32)
        inverse = 1.0 / (pack_ref[:, pairs:].astype(jnp.float32) + damping)
        for query in range(query_count):
            own = jnp.where(query_of == query, in_query, 0.0).astype(jnp.bfloat16)
            outer_sum = contract_last(own, out_query)
            weights_ref[slot // 2, pl.ds((2 * query + slot % 2) * rows, rows), :] = (
                outer_sum * inverse
            ).astype(jnp.bfloat16)


def project(acts_ref, start, pieces, group, first=0):
    columns = pl.ds(
        pl.multiple_of(group * (acts_ref.shape[1] // 2) + first, LANES), pieces[0].shape[1]
    )
    stacked = jnp.concatenate([piece[...] for piece in pieces], axis=0)
    return contract_last(acts_ref[pl.ds(start, BLOCK), columns], stacked)


def mixing(start, weights, grad_ref):
    return contract_last(grad_ref[pl.ds(start, BLOCK), :], weights)


def mix(start, projected, mixed, onehot_ref):
    product = jnp.concatenate([projected] * (mixed.shape[1] // LANES), axis=1) * mixed
    high = product.astype(jnp.bfloat16)
    low = (product - high.astype(jnp.float32)).astype(jnp.bfloat16)
    onehot = onehot_ref[:, pl.ds(start, BLOCK)]
    return jnp.dot(onehot, high, preferred_element_type=jnp.float32) + jnp.dot(
        onehot, low, preferred_element_type=jnp.float32
    )


def blocks(tokens, body, initial):
    def step(index, carry):
        return body(pl.multiple_of(index * BLOCK, LANES), carry)

    return lax.fori_loop(0, tokens // BLOCK, step, initial, unroll=True)


def weight_kernel(query_count, *refs):
    packs, (out_query_ref, weights_ref) = refs[:4], refs[4:]
    weigh(query_count, packs, out_query_ref[...], weights_ref)


def load_kernel(source_ref, acts_ref, copied):
    copies = cut_copies(source_ref, acts_ref, copied, copied.shape[0])
    for copy in copies:
        copy.start()
    for copy in copies:
        copy.wait()


def first_kernel(acts_ref, *refs):
    slots, total_ref = refs[:8], refs[8]
    columns = slots[0].shape[1]
    group = lax.axis_index("groups")

    def body(start, carry):
        total = 0.0
        for place in range(4):
            half = group if place < 2 else 1 - group
            total = total + project(
                acts_ref, start, (slots[place], slots[4 + place]), half, place % 2 * columns
            )
        total_ref[pl.ds(start, BLOCK), :] = total
        return carry

    blocks(acts_ref.shape[0], body, 0)


def mine_kernel(
    acts_ref, mine_2_ref, mine_3_ref, first_ref, weights_ref, grad_ref, onehot_ref,
    total_ref, mixed_ref, sums_ref,
):
    group = lax.axis_index("groups")

    def body(start, sums):
        rows = pl.ds(start, BLOCK)
        total_ref[rows, :] = project(acts_ref, start, (mine_2_ref, mine_3_ref), group)
        mixed_ref[rows, :] = mixing(start, weights_ref[1], grad_ref)
        mixed = mixing(start, weights_ref[0], grad_ref)
        return sums + mix(start, first_ref[rows, :], mixed, onehot_ref)

    sums_ref[...] = blocks(acts_ref.shape[0], body, jnp.zeros(sums_ref.shape, jnp.float32))


def last_kernel(
    query_count, acts_ref, theirs_2_ref, left_ref, right_ref, total_ref, mixed_ref, onehot_ref,
    before_ref, out_ref,
):
    other = 1 - lax.axis_index("groups")
    cut = left_ref.shape[1]

    def body(start, sums):
        total = total_ref[pl.ds(start, BLOCK), :]
        total = total + project(
            acts_ref, start, (theirs_2_ref.at[:, :cut], left_ref), other
        )
        total = total + project(
            acts_ref, start, (theirs_2_ref.at[:, cut:], right_ref), other, cut
        )
        return sums + mix(start, total, mixed_ref[pl.ds(start, BLOCK), :], onehot_ref)

    sums = blocks(acts_ref.shape[0], body, before_ref[...])
    width = sums.shape[1]
    query_of = lax.broadcasted_iota(jnp.int32, (query_count, width), 1) // (width // query_count)
    chosen = query_of == lax.broadcasted_iota(jnp.int32, (query_count, width), 0)
    scores = contract_last(chosen.astype(jnp.float32), sums, precision=lax.Precision.HIGHEST)
    columns = out_ref.shape[1]
    for place in range(out_ref.shape[0] // query_count):
        out_ref[pl.ds(place * query_count, query_count), :] = scores[
            :, place * columns : (place + 1) * columns
        ]


def call(kernel, out_shape, *operands, **options):
    return pl.pallas_call(
        kernel,
        out_shape=out_shape,
        compiler_params=pltpu.CompilerParams(vmem_limit_bytes=VMEM_LIMIT),
        cost_estimate=pl.CostEstimate(flops=1, bytes_accessed=1, transcendentals=0),
        **options,
    )(*operands)


def precondition(in_rows, eig_rows, out_query):
    row_count = in_rows.shape[0]
    basis_width = out_query.shape[0]
    query_count = out_query.shape[1] // R
    outer_sum = jnp.einsum(
        "jqr,iqr->qji",
        in_rows.reshape(row_count, query_count, R),
        out_query.reshape(basis_width, query_count, R),
        preferred_element_type=jnp.float32,
    )
    inverse = 1.0 / (eig_rows.astype(jnp.float32) + damping)
    return (outer_sum * inverse[None, :, :]).astype(jnp.bfloat16)


def plain_scores(acts, basis_in, pack, out_query, grad_proj, onehot):
    pack = lax.all_gather(pack, "blk", axis=0, tiled=True)
    piece = lax.all_gather(basis_in, "blk", axis=0, tiled=True)
    pairs = out_query.shape[1]
    weighted = precondition(pack[:, :pairs], pack[:, pairs:], out_query)
    projected = contract_last(acts, piece)
    per_token = jnp.stack(
        [jnp.sum(projected * contract_last(grad_proj, slab), axis=1) for slab in weighted]
    )
    return contract_last(per_token, onehot, precision=lax.Precision.HIGHEST)


def stepped_scores(
    acts, out_grads, basis_in, basis_out, eigvals, query_out, query_in, onehot
):
    rows, width = basis_in.shape[0], basis_out.shape[0]
    tokens, seq_count = acts.shape[0], onehot.shape[0]
    query_count = query_in.shape[1] // R
    pair = [(0, 1), (1, 0)]
    place = lax.axis_index("blk")
    inner = (place == 1) | (place == 2)

    def along(value):
        return lax.ppermute(value, "blk", [(i, i ^ 1) for i in range(4)])

    def swapped(value):
        return lax.ppermute(value, "groups", pair)

    def across(value, at_ends):
        return lax.ppermute(
            value,
            AXES,
            pairing(lambda g, b, e, r: (g, 3 - b, e, r) if b in (1, 2) else at_ends(g, b, e, r)),
        )

    chunks = take_chunks(basis_in)
    half, other_half = chunks[:2], chunks[2:]
    to_core = lambda g, b, e, r: (g, b, e, 1 - r)
    over_y = lambda g, b, e, r: (1 - g, b, e, r)
    mine_1, middle_3 = [], []
    for chunk in half:
        middle_3.append(across(chunk, to_core))
        mine_1.append(along(chunk))

    split = rows + width
    keep, send = small_parts(held(basis_in, *half), query_in, basis_out, query_out, out_grads)
    other = lax.ppermute(send, "rep", pair)
    keep = keep + held(other, *mine_1, *middle_3)
    other = lax.ppermute(keep, "eig", pair)

    arrived = []
    for after, first, middle, rest in zip((half[0], keep), mine_1, middle_3, other_half):
        from_pair = along(jnp.where(inner, middle, held(rest, first, after)))
        from_across = across(held(first, middle, after), over_y)
        arrived.append((from_pair, from_across))

    acts = call(
        load_kernel,
        pltpu.VMEM(acts.shape, acts.dtype),
        in_hbm(held(acts, keep)),
        in_specs=[pl.BlockSpec(memory_space=pl.ANY)],
        scratch_shapes=[pltpu.SemaphoreType.DMA((8,))],
    )
    acts = in_vmem(acts)
    ready = [chunk for both in arrived for chunk in both] + [acts]
    mine_2 = jnp.concatenate(
        [jnp.where(inner, held(there, *ready), here) for here, there in arrived], axis=1
    )
    theirs_1 = [
        jnp.where(inner, held(here, mine_2), held(there, mine_2)) for here, there in arrived
    ]
    theirs_2 = swapped(mine_2)
    mine_3 = along(mine_2)

    small = (keep + held(other, mine_2)).astype(jnp.bfloat16)
    in_query, out_query, grad_half = small[:rows], small[rows:split], small[split:]
    packs = by_distance(jnp.concatenate([in_query, eigvals], axis=1))
    grad_other = lax.ppermute(grad_half, "rep", pair)
    of_first = lax.axis_index("rep") == 0
    grad_proj = jnp.concatenate(
        [
            jnp.where(of_first, grad_half, grad_other),
            jnp.where(of_first, grad_other, grad_half),
        ],
        axis=0,
    )
    total_shape = jax.ShapeDtypeStruct((tokens, LANES), jnp.float32)
    first_total = call(
        first_kernel, total_shape, acts, *half, *other_half, *mine_1, *theirs_1
    )

    cut = mine_3.shape[1] // 2
    left_3 = along(held(theirs_2, first_total, *packs[1:])[:, :cut])
    right_3 = swapped(held(mine_3, first_total, *packs[1:])[:, cut:])
    mixed_width = 2 * query_count * rows
    weights = call(
        functools.partial(weight_kernel, query_count),
        jax.ShapeDtypeStruct((2, mixed_width, width), jnp.bfloat16),
        *packs, out_query,
    )
    total, mixed, sums = call(
        mine_kernel,
        [
            total_shape,
            jax.ShapeDtypeStruct((tokens, mixed_width), jnp.float32),
            jax.ShapeDtypeStruct((seq_count, mixed_width), jnp.float32),
        ],
        acts, mine_2, mine_3, first_total, weights, grad_proj, onehot,
    )
    places = lax.axis_size("blk")
    return call(
        functools.partial(last_kernel, query_count),
        jax.ShapeDtypeStruct((places * query_count, seq_count // places), jnp.float32),
        acts, theirs_2, left_3, right_3, total, mixed, onehot, sums,
    )


def plain_path(acts, out_grads, basis_in, basis_out, eigvals, query_out, query_in, onehot):
    def whole_sum(part):
        return swap_sum(swap_sum(part, "rep"), "eig").astype(jnp.bfloat16)

    in_query = whole_sum(jnp.dot(basis_in, query_in, preferred_element_type=jnp.float32))
    out_query = whole_sum(jnp.dot(basis_out, query_out, preferred_element_type=jnp.float32))
    grad_proj = whole_sum(contract_last(out_grads, basis_out))
    pack = jnp.concatenate([in_query, eigvals], axis=1)
    scores = plain_scores(acts, basis_in, pack, out_query, grad_proj, onehot.astype(jnp.float32))
    queries, columns = scores.shape
    places = lax.axis_size("blk")
    parts = scores.reshape(queries, places, columns // places)
    return parts.transpose(1, 0, 2).reshape(places * queries, columns // places)


def on_device(acts, out_grads, basis_in, basis_out, eigvals, query_out, query_in, seq_ids, owner):
    rows, features = basis_in.shape
    pairs = query_in.shape[1]
    seq_count = owner.shape[0]
    labels = jnp.arange(seq_count, dtype=jnp.int32)
    column_of = jnp.sum(jnp.where(seq_ids[None, :] == labels[:, None], owner[:, None], 0), axis=0)
    onehot = (labels[:, None] == column_of[None, :]).astype(jnp.bfloat16)
    stepped = (
        all(lax.axis_size(axis) == size for axis, size in zip(AXES, (2, 4, 2, 2)))
        and 2 * rows == LANES
        and (rows + basis_out.shape[0]) % 16 == acts.shape[0] % 32 == 0
        and features % (4 * LANES) == 0
        and acts.shape[0] % BLOCK == 0
        and pairs == basis_out.shape[0] == LANES
    )
    way = stepped_scores if stepped else plain_path
    parts = way(acts, out_grads, basis_in, basis_out, eigvals, query_out, query_in, onehot)
    own_queries = pairs // R // lax.axis_size(("eig", "rep"))
    own_columns = seq_count // lax.axis_size("blk")
    parts = lax.all_to_all(parts, ("blk", "eig", "rep"), 0, 0, tiled=True)
    return jnp.sum(parts.reshape(-1, own_queries, own_columns), axis=0)


def solution(mesh):
    return jax.shard_map(
        on_device,
        mesh=mesh,
        in_specs=(
            P(("groups", "blk"), ("eig", "rep")),
            P(("groups", "blk"), ("eig", "rep")),
            P("blk", ("eig", "rep")),
            P(None, ("eig", "rep")),
            P("blk", None),
            P(("eig", "rep"), "groups"),
            P(("eig", "rep"), "groups"),
            P(("groups", "blk")),
            P("groups"),
        ),
        out_specs=P(("groups", "eig", "rep"), "blk"),
        check_vma=False,
    )
```

```python
import functools
import itertools

import jax
import jax.numpy as jnp
from jax import lax
from jax.experimental import pallas as pl
from jax.experimental.pallas import tpu as pltpu
from jax.sharding import PartitionSpec as P

R = 32
LANES = 128
BLOCK = 256
VMEM_LIMIT = 16 * 1024 * 1024
AXES = ("groups", "blk", "eig", "rep")


damping = 0.05


def contract_last(left_side, right_side, precision=None):
    return lax.dot_general(
        left_side,
        right_side,
        (((1,), (1,)), ((), ())),
        precision=precision,
        preferred_element_type=jnp.float32,
    )


def swap_sum(value, axis):
    size = lax.axis_size(axis)
    if size & (size - 1):
        return lax.psum(value, axis)
    step = 1
    while step < size:
        pairs = [(i, i ^ step) for i in range(size)]
        value = value + lax.ppermute(value, axis, pairs)
        step *= 2
    return value


def by_distance(value, axis="blk"):
    size = lax.axis_size(axis)
    return [value] + [
        lax.ppermute(value, axis, [(i, i ^ k) for i in range(size)]) for k in range(1, size)
    ]


def held(value, *until):
    return lax.optimization_barrier((value, *until))[0]


def in_hbm(value):
    return pltpu.with_memory_space_constraint(value, pltpu.HBM)


def in_vmem(value):
    return pltpu.with_memory_space_constraint(value, pltpu.VMEM)


def pairing(partner):
    sizes = [lax.axis_size(axis) for axis in AXES]
    places = list(itertools.product(*map(range, sizes)))
    return [(number, places.index(partner(*place))) for number, place in enumerate(places)]


def chunks_kernel(whole_ref, *refs):
    chunk_refs, copied = refs[:4], refs[4]
    columns = chunk_refs[0].shape[1]
    group = lax.axis_index("groups")
    copies = []
    for place, chunk_ref in enumerate(chunk_refs):
        half = group if place < 2 else 1 - group
        begin = pl.multiple_of((2 * half + place % 2) * columns, LANES)
        source = whole_ref.at[:, pl.ds(begin, columns)]
        copies.append(pltpu.make_async_copy(source, chunk_ref, copied.at[place]))
    for copy in copies:
        copy.start()
    for copy in copies:
        copy.wait()


def take_chunks(whole):
    rows, columns = whole.shape
    return pl.pallas_call(
        chunks_kernel,
        in_specs=[pl.BlockSpec(memory_space=pl.ANY)],
        out_shape=[pltpu.VMEM((rows, columns // 4), whole.dtype)] * 4,
        scratch_shapes=[pltpu.SemaphoreType.DMA((4,))],
    )(in_hbm(whole))


def cut_copies(source, target, copied, parts):
    size = source.shape[0] // parts
    places = [pl.ds(part * size, size) for part in range(parts)]
    return [
        pltpu.make_async_copy(source.at[place], target.at[place], copied.at[part])
        for part, place in enumerate(places)
    ]


def parts_kernel(*refs):
    sources, keep_ref, send_ref, copied = refs[:5], refs[5], refs[6], refs[-1]
    held_refs = out_ref, out_query_ref, in_ref, in_query_ref, grads_ref = refs[7:-2]
    sum_ref = refs[-2]
    copies = [
        cut_copies(source, target, copied.at[place], parts)
        for place, (source, target, parts) in enumerate(zip(sources, held_refs, (1, 1, 2, 4, 4)))
    ]
    for group in copies:
        for copy in group:
            copy.start()

    def wait(*places):
        for place in places:
            for copy in copies[place]:
                copy.wait()

    rows, width = in_ref.shape[0], out_ref.shape[0]
    wait(0, 1)
    sum_ref[rows : rows + width] = jnp.dot(
        out_ref[...], out_query_ref[...], preferred_element_type=jnp.float32
    )
    wait(2, 3)
    sum_ref[:rows] = jnp.dot(in_ref[...], in_query_ref[...], preferred_element_type=jnp.float32)
    blocks_copied = copies[4]
    size = grads_ref.shape[0] // len(blocks_copied)

    @pl.loop(0, len(blocks_copied))
    def _(step):
        start = pl.multiple_of(step * size, 16)
        place = pl.ds(start, size)
        pltpu.make_async_copy(
            sources[4].at[place], grads_ref.at[place], copied.at[4, step]
        ).wait()
        sum_ref[pl.ds(rows + width + start, size), :] = contract_last(
            grads_ref[place, :], out_ref[...]
        )

    core, split = lax.axis_index("rep"), rows + width
    half = grads_ref.shape[0] // 2
    for part_ref, whose in ((keep_ref, core), (send_ref, 1 - core)):
        part_ref[:split] = sum_ref[:split]
        start = pl.multiple_of(split + whose * half, 8)
        part_ref[split:] = sum_ref[pl.ds(start, half), :]


def small_parts(basis_in, query_in, basis_out, query_out, out_grads):
    split, tokens, pairs = basis_in.shape[0] + basis_out.shape[0], out_grads.shape[0], query_in.shape[1]
    high = split + tokens
    sources = (basis_out, query_out, basis_in, query_in, out_grads)
    half = jax.ShapeDtypeStruct((split + tokens // 2, pairs), jnp.float32)
    return pl.pallas_call(
        parts_kernel,
        in_specs=[pl.BlockSpec(memory_space=pl.ANY)] * len(sources),
        out_shape=[half, half],
        scratch_shapes=[pltpu.VMEM(source.shape, source.dtype) for source in sources]
        + [pltpu.VMEM((high, pairs), jnp.float32), pltpu.SemaphoreType.DMA((len(sources), 8))],
        compiler_params=pltpu.CompilerParams(vmem_limit_bytes=VMEM_LIMIT),
    )(*[in_hbm(source) for source in sources])


def weigh(query_count, packs, out_query, weights_ref):
    rows, pairs = packs[0].shape[0], out_query.shape[1]
    query_of = lax.broadcasted_iota(jnp.int32, (rows, pairs), 1) // R
    for slot, pack_ref in enumerate(packs):
        in_query = pack_ref[:, :pairs].astype(jnp.float32)
        inverse = 1.0 / (pack_ref[:, pairs:].astype(jnp.float32) + damping)
        for query in range(query_count):
            own = jnp.where(query_of == query, in_query, 0.0).astype(jnp.bfloat16)
            outer_sum = contract_last(own, out_query)
            weights_ref[slot // 2, pl.ds((2 * query + slot % 2) * rows, rows), :] = (
                outer_sum * inverse
            ).astype(jnp.bfloat16)


def project(acts_ref, start, pieces, group, first=0):
    columns = pl.ds(
        pl.multiple_of(group * (acts_ref.shape[1] // 2) + first, LANES), pieces[0].shape[1]
    )
    stacked = jnp.concatenate([piece[...] for piece in pieces], axis=0)
    return contract_last(acts_ref[pl.ds(start, BLOCK), columns], stacked)


def mixing(start, weights, grad_ref):
    return contract_last(grad_ref[pl.ds(start, BLOCK), :], weights)


def mix(start, projected, mixed, onehot_ref):
    product = jnp.concatenate([projected] * (mixed.shape[1] // LANES), axis=1) * mixed
    high = product.astype(jnp.bfloat16)
    low = (product - high.astype(jnp.float32)).astype(jnp.bfloat16)
    onehot = onehot_ref[:, pl.ds(start, BLOCK)]
    return jnp.dot(onehot, high, preferred_element_type=jnp.float32) + jnp.dot(
        onehot, low, preferred_element_type=jnp.float32
    )


def blocks(tokens, body, initial):
    def step(index, carry):
        return body(pl.multiple_of(index * BLOCK, LANES), carry)

    return lax.fori_loop(0, tokens // BLOCK, step, initial, unroll=True)


def weight_kernel(query_count, *refs):
    packs, (out_query_ref, weights_ref) = refs[:4], refs[4:]
    weigh(query_count, packs, out_query_ref[...], weights_ref)


def load_kernel(source_ref, acts_ref, copied):
    copies = cut_copies(source_ref, acts_ref, copied, copied.shape[0])
    for copy in copies:
        copy.start()
    for copy in copies:
        copy.wait()


def first_kernel(acts_ref, *refs):
    slots, total_ref = refs[:8], refs[8]
    columns = slots[0].shape[1]
    group = lax.axis_index("groups")

    def body(start, carry):
        total = 0.0
        for place in range(4):
            half = group if place < 2 else 1 - group
            total = total + project(
                acts_ref, start, (slots[place], slots[4 + place]), half, place % 2 * columns
            )
        total_ref[pl.ds(start, BLOCK), :] = total
        return carry

    blocks(acts_ref.shape[0], body, 0)


def mine_kernel(
    acts_ref, mine_2_ref, mine_3_ref, first_ref, weights_ref, grad_ref, onehot_ref,
    total_ref, mixed_ref, sums_ref,
):
    group = lax.axis_index("groups")

    def body(start, sums):
        rows = pl.ds(start, BLOCK)
        total_ref[rows, :] = project(acts_ref, start, (mine_2_ref, mine_3_ref), group)
        mixed_ref[rows, :] = mixing(start, weights_ref[1], grad_ref)
        mixed = mixing(start, weights_ref[0], grad_ref)
        return sums + mix(start, first_ref[rows, :], mixed, onehot_ref)

    sums_ref[...] = blocks(acts_ref.shape[0], body, jnp.zeros(sums_ref.shape, jnp.float32))


def last_kernel(
    query_count, acts_ref, theirs_2_ref, left_ref, right_ref, total_ref, mixed_ref, onehot_ref,
    before_ref, out_ref,
):
    other = 1 - lax.axis_index("groups")
    cut = left_ref.shape[1]

    def body(start, sums):
        total = total_ref[pl.ds(start, BLOCK), :]
        total = total + project(
            acts_ref, start, (theirs_2_ref.at[:, :cut], left_ref), other
        )
        total = total + project(
            acts_ref, start, (theirs_2_ref.at[:, cut:], right_ref), other, cut
        )
        return sums + mix(start, total, mixed_ref[pl.ds(start, BLOCK), :], onehot_ref)

    sums = blocks(acts_ref.shape[0], body, before_ref[...])
    width = sums.shape[1]
    query_of = lax.broadcasted_iota(jnp.int32, (query_count, width), 1) // (width // query_count)
    chosen = query_of == lax.broadcasted_iota(jnp.int32, (query_count, width), 0)
    scores = contract_last(chosen.astype(jnp.float32), sums, precision=lax.Precision.HIGHEST)
    columns = out_ref.shape[1]
    for place in range(out_ref.shape[0] // query_count):
        out_ref[pl.ds(place * query_count, query_count), :] = scores[
            :, place * columns : (place + 1) * columns
        ]


def call(kernel, out_shape, *operands, **options):
    return pl.pallas_call(
        kernel,
        out_shape=out_shape,
        compiler_params=pltpu.CompilerParams(vmem_limit_bytes=VMEM_LIMIT),
        cost_estimate=pl.CostEstimate(flops=1, bytes_accessed=1, transcendentals=0),
        **options,
    )(*operands)


def precondition(in_rows, eig_rows, out_query):
    row_count = in_rows.shape[0]
    basis_width = out_query.shape[0]
    query_count = out_query.shape[1] // R
    outer_sum = jnp.einsum(
        "jqr,iqr->qji",
        in_rows.reshape(row_count, query_count, R),
        out_query.reshape(basis_width, query_count, R),
        preferred_element_type=jnp.float32,
    )
    inverse = 1.0 / (eig_rows.astype(jnp.float32) + damping)
    return (outer_sum * inverse[None, :, :]).astype(jnp.bfloat16)


def plain_scores(acts, basis_in, pack, out_query, grad_proj, onehot):
    pack = lax.all_gather(pack, "blk", axis=0, tiled=True)
    piece = lax.all_gather(basis_in, "blk", axis=0, tiled=True)
    pairs = out_query.shape[1]
    weighted = precondition(pack[:, :pairs], pack[:, pairs:], out_query)
    projected = contract_last(acts, piece)
    per_token = jnp.stack(
        [jnp.sum(projected * contract_last(grad_proj, slab), axis=1) for slab in weighted]
    )
    return contract_last(per_token, onehot, precision=lax.Precision.HIGHEST)


def stepped_scores(
    acts, out_grads, basis_in, basis_out, eigvals, query_out, query_in, onehot
):
    rows, width = basis_in.shape[0], basis_out.shape[0]
    tokens, seq_count = acts.shape[0], onehot.shape[0]
    query_count = query_in.shape[1] // R
    pair = [(0, 1), (1, 0)]
    place = lax.axis_index("blk")
    inner = (place == 1) | (place == 2)
    of_first = lax.axis_index("rep") == 0

    def along(value):
        return lax.ppermute(value, "blk", [(i, i ^ 1) for i in range(4)])

    def swapped(value):
        return lax.ppermute(value, "groups", pair)

    def across(value, at_ends):
        return lax.ppermute(
            value,
            AXES,
            pairing(lambda g, b, e, r: (g, 3 - b, e, r) if b in (1, 2) else at_ends(g, b, e, r)),
        )

    chunks = take_chunks(basis_in)
    half, other_half = chunks[:2], chunks[2:]
    to_core = lambda g, b, e, r: (g, b, e, 1 - r)
    over_y = lambda g, b, e, r: (1 - g, b, e, r)
    mine_1, middle_3 = [], []
    for chunk in half:
        middle_3.append(across(chunk, to_core))
        mine_1.append(along(chunk))

    split = rows + width
    early, inner, of_first, _ = lax.optimization_barrier((basis_in, inner, of_first, half))
    keep, send = small_parts(early, query_in, basis_out, query_out, out_grads)
    other = lax.ppermute(send, "rep", pair)
    keep = keep + held(other, *mine_1, *middle_3)
    other = lax.ppermute(keep, "eig", pair)

    arrived = []
    for after, first, middle, rest in zip((half[0], keep), mine_1, middle_3, other_half):
        from_pair = along(jnp.where(inner, middle, held(rest, first, after)))
        from_across = across(held(first, middle, after), over_y)
        arrived.append((from_pair, from_across))

    acts = call(
        load_kernel,
        pltpu.VMEM(acts.shape, acts.dtype),
        in_hbm(held(acts, keep)),
        in_specs=[pl.BlockSpec(memory_space=pl.ANY)],
        scratch_shapes=[pltpu.SemaphoreType.DMA((8,))],
    )
    acts = in_vmem(acts)
    ready = [chunk for both in arrived for chunk in both] + [acts]
    mine_2 = jnp.concatenate(
        [jnp.where(inner, held(there, *ready), here) for here, there in arrived], axis=1
    )
    theirs_1 = [
        jnp.where(inner, held(here, mine_2), held(there, mine_2)) for here, there in arrived
    ]
    theirs_2 = swapped(mine_2)
    mine_3 = along(mine_2)

    small = (keep + held(other, mine_2)).astype(jnp.bfloat16)
    in_query, out_query, grad_half = small[:rows], small[rows:split], small[split:]
    packs = by_distance(jnp.concatenate([in_query, eigvals], axis=1))
    grad_other = lax.ppermute(grad_half, "rep", pair)
    grad_proj = jnp.concatenate(
        [
            jnp.where(of_first, grad_half, grad_other),
            jnp.where(of_first, grad_other, grad_half),
        ],
        axis=0,
    )
    total_shape = jax.ShapeDtypeStruct((tokens, LANES), jnp.float32)
    first_total = call(
        first_kernel, total_shape, acts, *half, *other_half, *mine_1, *theirs_1
    )

    cut = mine_3.shape[1] // 2
    left_3 = along(held(theirs_2, first_total, *packs[1:])[:, :cut])
    right_3 = swapped(held(mine_3, first_total, *packs[1:])[:, cut:])
    mixed_width = 2 * query_count * rows
    weights = call(
        functools.partial(weight_kernel, query_count),
        jax.ShapeDtypeStruct((2, mixed_width, width), jnp.bfloat16),
        *packs, out_query,
    )
    total, mixed, sums = call(
        mine_kernel,
        [
            total_shape,
            jax.ShapeDtypeStruct((tokens, mixed_width), jnp.float32),
            jax.ShapeDtypeStruct((seq_count, mixed_width), jnp.float32),
        ],
        acts, mine_2, mine_3, first_total, weights, grad_proj, onehot,
    )
    places = lax.axis_size("blk")
    return call(
        functools.partial(last_kernel, query_count),
        jax.ShapeDtypeStruct((places * query_count, seq_count // places), jnp.float32),
        acts, theirs_2, left_3, right_3, total, mixed, onehot, sums,
    )


def plain_path(acts, out_grads, basis_in, basis_out, eigvals, query_out, query_in, onehot):
    def whole_sum(part):
        return swap_sum(swap_sum(part, "rep"), "eig").astype(jnp.bfloat16)

    in_query = whole_sum(jnp.dot(basis_in, query_in, preferred_element_type=jnp.float32))
    out_query = whole_sum(jnp.dot(basis_out, query_out, preferred_element_type=jnp.float32))
    grad_proj = whole_sum(contract_last(out_grads, basis_out))
    pack = jnp.concatenate([in_query, eigvals], axis=1)
    scores = plain_scores(acts, basis_in, pack, out_query, grad_proj, onehot.astype(jnp.float32))
    queries, columns = scores.shape
    places = lax.axis_size("blk")
    parts = scores.reshape(queries, places, columns // places)
    return parts.transpose(1, 0, 2).reshape(places * queries, columns // places)


def on_device(acts, out_grads, basis_in, basis_out, eigvals, query_out, query_in, seq_ids, owner):
    rows, features = basis_in.shape
    pairs = query_in.shape[1]
    seq_count = owner.shape[0]
    labels = jnp.arange(seq_count, dtype=jnp.int32)
    column_of = jnp.sum(jnp.where(seq_ids[None, :] == labels[:, None], owner[:, None], 0), axis=0)
    onehot = (labels[:, None] == column_of[None, :]).astype(jnp.bfloat16)
    stepped = (
        all(lax.axis_size(axis) == size for axis, size in zip(AXES, (2, 4, 2, 2)))
        and 2 * rows == LANES
        and (rows + basis_out.shape[0]) % 16 == acts.shape[0] % 32 == 0
        and features % (4 * LANES) == 0
        and acts.shape[0] % BLOCK == 0
        and pairs == basis_out.shape[0] == LANES
    )
    way = stepped_scores if stepped else plain_path
    parts = way(acts, out_grads, basis_in, basis_out, eigvals, query_out, query_in, onehot)
    own_queries = pairs // R // lax.axis_size(("eig", "rep"))
    own_columns = seq_count // lax.axis_size("blk")
    parts = lax.all_to_all(parts, ("blk", "eig", "rep"), 0, 0, tiled=True)
    return jnp.sum(parts.reshape(-1, own_queries, own_columns), axis=0)


def solution(mesh):
    return jax.shard_map(
        on_device,
        mesh=mesh,
        in_specs=(
            P(("groups", "blk"), ("eig", "rep")),
            P(("groups", "blk"), ("eig", "rep")),
            P("blk", ("eig", "rep")),
            P(None, ("eig", "rep")),
            P("blk", None),
            P(("eig", "rep"), "groups"),
            P(("eig", "rep"), "groups"),
            P(("groups", "blk")),
            P("groups"),
        ),
        out_specs=P(("groups", "eig", "rep"), "blk"),
        check_vma=False,
    )
```

```python
import functools
import itertools

import jax
import jax.numpy as jnp
from jax import lax
from jax.experimental import pallas as pl
from jax.experimental.pallas import tpu as pltpu
from jax.sharding import PartitionSpec as P

R = 32
LANES = 128
BLOCK = 384
VMEM_LIMIT = 16 * 1024 * 1024
AXES = ("groups", "blk", "eig", "rep")


damping = 0.05


def contract_last(left_side, right_side, precision=None):
    return lax.dot_general(
        left_side,
        right_side,
        (((1,), (1,)), ((), ())),
        precision=precision,
        preferred_element_type=jnp.float32,
    )


def swap_sum(value, axis):
    size = lax.axis_size(axis)
    if size & (size - 1):
        return lax.psum(value, axis)
    step = 1
    while step < size:
        pairs = [(i, i ^ step) for i in range(size)]
        value = value + lax.ppermute(value, axis, pairs)
        step *= 2
    return value


def by_distance(value, axis="blk"):
    size = lax.axis_size(axis)
    return [value] + [
        lax.ppermute(value, axis, [(i, i ^ k) for i in range(size)]) for k in range(1, size)
    ]


def held(value, *until):
    return lax.optimization_barrier((value, *until))[0]


def in_hbm(value):
    return pltpu.with_memory_space_constraint(value, pltpu.HBM)


def in_vmem(value):
    return pltpu.with_memory_space_constraint(value, pltpu.VMEM)


def pairing(partner):
    sizes = [lax.axis_size(axis) for axis in AXES]
    places = list(itertools.product(*map(range, sizes)))
    return [(number, places.index(partner(*place))) for number, place in enumerate(places)]


def chunks_kernel(whole_ref, *refs):
    chunk_refs, copied = refs[:4], refs[4]
    columns = chunk_refs[0].shape[1]
    group = lax.axis_index("groups")
    copies = []
    for place, chunk_ref in enumerate(chunk_refs):
        half = group if place < 2 else 1 - group
        begin = pl.multiple_of((2 * half + place % 2) * columns, LANES)
        source = whole_ref.at[:, pl.ds(begin, columns)]
        copies.append(pltpu.make_async_copy(source, chunk_ref, copied.at[place]))
    for copy in copies:
        copy.start()
    for copy in copies:
        copy.wait()


def take_chunks(whole):
    rows, columns = whole.shape
    return pl.pallas_call(
        chunks_kernel,
        in_specs=[pl.BlockSpec(memory_space=pl.ANY)],
        out_shape=[pltpu.VMEM((rows, columns // 4), whole.dtype)] * 4,
        scratch_shapes=[pltpu.SemaphoreType.DMA((4,))],
    )(in_hbm(whole))


def cut_copies(source, target, copied, parts):
    size = source.shape[0] // parts
    places = [pl.ds(part * size, size) for part in range(parts)]
    return [
        pltpu.make_async_copy(source.at[place], target.at[place], copied.at[part])
        for part, place in enumerate(places)
    ]


def parts_kernel(*refs):
    sources, keep_ref, send_ref, copied = refs[:5], refs[5], refs[6], refs[-1]
    held_refs = out_ref, out_query_ref, in_ref, in_query_ref, grads_ref = refs[7:-2]
    sum_ref = refs[-2]
    copies = [
        cut_copies(source, target, copied.at[place], parts)
        for place, (source, target, parts) in enumerate(zip(sources, held_refs, (1, 1, 2, 4, 4)))
    ]
    for group in copies:
        for copy in group:
            copy.start()

    def wait(*places):
        for place in places:
            for copy in copies[place]:
                copy.wait()

    rows, width = in_ref.shape[0], out_ref.shape[0]
    wait(0, 1)
    sum_ref[rows : rows + width] = jnp.dot(
        out_ref[...], out_query_ref[...], preferred_element_type=jnp.float32
    )
    wait(2, 3)
    sum_ref[:rows] = jnp.dot(in_ref[...], in_query_ref[...], preferred_element_type=jnp.float32)
    blocks_copied = copies[4]
    size = grads_ref.shape[0] // len(blocks_copied)

    @pl.loop(0, len(blocks_copied))
    def _(step):
        start = pl.multiple_of(step * size, 16)
        place = pl.ds(start, size)
        pltpu.make_async_copy(
            sources[4].at[place], grads_ref.at[place], copied.at[4, step]
        ).wait()
        sum_ref[pl.ds(rows + width + start, size), :] = contract_last(
            grads_ref[place, :], out_ref[...]
        )

    core, split = lax.axis_index("rep"), rows + width
    half = grads_ref.shape[0] // 2
    for part_ref, whose in ((keep_ref, core), (send_ref, 1 - core)):
        part_ref[:split] = sum_ref[:split]
        start = pl.multiple_of(split + whose * half, 8)
        part_ref[split:] = sum_ref[pl.ds(start, half), :]


def small_parts(basis_in, query_in, basis_out, query_out, out_grads):
    split, tokens, pairs = basis_in.shape[0] + basis_out.shape[0], out_grads.shape[0], query_in.shape[1]
    high = split + tokens
    sources = (basis_out, query_out, basis_in, query_in, out_grads)
    half = jax.ShapeDtypeStruct((split + tokens // 2, pairs), jnp.float32)
    return pl.pallas_call(
        parts_kernel,
        in_specs=[pl.BlockSpec(memory_space=pl.ANY)] * len(sources),
        out_shape=[half, half],
        scratch_shapes=[pltpu.VMEM(source.shape, source.dtype) for source in sources]
        + [pltpu.VMEM((high, pairs), jnp.float32), pltpu.SemaphoreType.DMA((len(sources), 8))],
        compiler_params=pltpu.CompilerParams(vmem_limit_bytes=VMEM_LIMIT),
    )(*[in_hbm(source) for source in sources])


def weigh(query_count, packs, out_query, weights_ref):
    rows, pairs = packs[0].shape[0], out_query.shape[1]
    query_of = lax.broadcasted_iota(jnp.int32, (rows, pairs), 1) // R
    for slot, pack_ref in enumerate(packs):
        in_query = pack_ref[:, :pairs].astype(jnp.float32)
        inverse = 1.0 / (pack_ref[:, pairs:].astype(jnp.float32) + damping)
        for query in range(query_count):
            own = jnp.where(query_of == query, in_query, 0.0).astype(jnp.bfloat16)
            outer_sum = contract_last(own, out_query)
            weights_ref[slot // 2, pl.ds((2 * query + slot % 2) * rows, rows), :] = (
                outer_sum * inverse
            ).astype(jnp.bfloat16)


def project(acts_ref, start, pieces, group, first=0):
    columns = pl.ds(
        pl.multiple_of(group * (acts_ref.shape[1] // 2) + first, LANES), pieces[0].shape[1]
    )
    stacked = jnp.concatenate([piece[...] for piece in pieces], axis=0)
    return contract_last(acts_ref[pl.ds(start, BLOCK), columns], stacked)


def mixing(start, weights, grad_ref):
    return contract_last(grad_ref[pl.ds(start, BLOCK), :], weights)


def mix(start, projected, mixed, onehot_ref):
    product = jnp.concatenate([projected] * (mixed.shape[1] // LANES), axis=1) * mixed
    high = product.astype(jnp.bfloat16)
    low = (product - high.astype(jnp.float32)).astype(jnp.bfloat16)
    onehot = onehot_ref[:, pl.ds(start, BLOCK)]
    return jnp.dot(onehot, high, preferred_element_type=jnp.float32) + jnp.dot(
        onehot, low, preferred_element_type=jnp.float32
    )


def blocks(tokens, body, initial):
    def step(index, carry):
        return body(pl.multiple_of(index * BLOCK, LANES), carry)

    return lax.fori_loop(0, tokens // BLOCK, step, initial, unroll=True)


def weight_kernel(query_count, *refs):
    packs, (out_query_ref, weights_ref) = refs[:4], refs[4:]
    weigh(query_count, packs, out_query_ref[...], weights_ref)


def first_kernel(source_ref, *refs):
    slots, (total_ref, acts_ref, copied) = refs[:8], refs[8:]
    columns = slots[0].shape[1]
    group = lax.axis_index("groups")
    steps = acts_ref.shape[0] // BLOCK
    parts = 8

    def copies(step):
        size = BLOCK // parts
        begin = pl.multiple_of(step * BLOCK, BLOCK)
        places = [pl.ds(begin + part * size, size) for part in range(parts)]
        return [
            pltpu.make_async_copy(source_ref.at[place], acts_ref.at[place], copied.at[step, part])
            for part, place in enumerate(places)
        ]

    for copy in copies(0):
        copy.start()

    @pl.loop(0, steps)
    def _(step):
        for copy in copies(step):
            copy.wait()

        @pl.when(step + 1 < steps)
        def _():
            for copy in copies(step + 1):
                copy.start()

        start = pl.multiple_of(step * BLOCK, LANES)
        total = 0.0
        for place in range(4):
            half = group if place < 2 else 1 - group
            total = total + project(
                acts_ref, start, (slots[place], slots[4 + place]), half, place % 2 * columns
            )
        total_ref[pl.ds(start, BLOCK), :] = total


def mine_kernel(
    acts_ref, mine_2_ref, mine_3_ref, first_ref, weights_ref, grad_ref, onehot_ref,
    total_ref, mixed_ref, sums_ref,
):
    group = lax.axis_index("groups")

    def body(start, sums):
        rows = pl.ds(start, BLOCK)
        total_ref[rows, :] = project(acts_ref, start, (mine_2_ref, mine_3_ref), group)
        mixed_ref[rows, :] = mixing(start, weights_ref[1], grad_ref)
        mixed = mixing(start, weights_ref[0], grad_ref)
        return sums + mix(start, first_ref[rows, :], mixed, onehot_ref)

    sums_ref[...] = blocks(acts_ref.shape[0], body, jnp.zeros(sums_ref.shape, jnp.float32))


def last_kernel(
    query_count, acts_ref, theirs_2_ref, left_ref, right_ref, total_ref, mixed_ref, onehot_ref,
    before_ref, out_ref,
):
    other = 1 - lax.axis_index("groups")
    cut = left_ref.shape[1]

    def body(start, sums):
        total = total_ref[pl.ds(start, BLOCK), :]
        total = total + project(
            acts_ref, start, (theirs_2_ref.at[:, :cut], left_ref), other
        )
        total = total + project(
            acts_ref, start, (theirs_2_ref.at[:, cut:], right_ref), other, cut
        )
        return sums + mix(start, total, mixed_ref[pl.ds(start, BLOCK), :], onehot_ref)

    sums = blocks(acts_ref.shape[0], body, before_ref[...])
    width = sums.shape[1]
    query_of = lax.broadcasted_iota(jnp.int32, (query_count, width), 1) // (width // query_count)
    chosen = query_of == lax.broadcasted_iota(jnp.int32, (query_count, width), 0)
    scores = contract_last(chosen.astype(jnp.float32), sums, precision=lax.Precision.HIGHEST)
    columns = out_ref.shape[1]
    for place in range(out_ref.shape[0] // query_count):
        out_ref[pl.ds(place * query_count, query_count), :] = scores[
            :, place * columns : (place + 1) * columns
        ]


def call(kernel, out_shape, *operands, **options):
    return pl.pallas_call(
        kernel,
        out_shape=out_shape,
        compiler_params=pltpu.CompilerParams(vmem_limit_bytes=VMEM_LIMIT),
        cost_estimate=pl.CostEstimate(flops=1, bytes_accessed=1, transcendentals=0),
        **options,
    )(*operands)


def precondition(in_rows, eig_rows, out_query):
    row_count = in_rows.shape[0]
    basis_width = out_query.shape[0]
    query_count = out_query.shape[1] // R
    outer_sum = jnp.einsum(
        "jqr,iqr->qji",
        in_rows.reshape(row_count, query_count, R),
        out_query.reshape(basis_width, query_count, R),
        preferred_element_type=jnp.float32,
    )
    inverse = 1.0 / (eig_rows.astype(jnp.float32) + damping)
    return (outer_sum * inverse[None, :, :]).astype(jnp.bfloat16)


def plain_scores(acts, basis_in, pack, out_query, grad_proj, onehot):
    pack = lax.all_gather(pack, "blk", axis=0, tiled=True)
    piece = lax.all_gather(basis_in, "blk", axis=0, tiled=True)
    pairs = out_query.shape[1]
    weighted = precondition(pack[:, :pairs], pack[:, pairs:], out_query)
    projected = contract_last(acts, piece)
    per_token = jnp.stack(
        [jnp.sum(projected * contract_last(grad_proj, slab), axis=1) for slab in weighted]
    )
    return contract_last(per_token, onehot, precision=lax.Precision.HIGHEST)


def stepped_scores(
    acts, out_grads, basis_in, basis_out, eigvals, query_out, query_in, onehot
):
    rows, width = basis_in.shape[0], basis_out.shape[0]
    tokens, seq_count = acts.shape[0], onehot.shape[0]
    query_count = query_in.shape[1] // R
    pair = [(0, 1), (1, 0)]
    place = lax.axis_index("blk")
    inner = (place == 1) | (place == 2)

    def along(value):
        return lax.ppermute(value, "blk", [(i, i ^ 1) for i in range(4)])

    def swapped(value):
        return lax.ppermute(value, "groups", pair)

    def across(value, at_ends):
        return lax.ppermute(
            value,
            AXES,
            pairing(lambda g, b, e, r: (g, 3 - b, e, r) if b in (1, 2) else at_ends(g, b, e, r)),
        )

    chunks = take_chunks(basis_in)
    half, other_half = chunks[:2], chunks[2:]
    to_core = lambda g, b, e, r: (g, b, e, 1 - r)
    over_y = lambda g, b, e, r: (1 - g, b, e, r)
    mine_1, middle_3 = [], []
    for chunk in half:
        middle_3.append(across(chunk, to_core))
        mine_1.append(along(chunk))

    split = rows + width
    keep, send = small_parts(held(basis_in, *half), query_in, basis_out, query_out, out_grads)
    other = lax.ppermute(send, "rep", pair)
    keep = keep + held(other, mine_1[0], middle_3[0])
    other = lax.ppermute(keep, "eig", pair)

    arrived = []
    for first, middle, rest in zip(mine_1, middle_3, other_half):
        from_pair = along(jnp.where(inner, middle, held(rest, first, keep)))
        from_across = across(held(first, middle, keep), over_y)
        arrived.append((from_pair, from_across))

    small = (keep + held(other, *arrived[0])).astype(jnp.bfloat16)
    ready = [chunk for both in arrived for chunk in both] + [small]
    mine_2 = jnp.concatenate(
        [jnp.where(inner, held(there, *ready), here) for here, there in arrived], axis=1
    )
    theirs_1 = [
        jnp.where(inner, held(here, mine_2), held(there, mine_2)) for here, there in arrived
    ]
    theirs_2 = swapped(mine_2)
    mine_3 = along(mine_2)

    in_query, out_query, grad_half = small[:rows], small[rows:split], small[split:]
    packs = by_distance(jnp.concatenate([in_query, eigvals], axis=1))
    grad_other = lax.ppermute(grad_half, "rep", pair)
    of_first = lax.axis_index("rep") == 0
    grad_proj = jnp.concatenate(
        [
            jnp.where(of_first, grad_half, grad_other),
            jnp.where(of_first, grad_other, grad_half),
        ],
        axis=0,
    )
    total_shape = jax.ShapeDtypeStruct((tokens, LANES), jnp.float32)
    first_total, acts = call(
        first_kernel,
        [total_shape, pltpu.VMEM(acts.shape, acts.dtype)],
        in_hbm(held(acts, grad_half)), *half, *other_half, *mine_1, *theirs_1,
        in_specs=[pl.BlockSpec(memory_space=pl.ANY)]
        + [pl.BlockSpec(memory_space=pltpu.VMEM)] * 8,
        scratch_shapes=[pltpu.SemaphoreType.DMA((tokens // BLOCK, 8))],
    )
    acts = in_vmem(acts)

    cut = mine_3.shape[1] // 2
    left_3 = along(held(theirs_2, first_total, *packs[1:])[:, :cut])
    right_3 = swapped(held(mine_3, first_total, *packs[1:])[:, cut:])
    mixed_width = 2 * query_count * rows
    weights = call(
        functools.partial(weight_kernel, query_count),
        jax.ShapeDtypeStruct((2, mixed_width, width), jnp.bfloat16),
        *packs, out_query,
    )
    total, mixed, sums = call(
        mine_kernel,
        [
            total_shape,
            jax.ShapeDtypeStruct((tokens, mixed_width), jnp.float32),
            jax.ShapeDtypeStruct((seq_count, mixed_width), jnp.float32),
        ],
        acts, mine_2, mine_3, first_total, weights, grad_proj, onehot,
    )
    places = lax.axis_size("blk")
    return call(
        functools.partial(last_kernel, query_count),
        jax.ShapeDtypeStruct((places * query_count, seq_count // places), jnp.float32),
        acts, theirs_2, left_3, right_3, total, mixed, onehot, sums,
    )


def plain_path(acts, out_grads, basis_in, basis_out, eigvals, query_out, query_in, onehot):
    def whole_sum(part):
        return swap_sum(swap_sum(part, "rep"), "eig").astype(jnp.bfloat16)

    in_query = whole_sum(jnp.dot(basis_in, query_in, preferred_element_type=jnp.float32))
    out_query = whole_sum(jnp.dot(basis_out, query_out, preferred_element_type=jnp.float32))
    grad_proj = whole_sum(contract_last(out_grads, basis_out))
    pack = jnp.concatenate([in_query, eigvals], axis=1)
    scores = plain_scores(acts, basis_in, pack, out_query, grad_proj, onehot.astype(jnp.float32))
    queries, columns = scores.shape
    places = lax.axis_size("blk")
    parts = scores.reshape(queries, places, columns // places)
    return parts.transpose(1, 0, 2).reshape(places * queries, columns // places)


def on_device(acts, out_grads, basis_in, basis_out, eigvals, query_out, query_in, seq_ids, owner):
    rows, features = basis_in.shape
    pairs = query_in.shape[1]
    seq_count = owner.shape[0]
    labels = jnp.arange(seq_count, dtype=jnp.int32)
    column_of = jnp.sum(jnp.where(seq_ids[None, :] == labels[:, None], owner[:, None], 0), axis=0)
    onehot = (labels[:, None] == column_of[None, :]).astype(jnp.bfloat16)
    stepped = (
        all(lax.axis_size(axis) == size for axis, size in zip(AXES, (2, 4, 2, 2)))
        and 2 * rows == LANES
        and (rows + basis_out.shape[0]) % 16 == acts.shape[0] % 32 == 0
        and features % (4 * LANES) == 0
        and acts.shape[0] % BLOCK == 0
        and pairs == basis_out.shape[0] == LANES
    )
    way = stepped_scores if stepped else plain_path
    parts = way(acts, out_grads, basis_in, basis_out, eigvals, query_out, query_in, onehot)
    own_queries = pairs // R // lax.axis_size(("eig", "rep"))
    own_columns = seq_count // lax.axis_size("blk")
    parts = lax.all_to_all(parts, ("blk", "eig", "rep"), 0, 0, tiled=True)
    return jnp.sum(parts.reshape(-1, own_queries, own_columns), axis=0)


def solution(mesh):
    return jax.shard_map(
        on_device,
        mesh=mesh,
        in_specs=(
            P(("groups", "blk"), ("eig", "rep")),
            P(("groups", "blk"), ("eig", "rep")),
            P("blk", ("eig", "rep")),
            P(None, ("eig", "rep")),
            P("blk", None),
            P(("eig", "rep"), "groups"),
            P(("eig", "rep"), "groups"),
            P(("groups", "blk")),
            P("groups"),
        ),
        out_specs=P(("groups", "eig", "rep"), "blk"),
        check_vma=False,
    )
```

```python
import functools
import itertools

import jax
import jax.numpy as jnp
from jax import lax
from jax.experimental import pallas as pl
from jax.experimental.pallas import tpu as pltpu
from jax.sharding import PartitionSpec as P

R = 32
LANES = 128
BLOCK = 256
VMEM_LIMIT = 16 * 1024 * 1024
AXES = ("groups", "blk", "eig", "rep")


damping = 0.05


def contract_last(left_side, right_side, precision=None):
    return lax.dot_general(
        left_side,
        right_side,
        (((1,), (1,)), ((), ())),
        precision=precision,
        preferred_element_type=jnp.float32,
    )


def swap_sum(value, axis):
    size = lax.axis_size(axis)
    if size & (size - 1):
        return lax.psum(value, axis)
    step = 1
    while step < size:
        pairs = [(i, i ^ step) for i in range(size)]
        value = value + lax.ppermute(value, axis, pairs)
        step *= 2
    return value


def by_distance(value, axis="blk"):
    size = lax.axis_size(axis)
    return [value] + [
        lax.ppermute(value, axis, [(i, i ^ k) for i in range(size)]) for k in range(1, size)
    ]


def held(value, *until):
    return lax.optimization_barrier((value, *until))[0]


def in_hbm(value):
    return pltpu.with_memory_space_constraint(value, pltpu.HBM)


def in_vmem(value):
    return pltpu.with_memory_space_constraint(value, pltpu.VMEM)


def pairing(partner):
    sizes = [lax.axis_size(axis) for axis in AXES]
    places = list(itertools.product(*map(range, sizes)))
    return [(number, places.index(partner(*place))) for number, place in enumerate(places)]


def chunks_kernel(whole_ref, *refs):
    chunk_refs, copied = refs[:4], refs[4]
    columns = chunk_refs[0].shape[1]
    group = lax.axis_index("groups")
    copies = []
    for place, chunk_ref in enumerate(chunk_refs):
        half = group if place < 2 else 1 - group
        begin = pl.multiple_of((2 * half + place % 2) * columns, LANES)
        source = whole_ref.at[:, pl.ds(begin, columns)]
        copies.append(pltpu.make_async_copy(source, chunk_ref, copied.at[place]))
    for copy in copies:
        copy.start()
    for copy in copies:
        copy.wait()


def take_chunks(whole):
    rows, columns = whole.shape
    return pl.pallas_call(
        chunks_kernel,
        in_specs=[pl.BlockSpec(memory_space=pl.ANY)],
        out_shape=[pltpu.VMEM((rows, columns // 4), whole.dtype)] * 4,
        scratch_shapes=[pltpu.SemaphoreType.DMA((4,))],
    )(in_hbm(whole))


def cut_copies(source, target, copied, parts):
    size = source.shape[0] // parts
    places = [pl.ds(part * size, size) for part in range(parts)]
    return [
        pltpu.make_async_copy(source.at[place], target.at[place], copied.at[part])
        for part, place in enumerate(places)
    ]


def parts_kernel(*refs):
    sources, keep_ref, send_ref, copied = refs[:5], refs[5], refs[6], refs[-1]
    held_refs = out_ref, out_query_ref, in_ref, in_query_ref, grads_ref = refs[7:-2]
    sum_ref = refs[-2]
    copies = [
        cut_copies(source, target, copied.at[place], parts)
        for place, (source, target, parts) in enumerate(zip(sources, held_refs, (1, 1, 2, 4, 4)))
    ]
    for group in copies:
        for copy in group:
            copy.start()

    def wait(*places):
        for place in places:
            for copy in copies[place]:
                copy.wait()

    rows, width = in_ref.shape[0], out_ref.shape[0]
    wait(0, 1)
    sum_ref[rows : rows + width] = jnp.dot(
        out_ref[...], out_query_ref[...], preferred_element_type=jnp.float32
    )
    wait(2, 3)
    sum_ref[:rows] = jnp.dot(in_ref[...], in_query_ref[...], preferred_element_type=jnp.float32)
    blocks_copied = copies[4]
    size = grads_ref.shape[0] // len(blocks_copied)

    @pl.loop(0, len(blocks_copied))
    def _(step):
        start = pl.multiple_of(step * size, 16)
        place = pl.ds(start, size)
        pltpu.make_async_copy(
            sources[4].at[place], grads_ref.at[place], copied.at[4, step]
        ).wait()
        sum_ref[pl.ds(rows + width + start, size), :] = contract_last(
            grads_ref[place, :], out_ref[...]
        )

    core, split = lax.axis_index("rep"), rows + width
    half = grads_ref.shape[0] // 2
    for part_ref, whose in ((keep_ref, core), (send_ref, 1 - core)):
        part_ref[:split] = sum_ref[:split]
        start = pl.multiple_of(split + whose * half, 8)
        part_ref[split:] = sum_ref[pl.ds(start, half), :]


def small_parts(basis_in, query_in, basis_out, query_out, out_grads):
    split, tokens, pairs = basis_in.shape[0] + basis_out.shape[0], out_grads.shape[0], query_in.shape[1]
    high = split + tokens
    sources = (basis_out, query_out, basis_in, query_in, out_grads)
    half = jax.ShapeDtypeStruct((split + tokens // 2, pairs), jnp.float32)
    return pl.pallas_call(
        parts_kernel,
        in_specs=[pl.BlockSpec(memory_space=pl.ANY)] * len(sources),
        out_shape=[half, half],
        scratch_shapes=[pltpu.VMEM(source.shape, source.dtype) for source in sources]
        + [pltpu.VMEM((high, pairs), jnp.float32), pltpu.SemaphoreType.DMA((len(sources), 8))],
        compiler_params=pltpu.CompilerParams(vmem_limit_bytes=VMEM_LIMIT),
    )(*[in_hbm(source) for source in sources])


def weigh(query_count, packs, out_query, weights_ref):
    rows, pairs = packs[0].shape[0], out_query.shape[1]
    query_of = lax.broadcasted_iota(jnp.int32, (rows, pairs), 1) // R
    for slot, pack_ref in enumerate(packs):
        in_query = pack_ref[:, :pairs].astype(jnp.float32)
        inverse = 1.0 / (pack_ref[:, pairs:].astype(jnp.float32) + damping)
        for query in range(query_count):
            own = jnp.where(query_of == query, in_query, 0.0).astype(jnp.bfloat16)
            outer_sum = contract_last(own, out_query)
            weights_ref[slot // 2, pl.ds((2 * query + slot % 2) * rows, rows), :] = (
                outer_sum * inverse
            ).astype(jnp.bfloat16)


def project(acts_ref, start, pieces, group, first=0, size=BLOCK):
    columns = pl.ds(
        pl.multiple_of(group * (acts_ref.shape[1] // 2) + first, LANES), pieces[0].shape[1]
    )
    stacked = jnp.concatenate([piece[...] for piece in pieces], axis=0)
    return contract_last(acts_ref[pl.ds(start, size), columns], stacked)


def mixing(start, weights, grad_ref):
    return contract_last(grad_ref[pl.ds(start, BLOCK), :], weights)


def mix(start, projected, mixed, onehot_ref, size=BLOCK):
    product = jnp.concatenate([projected] * (mixed.shape[1] // LANES), axis=1) * mixed
    high = product.astype(jnp.bfloat16)
    low = (product - high.astype(jnp.float32)).astype(jnp.bfloat16)
    onehot = onehot_ref[:, pl.ds(start, size)]
    return jnp.dot(onehot, high, preferred_element_type=jnp.float32) + jnp.dot(
        onehot, low, preferred_element_type=jnp.float32
    )


def blocks(tokens, body, initial, size=BLOCK):
    def step(index, carry):
        return body(pl.multiple_of(index * size, LANES), carry)

    return lax.fori_loop(0, tokens // size, step, initial, unroll=True)


def weight_kernel(query_count, *refs):
    packs, (out_query_ref, weights_ref) = refs[:4], refs[4:]
    weigh(query_count, packs, out_query_ref[...], weights_ref)


def first_kernel(source_ref, *refs):
    slots, (total_ref, acts_ref, copied) = refs[:8], refs[8:]
    columns = slots[0].shape[1]
    group = lax.axis_index("groups")
    steps = acts_ref.shape[0] // BLOCK
    parts = 8

    def copies(step):
        size = BLOCK // parts
        begin = pl.multiple_of(step * BLOCK, BLOCK)
        places = [pl.ds(begin + part * size, size) for part in range(parts)]
        return [
            pltpu.make_async_copy(source_ref.at[place], acts_ref.at[place], copied.at[step, part])
            for part, place in enumerate(places)
        ]

    for copy in copies(0):
        copy.start()

    @pl.loop(0, steps)
    def _(step):
        for copy in copies(step):
            copy.wait()

        @pl.when(step + 1 < steps)
        def _():
            for copy in copies(step + 1):
                copy.start()

        start = pl.multiple_of(step * BLOCK, LANES)
        total = 0.0
        for place in range(4):
            half = group if place < 2 else 1 - group
            total = total + project(
                acts_ref, start, (slots[place], slots[4 + place]), half, place % 2 * columns
            )
        total_ref[pl.ds(start, BLOCK), :] = total


def mine_kernel(
    acts_ref, mine_2_ref, mine_3_ref, first_ref, weights_ref, grad_ref, onehot_ref,
    total_ref, mixed_ref, sums_ref,
):
    group = lax.axis_index("groups")

    def body(start, sums):
        rows = pl.ds(start, BLOCK)
        total_ref[rows, :] = project(acts_ref, start, (mine_2_ref, mine_3_ref), group)
        mixed_ref[rows, :] = mixing(start, weights_ref[1], grad_ref)
        mixed = mixing(start, weights_ref[0], grad_ref)
        return sums + mix(start, first_ref[rows, :], mixed, onehot_ref)

    sums_ref[...] = blocks(acts_ref.shape[0], body, jnp.zeros(sums_ref.shape, jnp.float32))


def last_kernel(
    query_count, acts_ref, theirs_2_ref, left_ref, right_ref, total_ref, mixed_ref, onehot_ref,
    before_ref, out_ref,
):
    other = 1 - lax.axis_index("groups")
    cut = left_ref.shape[1]

    size = LANES

    def body(start, sums):
        total = total_ref[pl.ds(start, size), :]
        total = total + project(
            acts_ref, start, (theirs_2_ref.at[:, :cut], left_ref), other, 0, size
        )
        total = total + project(
            acts_ref, start, (theirs_2_ref.at[:, cut:], right_ref), other, cut, size
        )
        return sums + mix(start, total, mixed_ref[pl.ds(start, size), :], onehot_ref, size)

    sums = blocks(acts_ref.shape[0], body, before_ref[...], size)
    width = sums.shape[1]
    query_of = lax.broadcasted_iota(jnp.int32, (query_count, width), 1) // (width // query_count)
    chosen = query_of == lax.broadcasted_iota(jnp.int32, (query_count, width), 0)
    scores = contract_last(chosen.astype(jnp.float32), sums, precision=lax.Precision.HIGHEST)
    columns = out_ref.shape[1]
    for place in range(out_ref.shape[0] // query_count):
        out_ref[pl.ds(place * query_count, query_count), :] = scores[
            :, place * columns : (place + 1) * columns
        ]


def call(kernel, out_shape, *operands, **options):
    return pl.pallas_call(
        kernel,
        out_shape=out_shape,
        compiler_params=pltpu.CompilerParams(vmem_limit_bytes=VMEM_LIMIT),
        cost_estimate=pl.CostEstimate(flops=1, bytes_accessed=1, transcendentals=0),
        **options,
    )(*operands)


def precondition(in_rows, eig_rows, out_query):
    row_count = in_rows.shape[0]
    basis_width = out_query.shape[0]
    query_count = out_query.shape[1] // R
    outer_sum = jnp.einsum(
        "jqr,iqr->qji",
        in_rows.reshape(row_count, query_count, R),
        out_query.reshape(basis_width, query_count, R),
        preferred_element_type=jnp.float32,
    )
    inverse = 1.0 / (eig_rows.astype(jnp.float32) + damping)
    return (outer_sum * inverse[None, :, :]).astype(jnp.bfloat16)


def plain_scores(acts, basis_in, pack, out_query, grad_proj, onehot):
    pack = lax.all_gather(pack, "blk", axis=0, tiled=True)
    piece = lax.all_gather(basis_in, "blk", axis=0, tiled=True)
    pairs = out_query.shape[1]
    weighted = precondition(pack[:, :pairs], pack[:, pairs:], out_query)
    projected = contract_last(acts, piece)
    per_token = jnp.stack(
        [jnp.sum(projected * contract_last(grad_proj, slab), axis=1) for slab in weighted]
    )
    return contract_last(per_token, onehot, precision=lax.Precision.HIGHEST)


def stepped_scores(
    acts, out_grads, basis_in, basis_out, eigvals, query_out, query_in, onehot
):
    rows, width = basis_in.shape[0], basis_out.shape[0]
    tokens, seq_count = acts.shape[0], onehot.shape[0]
    query_count = query_in.shape[1] // R
    pair = [(0, 1), (1, 0)]
    place = lax.axis_index("blk")
    inner = (place == 1) | (place == 2)

    def along(value):
        return lax.ppermute(value, "blk", [(i, i ^ 1) for i in range(4)])

    def swapped(value):
        return lax.ppermute(value, "groups", pair)

    def across(value, at_ends):
        return lax.ppermute(
            value,
            AXES,
            pairing(lambda g, b, e, r: (g, 3 - b, e, r) if b in (1, 2) else at_ends(g, b, e, r)),
        )

    chunks = take_chunks(basis_in)
    half, other_half = chunks[:2], chunks[2:]
    to_core = lambda g, b, e, r: (g, b, e, 1 - r)
    over_y = lambda g, b, e, r: (1 - g, b, e, r)
    mine_1, middle_3 = [], []
    for chunk in half:
        middle_3.append(across(chunk, to_core))
        mine_1.append(along(chunk))

    split = rows + width
    keep, send = small_parts(held(basis_in, *half), query_in, basis_out, query_out, out_grads)
    other = lax.ppermute(send, "rep", pair)
    keep = keep + held(other, mine_1[0], middle_3[0])
    other = lax.ppermute(keep, "eig", pair)

    arrived = []
    for first, middle, rest in zip(mine_1, middle_3, other_half):
        from_pair = along(jnp.where(inner, middle, held(rest, first, keep)))
        from_across = across(held(first, middle, keep), over_y)
        arrived.append((from_pair, from_across))

    small = (keep + held(other, *arrived[0])).astype(jnp.bfloat16)
    ready = [chunk for both in arrived for chunk in both] + [small]
    mine_2 = jnp.concatenate(
        [jnp.where(inner, held(there, *ready), here) for here, there in arrived], axis=1
    )
    theirs_1 = [
        jnp.where(inner, held(here, mine_2), held(there, mine_2)) for here, there in arrived
    ]
    theirs_2 = swapped(mine_2)
    mine_3 = along(mine_2)

    in_query, out_query, grad_half = small[:rows], small[rows:split], small[split:]
    packs = by_distance(jnp.concatenate([in_query, eigvals], axis=1))
    grad_other = lax.ppermute(grad_half, "rep", pair)
    of_first = lax.axis_index("rep") == 0
    grad_proj = jnp.concatenate(
        [
            jnp.where(of_first, grad_half, grad_other),
            jnp.where(of_first, grad_other, grad_half),
        ],
        axis=0,
    )
    total_shape = jax.ShapeDtypeStruct((tokens, LANES), jnp.float32)
    first_total, acts = call(
        first_kernel,
        [total_shape, pltpu.VMEM(acts.shape, acts.dtype)],
        in_hbm(held(acts, grad_half)), *half, *other_half, *mine_1, *theirs_1,
        in_specs=[pl.BlockSpec(memory_space=pl.ANY)]
        + [pl.BlockSpec(memory_space=pltpu.VMEM)] * 8,
        scratch_shapes=[pltpu.SemaphoreType.DMA((tokens // BLOCK, 8))],
    )
    acts = in_vmem(acts)

    cut = mine_3.shape[1] // 2
    left_3 = along(held(theirs_2, first_total, *packs[1:])[:, :cut])
    right_3 = swapped(held(mine_3, first_total, *packs[1:])[:, cut:])
    mixed_width = 2 * query_count * rows
    weights = call(
        functools.partial(weight_kernel, query_count),
        jax.ShapeDtypeStruct((2, mixed_width, width), jnp.bfloat16),
        *packs, out_query,
    )
    total, mixed, sums = call(
        mine_kernel,
        [
            total_shape,
            jax.ShapeDtypeStruct((tokens, mixed_width), jnp.float32),
            jax.ShapeDtypeStruct((seq_count, mixed_width), jnp.float32),
        ],
        acts, mine_2, mine_3, first_total, weights, grad_proj, onehot,
    )
    places = lax.axis_size("blk")
    return call(
        functools.partial(last_kernel, query_count),
        jax.ShapeDtypeStruct((places * query_count, seq_count // places), jnp.float32),
        acts, theirs_2, left_3, right_3, total, mixed, onehot, sums,
    )


def plain_path(acts, out_grads, basis_in, basis_out, eigvals, query_out, query_in, onehot):
    def whole_sum(part):
        return swap_sum(swap_sum(part, "rep"), "eig").astype(jnp.bfloat16)

    in_query = whole_sum(jnp.dot(basis_in, query_in, preferred_element_type=jnp.float32))
    out_query = whole_sum(jnp.dot(basis_out, query_out, preferred_element_type=jnp.float32))
    grad_proj = whole_sum(contract_last(out_grads, basis_out))
    pack = jnp.concatenate([in_query, eigvals], axis=1)
    scores = plain_scores(acts, basis_in, pack, out_query, grad_proj, onehot.astype(jnp.float32))
    queries, columns = scores.shape
    places = lax.axis_size("blk")
    parts = scores.reshape(queries, places, columns // places)
    return parts.transpose(1, 0, 2).reshape(places * queries, columns // places)


def on_device(acts, out_grads, basis_in, basis_out, eigvals, query_out, query_in, seq_ids, owner):
    rows, features = basis_in.shape
    pairs = query_in.shape[1]
    seq_count = owner.shape[0]
    labels = jnp.arange(seq_count, dtype=jnp.int32)
    column_of = jnp.sum(jnp.where(seq_ids[None, :] == labels[:, None], owner[:, None], 0), axis=0)
    onehot = (labels[:, None] == column_of[None, :]).astype(jnp.bfloat16)
    stepped = (
        all(lax.axis_size(axis) == size for axis, size in zip(AXES, (2, 4, 2, 2)))
        and 2 * rows == LANES
        and (rows + basis_out.shape[0]) % 16 == acts.shape[0] % 32 == 0
        and features % (4 * LANES) == 0
        and acts.shape[0] % BLOCK == 0
        and pairs == basis_out.shape[0] == LANES
    )
    way = stepped_scores if stepped else plain_path
    parts = way(acts, out_grads, basis_in, basis_out, eigvals, query_out, query_in, onehot)
    own_queries = pairs // R // lax.axis_size(("eig", "rep"))
    own_columns = seq_count // lax.axis_size("blk")
    parts = lax.all_to_all(parts, ("blk", "eig", "rep"), 0, 0, tiled=True)
    return jnp.sum(parts.reshape(-1, own_queries, own_columns), axis=0)


def solution(mesh):
    return jax.shard_map(
        on_device,
        mesh=mesh,
        in_specs=(
            P(("groups", "blk"), ("eig", "rep")),
            P(("groups", "blk"), ("eig", "rep")),
            P("blk", ("eig", "rep")),
            P(None, ("eig", "rep")),
            P("blk", None),
            P(("eig", "rep"), "groups"),
            P(("eig", "rep"), "groups"),
            P(("groups", "blk")),
            P("groups"),
        ),
        out_specs=P(("groups", "eig", "rep"), "blk"),
        check_vma=False,
    )
```

```python
import functools
import itertools

import jax
import jax.numpy as jnp
from jax import lax
from jax.experimental import pallas as pl
from jax.experimental.pallas import tpu as pltpu
from jax.sharding import PartitionSpec as P

R = 32
LANES = 128
BLOCK = 256
VMEM_LIMIT = 16 * 1024 * 1024
AXES = ("groups", "blk", "eig", "rep")


damping = 0.05


def contract_last(left_side, right_side, precision=None):
    return lax.dot_general(
        left_side,
        right_side,
        (((1,), (1,)), ((), ())),
        precision=precision,
        preferred_element_type=jnp.float32,
    )


def swap_sum(value, axis):
    size = lax.axis_size(axis)
    if size & (size - 1):
        return lax.psum(value, axis)
    step = 1
    while step < size:
        pairs = [(i, i ^ step) for i in range(size)]
        value = value + lax.ppermute(value, axis, pairs)
        step *= 2
    return value


def by_distance(value, axis="blk"):
    size = lax.axis_size(axis)
    return [value] + [
        lax.ppermute(value, axis, [(i, i ^ k) for i in range(size)]) for k in range(1, size)
    ]


def held(value, *until):
    return lax.optimization_barrier((value, *until))[0]


def in_hbm(value):
    return pltpu.with_memory_space_constraint(value, pltpu.HBM)


def in_vmem(value):
    return pltpu.with_memory_space_constraint(value, pltpu.VMEM)


def pairing(partner):
    sizes = [lax.axis_size(axis) for axis in AXES]
    places = list(itertools.product(*map(range, sizes)))
    return [(number, places.index(partner(*place))) for number, place in enumerate(places)]


def chunks_kernel(whole_ref, *refs):
    chunk_refs, copied = refs[:4], refs[4]
    columns = chunk_refs[0].shape[1]
    group = lax.axis_index("groups")
    copies = []
    for place, chunk_ref in enumerate(chunk_refs):
        half = group if place < 2 else 1 - group
        begin = pl.multiple_of((2 * half + place % 2) * columns, LANES)
        source = whole_ref.at[:, pl.ds(begin, columns)]
        copies.append(pltpu.make_async_copy(source, chunk_ref, copied.at[place]))
    for copy in copies:
        copy.start()
    for copy in copies:
        copy.wait()


def take_chunks(whole):
    rows, columns = whole.shape
    return pl.pallas_call(
        chunks_kernel,
        in_specs=[pl.BlockSpec(memory_space=pl.ANY)],
        out_shape=[pltpu.VMEM((rows, columns // 4), whole.dtype)] * 4,
        scratch_shapes=[pltpu.SemaphoreType.DMA((4,))],
    )(in_hbm(whole))


def cut_copies(source, target, copied, parts):
    size = source.shape[0] // parts
    places = [pl.ds(part * size, size) for part in range(parts)]
    return [
        pltpu.make_async_copy(source.at[place], target.at[place], copied.at[part])
        for part, place in enumerate(places)
    ]


def parts_kernel(*refs):
    sources, keep_ref, send_ref, copied = refs[:5], refs[5], refs[6], refs[-1]
    held_refs = out_ref, out_query_ref, in_ref, in_query_ref, grads_ref = refs[7:-2]
    sum_ref = refs[-2]
    copies = [
        cut_copies(source, target, copied.at[place], parts)
        for place, (source, target, parts) in enumerate(zip(sources, held_refs, (1, 1, 2, 4, 4)))
    ]
    for group in copies:
        for copy in group:
            copy.start()

    def wait(*places):
        for place in places:
            for copy in copies[place]:
                copy.wait()

    rows, width = in_ref.shape[0], out_ref.shape[0]
    wait(0, 1)
    sum_ref[rows : rows + width] = jnp.dot(
        out_ref[...], out_query_ref[...], preferred_element_type=jnp.float32
    )
    wait(2, 3)
    sum_ref[:rows] = jnp.dot(in_ref[...], in_query_ref[...], preferred_element_type=jnp.float32)
    blocks_copied = copies[4]
    size = grads_ref.shape[0] // len(blocks_copied)

    @pl.loop(0, len(blocks_copied))
    def _(step):
        start = pl.multiple_of(step * size, 16)
        place = pl.ds(start, size)
        pltpu.make_async_copy(
            sources[4].at[place], grads_ref.at[place], copied.at[4, step]
        ).wait()
        sum_ref[pl.ds(rows + width + start, size), :] = contract_last(
            grads_ref[place, :], out_ref[...]
        )

    core, split = lax.axis_index("rep"), rows + width
    half = grads_ref.shape[0] // 2
    for part_ref, whose in ((keep_ref, core), (send_ref, 1 - core)):
        part_ref[:split] = sum_ref[:split]
        start = pl.multiple_of(split + whose * half, 8)
        part_ref[split:] = sum_ref[pl.ds(start, half), :]


def small_parts(basis_in, query_in, basis_out, query_out, out_grads):
    split, tokens, pairs = basis_in.shape[0] + basis_out.shape[0], out_grads.shape[0], query_in.shape[1]
    high = split + tokens
    sources = (basis_out, query_out, basis_in, query_in, out_grads)
    half = jax.ShapeDtypeStruct((split + tokens // 2, pairs), jnp.float32)
    return pl.pallas_call(
        parts_kernel,
        in_specs=[pl.BlockSpec(memory_space=pl.ANY)] * len(sources),
        out_shape=[half, half],
        scratch_shapes=[pltpu.VMEM(source.shape, source.dtype) for source in sources]
        + [pltpu.VMEM((high, pairs), jnp.float32), pltpu.SemaphoreType.DMA((len(sources), 8))],
        compiler_params=pltpu.CompilerParams(vmem_limit_bytes=VMEM_LIMIT),
    )(*[in_hbm(source) for source in sources])


def weigh(query_count, packs, out_query, weights_ref):
    rows, pairs = packs[0].shape[0], out_query.shape[1]
    query_of = lax.broadcasted_iota(jnp.int32, (rows, pairs), 1) // R
    for slot, pack_ref in enumerate(packs):
        in_query = pack_ref[:, :pairs].astype(jnp.float32)
        inverse = 1.0 / (pack_ref[:, pairs:].astype(jnp.float32) + damping)
        for query in range(query_count):
            own = jnp.where(query_of == query, in_query, 0.0).astype(jnp.bfloat16)
            outer_sum = contract_last(own, out_query)
            weights_ref[slot // 2, pl.ds((2 * query + slot % 2) * rows, rows), :] = (
                outer_sum * inverse
            ).astype(jnp.bfloat16)


def project(acts_ref, start, pieces, group, first=0):
    columns = pl.ds(
        pl.multiple_of(group * (acts_ref.shape[1] // 2) + first, LANES), pieces[0].shape[1]
    )
    stacked = jnp.concatenate([piece[...] for piece in pieces], axis=0)
    return contract_last(acts_ref[pl.ds(start, BLOCK), columns], stacked)


def mixing(start, weights, grad_ref):
    return contract_last(grad_ref[pl.ds(start, BLOCK), :], weights)


def mix(start, projected, mixed, onehot_ref):
    product = jnp.concatenate([projected] * (mixed.shape[1] // LANES), axis=1) * mixed
    high = product.astype(jnp.bfloat16)
    low = (product - high.astype(jnp.float32)).astype(jnp.bfloat16)
    onehot = onehot_ref[:, pl.ds(start, BLOCK)]
    return jnp.dot(onehot, high, preferred_element_type=jnp.float32) + jnp.dot(
        onehot, low, preferred_element_type=jnp.float32
    )


def blocks(tokens, body, initial):
    def step(index, carry):
        return body(pl.multiple_of(index * BLOCK, LANES), carry)

    return lax.fori_loop(0, tokens // BLOCK, step, initial, unroll=True)


def weight_kernel(query_count, *refs):
    packs, (out_query_ref, weights_ref) = refs[:4], refs[4:]
    weigh(query_count, packs, out_query_ref[...], weights_ref)


def load_kernel(source_ref, acts_ref, copied):
    copies = cut_copies(source_ref, acts_ref, copied, copied.shape[0])
    for copy in copies:
        copy.start()
    for copy in copies:
        copy.wait()


def first_kernel(acts_ref, *refs):
    slots, total_ref = refs[:8], refs[8]
    columns = slots[0].shape[1]
    group = lax.axis_index("groups")

    def body(start, carry):
        total = 0.0
        for place in range(4):
            half = group if place < 2 else 1 - group
            total = total + project(
                acts_ref, start, (slots[place], slots[4 + place]), half, place % 2 * columns
            )
        total_ref[pl.ds(start, BLOCK), :] = total
        return carry

    blocks(acts_ref.shape[0], body, 0)


def mine_kernel(
    acts_ref, mine_2_ref, mine_3_ref, first_ref, weights_ref, grad_ref, onehot_ref,
    total_ref, mixed_ref, sums_ref,
):
    group = lax.axis_index("groups")

    def body(start, sums):
        rows = pl.ds(start, BLOCK)
        total_ref[rows, :] = project(acts_ref, start, (mine_2_ref, mine_3_ref), group)
        mixed_ref[rows, :] = mixing(start, weights_ref[1], grad_ref)
        mixed = mixing(start, weights_ref[0], grad_ref)
        return sums + mix(start, first_ref[rows, :], mixed, onehot_ref)

    sums_ref[...] = blocks(acts_ref.shape[0], body, jnp.zeros(sums_ref.shape, jnp.float32))


def last_kernel(
    query_count, acts_ref, theirs_2_ref, left_ref, right_ref, total_ref, mixed_ref, onehot_ref,
    before_ref, out_ref,
):
    other = 1 - lax.axis_index("groups")
    cut = left_ref.shape[1]

    def body(start, sums):
        total = total_ref[pl.ds(start, BLOCK), :]
        total = total + project(
            acts_ref, start, (theirs_2_ref.at[:, :cut], left_ref), other
        )
        total = total + project(
            acts_ref, start, (theirs_2_ref.at[:, cut:], right_ref), other, cut
        )
        return sums + mix(start, total, mixed_ref[pl.ds(start, BLOCK), :], onehot_ref)

    sums = blocks(acts_ref.shape[0], body, before_ref[...])
    width = sums.shape[1]
    query_of = lax.broadcasted_iota(jnp.int32, (query_count, width), 1) // (width // query_count)
    chosen = query_of == lax.broadcasted_iota(jnp.int32, (query_count, width), 0)
    scores = contract_last(chosen.astype(jnp.float32), sums, precision=lax.Precision.HIGHEST)
    columns = out_ref.shape[1]
    for place in range(out_ref.shape[0] // query_count):
        out_ref[pl.ds(place * query_count, query_count), :] = scores[
            :, place * columns : (place + 1) * columns
        ]


def call(kernel, out_shape, *operands, **options):
    return pl.pallas_call(
        kernel,
        out_shape=out_shape,
        compiler_params=pltpu.CompilerParams(vmem_limit_bytes=VMEM_LIMIT),
        cost_estimate=pl.CostEstimate(flops=1, bytes_accessed=1, transcendentals=0),
        **options,
    )(*operands)


def precondition(in_rows, eig_rows, out_query):
    row_count = in_rows.shape[0]
    basis_width = out_query.shape[0]
    query_count = out_query.shape[1] // R
    outer_sum = jnp.einsum(
        "jqr,iqr->qji",
        in_rows.reshape(row_count, query_count, R),
        out_query.reshape(basis_width, query_count, R),
        preferred_element_type=jnp.float32,
    )
    inverse = 1.0 / (eig_rows.astype(jnp.float32) + damping)
    return (outer_sum * inverse[None, :, :]).astype(jnp.bfloat16)


def plain_scores(acts, basis_in, pack, out_query, grad_proj, onehot):
    pack = lax.all_gather(pack, "blk", axis=0, tiled=True)
    piece = lax.all_gather(basis_in, "blk", axis=0, tiled=True)
    pairs = out_query.shape[1]
    weighted = precondition(pack[:, :pairs], pack[:, pairs:], out_query)
    projected = contract_last(acts, piece)
    per_token = jnp.stack(
        [jnp.sum(projected * contract_last(grad_proj, slab), axis=1) for slab in weighted]
    )
    return contract_last(per_token, onehot, precision=lax.Precision.HIGHEST)


def stepped_scores(
    acts, out_grads, basis_in, basis_out, eigvals, query_out, query_in, onehot
):
    rows, width = basis_in.shape[0], basis_out.shape[0]
    tokens, seq_count = acts.shape[0], onehot.shape[0]
    query_count = query_in.shape[1] // R
    pair = [(0, 1), (1, 0)]
    place = lax.axis_index("blk")
    inner = (place == 1) | (place == 2)
    of_first = lax.axis_index("rep") == 0

    def along(value):
        return lax.ppermute(value, "blk", [(i, i ^ 1) for i in range(4)])

    def swapped(value):
        return lax.ppermute(value, "groups", pair)

    def across(value, at_ends):
        return lax.ppermute(
            value,
            AXES,
            pairing(lambda g, b, e, r: (g, 3 - b, e, r) if b in (1, 2) else at_ends(g, b, e, r)),
        )

    chunks = take_chunks(basis_in)
    half, other_half = chunks[:2], chunks[2:]
    to_core = lambda g, b, e, r: (g, b, e, 1 - r)
    over_y = lambda g, b, e, r: (1 - g, b, e, r)
    mine_1, middle_3 = [], []
    for chunk in half:
        middle_3.append(across(chunk, to_core))
        mine_1.append(along(chunk))

    split = rows + width
    early, inner, of_first, _ = lax.optimization_barrier((basis_in, inner, of_first, half))
    keep, send = small_parts(early, query_in, basis_out, query_out, out_grads)
    other = lax.ppermute(send, "rep", pair)
    keep = keep + held(other, mine_1[0], middle_3[0])
    other = lax.ppermute(keep, "eig", pair)

    arrived = []
    for first, middle, rest in zip(mine_1, middle_3, other_half):
        from_pair = along(jnp.where(inner, middle, held(rest, first, keep)))
        from_across = across(held(first, middle, keep), over_y)
        arrived.append((from_pair, from_across))

    small = (keep + held(other, *arrived[0])).astype(jnp.bfloat16)
    acts = call(
        load_kernel,
        pltpu.VMEM(acts.shape, acts.dtype),
        in_hbm(held(acts, keep)),
        in_specs=[pl.BlockSpec(memory_space=pl.ANY)],
        scratch_shapes=[pltpu.SemaphoreType.DMA((8,))],
    )
    acts = in_vmem(acts)
    ready = [chunk for both in arrived for chunk in both] + [small, acts]
    mine_2 = jnp.concatenate(
        [jnp.where(inner, held(there, *ready), here) for here, there in arrived], axis=1
    )
    theirs_1 = [
        jnp.where(inner, held(here, mine_2), held(there, mine_2)) for here, there in arrived
    ]
    theirs_2 = swapped(mine_2)
    mine_3 = along(mine_2)

    in_query, out_query, grad_half = small[:rows], small[rows:split], small[split:]
    packs = by_distance(jnp.concatenate([in_query, eigvals], axis=1))
    grad_other = lax.ppermute(grad_half, "rep", pair)
    grad_proj = jnp.concatenate(
        [
            jnp.where(of_first, grad_half, grad_other),
            jnp.where(of_first, grad_other, grad_half),
        ],
        axis=0,
    )
    total_shape = jax.ShapeDtypeStruct((tokens, LANES), jnp.float32)
    first_total = call(
        first_kernel, total_shape, acts, *half, *other_half, *mine_1, *theirs_1
    )

    cut = mine_3.shape[1] // 2
    left_3 = along(held(theirs_2, first_total, *packs[1:])[:, :cut])
    right_3 = swapped(held(mine_3, first_total, *packs[1:])[:, cut:])
    mixed_width = 2 * query_count * rows
    weights = call(
        functools.partial(weight_kernel, query_count),
        jax.ShapeDtypeStruct((2, mixed_width, width), jnp.bfloat16),
        *packs, out_query,
    )
    total, mixed, sums = call(
        mine_kernel,
        [
            total_shape,
            jax.ShapeDtypeStruct((tokens, mixed_width), jnp.float32),
            jax.ShapeDtypeStruct((seq_count, mixed_width), jnp.float32),
        ],
        acts, mine_2, mine_3, first_total, weights, grad_proj, onehot,
    )
    places = lax.axis_size("blk")
    return call(
        functools.partial(last_kernel, query_count),
        jax.ShapeDtypeStruct((places * query_count, seq_count // places), jnp.float32),
        acts, theirs_2, left_3, right_3, total, mixed, onehot, sums,
    )


def plain_path(acts, out_grads, basis_in, basis_out, eigvals, query_out, query_in, onehot):
    def whole_sum(part):
        return swap_sum(swap_sum(part, "rep"), "eig").astype(jnp.bfloat16)

    in_query = whole_sum(jnp.dot(basis_in, query_in, preferred_element_type=jnp.float32))
    out_query = whole_sum(jnp.dot(basis_out, query_out, preferred_element_type=jnp.float32))
    grad_proj = whole_sum(contract_last(out_grads, basis_out))
    pack = jnp.concatenate([in_query, eigvals], axis=1)
    scores = plain_scores(acts, basis_in, pack, out_query, grad_proj, onehot.astype(jnp.float32))
    queries, columns = scores.shape
    places = lax.axis_size("blk")
    parts = scores.reshape(queries, places, columns // places)
    return parts.transpose(1, 0, 2).reshape(places * queries, columns // places)


def on_device(acts, out_grads, basis_in, basis_out, eigvals, query_out, query_in, seq_ids, owner):
    rows, features = basis_in.shape
    pairs = query_in.shape[1]
    seq_count = owner.shape[0]
    labels = jnp.arange(seq_count, dtype=jnp.int32)
    column_of = jnp.sum(jnp.where(seq_ids[None, :] == labels[:, None], owner[:, None], 0), axis=0)
    onehot = (labels[:, None] == column_of[None, :]).astype(jnp.bfloat16)
    stepped = (
        all(lax.axis_size(axis) == size for axis, size in zip(AXES, (2, 4, 2, 2)))
        and 2 * rows == LANES
        and (rows + basis_out.shape[0]) % 16 == acts.shape[0] % 32 == 0
        and features % (4 * LANES) == 0
        and acts.shape[0] % BLOCK == 0
        and pairs == basis_out.shape[0] == LANES
    )
    way = stepped_scores if stepped else plain_path
    parts = way(acts, out_grads, basis_in, basis_out, eigvals, query_out, query_in, onehot)
    own_queries = pairs // R // lax.axis_size(("eig", "rep"))
    own_columns = seq_count // lax.axis_size("blk")
    parts = lax.all_to_all(parts, ("blk", "eig", "rep"), 0, 0, tiled=True)
    return jnp.sum(parts.reshape(-1, own_queries, own_columns), axis=0)


def solution(mesh):
    return jax.shard_map(
        on_device,
        mesh=mesh,
        in_specs=(
            P(("groups", "blk"), ("eig", "rep")),
            P(("groups", "blk"), ("eig", "rep")),
            P("blk", ("eig", "rep")),
            P(None, ("eig", "rep")),
            P("blk", None),
            P(("eig", "rep"), "groups"),
            P(("eig", "rep"), "groups"),
            P(("groups", "blk")),
            P("groups"),
        ),
        out_specs=P(("groups", "eig", "rep"), "blk"),
        check_vma=False,
    )
```

```python
import functools
import itertools

import jax
import jax.numpy as jnp
from jax import lax
from jax.experimental import pallas as pl
from jax.experimental.pallas import tpu as pltpu
from jax.sharding import PartitionSpec as P

R = 32
LANES = 128
BLOCK = 256
VMEM_LIMIT = 16 * 1024 * 1024
AXES = ("groups", "blk", "eig", "rep")


damping = 0.05


def contract_last(left_side, right_side, precision=None):
    return lax.dot_general(
        left_side,
        right_side,
        (((1,), (1,)), ((), ())),
        precision=precision,
        preferred_element_type=jnp.float32,
    )


def swap_sum(value, axis):
    size = lax.axis_size(axis)
    if size & (size - 1):
        return lax.psum(value, axis)
    step = 1
    while step < size:
        pairs = [(i, i ^ step) for i in range(size)]
        value = value + lax.ppermute(value, axis, pairs)
        step *= 2
    return value


def by_distance(value, axis="blk"):
    size = lax.axis_size(axis)
    return [value] + [
        lax.ppermute(value, axis, [(i, i ^ k) for i in range(size)]) for k in range(1, size)
    ]


def held(value, *until):
    return lax.optimization_barrier((value, *until))[0]


def in_hbm(value):
    return pltpu.with_memory_space_constraint(value, pltpu.HBM)


def in_vmem(value):
    return pltpu.with_memory_space_constraint(value, pltpu.VMEM)


def pairing(partner):
    sizes = [lax.axis_size(axis) for axis in AXES]
    places = list(itertools.product(*map(range, sizes)))
    return [(number, places.index(partner(*place))) for number, place in enumerate(places)]


def chunks_kernel(whole_ref, *refs):
    chunk_refs, copied = refs[:4], refs[4]
    columns = chunk_refs[0].shape[1]
    group = lax.axis_index("groups")
    copies = []
    for place, chunk_ref in enumerate(chunk_refs):
        half = group if place < 2 else 1 - group
        begin = pl.multiple_of((2 * half + place % 2) * columns, LANES)
        source = whole_ref.at[:, pl.ds(begin, columns)]
        copies.append(pltpu.make_async_copy(source, chunk_ref, copied.at[place]))
    for copy in copies:
        copy.start()
    for copy in copies:
        copy.wait()


def take_chunks(whole):
    rows, columns = whole.shape
    return pl.pallas_call(
        chunks_kernel,
        in_specs=[pl.BlockSpec(memory_space=pl.ANY)],
        out_shape=[pltpu.VMEM((rows, columns // 4), whole.dtype)] * 4,
        scratch_shapes=[pltpu.SemaphoreType.DMA((4,))],
    )(in_hbm(whole))


def cut_copies(source, target, copied, parts):
    size = source.shape[0] // parts
    places = [pl.ds(part * size, size) for part in range(parts)]
    return [
        pltpu.make_async_copy(source.at[place], target.at[place], copied.at[part])
        for part, place in enumerate(places)
    ]


def parts_kernel(*refs):
    sources, keep_ref, send_ref, copied = refs[:5], refs[5], refs[6], refs[-1]
    held_refs = out_ref, out_query_ref, in_ref, in_query_ref, grads_ref = refs[7:-2]
    sum_ref = refs[-2]
    copies = [
        cut_copies(source, target, copied.at[place], parts)
        for place, (source, target, parts) in enumerate(zip(sources, held_refs, (1, 1, 2, 4, 4)))
    ]
    for group in copies:
        for copy in group:
            copy.start()

    def wait(*places):
        for place in places:
            for copy in copies[place]:
                copy.wait()

    rows, width = in_ref.shape[0], out_ref.shape[0]
    wait(0, 1)
    sum_ref[rows : rows + width] = jnp.dot(
        out_ref[...], out_query_ref[...], preferred_element_type=jnp.float32
    )
    wait(2, 3)
    sum_ref[:rows] = jnp.dot(in_ref[...], in_query_ref[...], preferred_element_type=jnp.float32)
    blocks_copied = copies[4]
    size = grads_ref.shape[0] // len(blocks_copied)

    @pl.loop(0, len(blocks_copied))
    def _(step):
        start = pl.multiple_of(step * size, 16)
        place = pl.ds(start, size)
        pltpu.make_async_copy(
            sources[4].at[place], grads_ref.at[place], copied.at[4, step]
        ).wait()
        sum_ref[pl.ds(rows + width + start, size), :] = contract_last(
            grads_ref[place, :], out_ref[...]
        )

    core, split = lax.axis_index("rep"), rows + width
    half = grads_ref.shape[0] // 2
    for part_ref, whose in ((keep_ref, core), (send_ref, 1 - core)):
        part_ref[:split] = sum_ref[:split]
        start = pl.multiple_of(split + whose * half, 8)
        part_ref[split:] = sum_ref[pl.ds(start, half), :]


def small_parts(basis_in, query_in, basis_out, query_out, out_grads):
    split, tokens, pairs = basis_in.shape[0] + basis_out.shape[0], out_grads.shape[0], query_in.shape[1]
    high = split + tokens
    sources = (basis_out, query_out, basis_in, query_in, out_grads)
    half = jax.ShapeDtypeStruct((split + tokens // 2, pairs), jnp.float32)
    return pl.pallas_call(
        parts_kernel,
        in_specs=[pl.BlockSpec(memory_space=pl.ANY)] * len(sources),
        out_shape=[half, half],
        scratch_shapes=[pltpu.VMEM(source.shape, source.dtype) for source in sources]
        + [pltpu.VMEM((high, pairs), jnp.float32), pltpu.SemaphoreType.DMA((len(sources), 8))],
        compiler_params=pltpu.CompilerParams(vmem_limit_bytes=VMEM_LIMIT),
    )(*[in_hbm(source) for source in sources])


def weigh(query_count, packs, out_query, weights_ref):
    rows, pairs = packs[0].shape[0], out_query.shape[1]
    query_of = lax.broadcasted_iota(jnp.int32, (rows, pairs), 1) // R
    for slot, pack_ref in enumerate(packs):
        in_query = pack_ref[:, :pairs].astype(jnp.float32)
        inverse = 1.0 / (pack_ref[:, pairs:].astype(jnp.float32) + damping)
        for query in range(query_count):
            own = jnp.where(query_of == query, in_query, 0.0).astype(jnp.bfloat16)
            outer_sum = contract_last(own, out_query)
            weights_ref[slot // 2, pl.ds((2 * query + slot % 2) * rows, rows), :] = (
                outer_sum * inverse
            ).astype(jnp.bfloat16)


def project(acts_ref, start, pieces, group, first=0):
    columns = pl.ds(
        pl.multiple_of(group * (acts_ref.shape[1] // 2) + first, LANES), pieces[0].shape[1]
    )
    stacked = jnp.concatenate([piece[...] for piece in pieces], axis=0)
    return contract_last(acts_ref[pl.ds(start, BLOCK), columns], stacked)


def mixing(start, weights, grad_ref):
    return contract_last(grad_ref[pl.ds(start, BLOCK), :], weights)


def mix(start, projected, mixed, onehot_ref, once=False):
    product = jnp.concatenate([projected] * (mixed.shape[1] // LANES), axis=1) * mixed
    high = product.astype(jnp.bfloat16)
    onehot = onehot_ref[:, pl.ds(start, BLOCK)]
    if once:
        return jnp.dot(onehot, high, preferred_element_type=jnp.float32)
    low = (product - high.astype(jnp.float32)).astype(jnp.bfloat16)
    onehot = onehot_ref[:, pl.ds(start, BLOCK)]
    return jnp.dot(onehot, high, preferred_element_type=jnp.float32) + jnp.dot(
        onehot, low, preferred_element_type=jnp.float32
    )


def blocks(tokens, body, initial):
    def step(index, carry):
        return body(pl.multiple_of(index * BLOCK, LANES), carry)

    return lax.fori_loop(0, tokens // BLOCK, step, initial, unroll=True)


def weight_kernel(query_count, *refs):
    packs, (out_query_ref, weights_ref) = refs[:4], refs[4:]
    weigh(query_count, packs, out_query_ref[...], weights_ref)


def load_kernel(source_ref, acts_ref, copied):
    copies = cut_copies(source_ref, acts_ref, copied, copied.shape[0])
    for copy in copies:
        copy.start()
    for copy in copies:
        copy.wait()


def first_kernel(acts_ref, *refs):
    slots, total_ref = refs[:8], refs[8]
    columns = slots[0].shape[1]
    group = lax.axis_index("groups")

    def body(start, carry):
        total = 0.0
        for place in range(4):
            half = group if place < 2 else 1 - group
            total = total + project(
                acts_ref, start, (slots[place], slots[4 + place]), half, place % 2 * columns
            )
        total_ref[pl.ds(start, BLOCK), :] = total
        return carry

    blocks(acts_ref.shape[0], body, 0)


def mine_kernel(
    acts_ref, mine_2_ref, mine_3_ref, first_ref, weights_ref, grad_ref, onehot_ref,
    total_ref, mixed_ref, sums_ref,
):
    group = lax.axis_index("groups")

    def body(start, sums):
        rows = pl.ds(start, BLOCK)
        total_ref[rows, :] = project(acts_ref, start, (mine_2_ref, mine_3_ref), group)
        mixed_ref[rows, :] = mixing(start, weights_ref[1], grad_ref)
        mixed = mixing(start, weights_ref[0], grad_ref)
        return sums + mix(start, first_ref[rows, :], mixed, onehot_ref)

    sums_ref[...] = blocks(acts_ref.shape[0], body, jnp.zeros(sums_ref.shape, jnp.float32))


def last_kernel(
    query_count, acts_ref, theirs_2_ref, left_ref, right_ref, total_ref, mixed_ref, onehot_ref,
    before_ref, out_ref,
):
    other = 1 - lax.axis_index("groups")
    cut = left_ref.shape[1]

    def body(start, sums):
        total = total_ref[pl.ds(start, BLOCK), :]
        total = total + project(
            acts_ref, start, (theirs_2_ref.at[:, :cut], left_ref), other
        )
        total = total + project(
            acts_ref, start, (theirs_2_ref.at[:, cut:], right_ref), other, cut
        )
        return sums + mix(start, total, mixed_ref[pl.ds(start, BLOCK), :], onehot_ref, once=True)

    sums = blocks(acts_ref.shape[0], body, before_ref[...])
    width = sums.shape[1]
    query_of = lax.broadcasted_iota(jnp.int32, (query_count, width), 1) // (width // query_count)
    chosen = query_of == lax.broadcasted_iota(jnp.int32, (query_count, width), 0)
    scores = contract_last(chosen.astype(jnp.float32), sums, precision=lax.Precision.HIGHEST)
    columns = out_ref.shape[1]
    for place in range(out_ref.shape[0] // query_count):
        out_ref[pl.ds(place * query_count, query_count), :] = scores[
            :, place * columns : (place + 1) * columns
        ]


def call(kernel, out_shape, *operands, **options):
    return pl.pallas_call(
        kernel,
        out_shape=out_shape,
        compiler_params=pltpu.CompilerParams(vmem_limit_bytes=VMEM_LIMIT),
        cost_estimate=pl.CostEstimate(flops=1, bytes_accessed=1, transcendentals=0),
        **options,
    )(*operands)


def precondition(in_rows, eig_rows, out_query):
    row_count = in_rows.shape[0]
    basis_width = out_query.shape[0]
    query_count = out_query.shape[1] // R
    outer_sum = jnp.einsum(
        "jqr,iqr->qji",
        in_rows.reshape(row_count, query_count, R),
        out_query.reshape(basis_width, query_count, R),
        preferred_element_type=jnp.float32,
    )
    inverse = 1.0 / (eig_rows.astype(jnp.float32) + damping)
    return (outer_sum * inverse[None, :, :]).astype(jnp.bfloat16)


def plain_scores(acts, basis_in, pack, out_query, grad_proj, onehot):
    pack = lax.all_gather(pack, "blk", axis=0, tiled=True)
    piece = lax.all_gather(basis_in, "blk", axis=0, tiled=True)
    pairs = out_query.shape[1]
    weighted = precondition(pack[:, :pairs], pack[:, pairs:], out_query)
    projected = contract_last(acts, piece)
    per_token = jnp.stack(
        [jnp.sum(projected * contract_last(grad_proj, slab), axis=1) for slab in weighted]
    )
    return contract_last(per_token, onehot, precision=lax.Precision.HIGHEST)


def stepped_scores(
    acts, out_grads, basis_in, basis_out, eigvals, query_out, query_in, onehot
):
    rows, width = basis_in.shape[0], basis_out.shape[0]
    tokens, seq_count = acts.shape[0], onehot.shape[0]
    query_count = query_in.shape[1] // R
    pair = [(0, 1), (1, 0)]
    place = lax.axis_index("blk")
    inner = (place == 1) | (place == 2)
    of_first = lax.axis_index("rep") == 0

    def along(value):
        return lax.ppermute(value, "blk", [(i, i ^ 1) for i in range(4)])

    def swapped(value):
        return lax.ppermute(value, "groups", pair)

    def across(value, at_ends):
        return lax.ppermute(
            value,
            AXES,
            pairing(lambda g, b, e, r: (g, 3 - b, e, r) if b in (1, 2) else at_ends(g, b, e, r)),
        )

    chunks = take_chunks(basis_in)
    half, other_half = chunks[:2], chunks[2:]
    to_core = lambda g, b, e, r: (g, b, e, 1 - r)
    over_y = lambda g, b, e, r: (1 - g, b, e, r)
    mine_1, middle_3 = [], []
    for chunk in half:
        middle_3.append(across(chunk, to_core))
        mine_1.append(along(chunk))

    split = rows + width
    early, inner, of_first, _ = lax.optimization_barrier((basis_in, inner, of_first, half))
    keep, send = small_parts(early, query_in, basis_out, query_out, out_grads)
    other = lax.ppermute(send, "rep", pair)
    keep = keep + held(other, mine_1[0], middle_3[0])
    other = lax.ppermute(keep, "eig", pair)

    arrived = []
    for first, middle, rest in zip(mine_1, middle_3, other_half):
        from_pair = along(jnp.where(inner, middle, held(rest, first, keep)))
        from_across = across(held(first, middle, keep), over_y)
        arrived.append((from_pair, from_across))

    small = (keep + held(other, *arrived[0])).astype(jnp.bfloat16)
    acts = call(
        load_kernel,
        pltpu.VMEM(acts.shape, acts.dtype),
        in_hbm(held(acts, keep)),
        in_specs=[pl.BlockSpec(memory_space=pl.ANY)],
        scratch_shapes=[pltpu.SemaphoreType.DMA((8,))],
    )
    acts = in_vmem(acts)
    ready = [chunk for both in arrived for chunk in both] + [small, acts]
    mine_2 = jnp.concatenate(
        [jnp.where(inner, held(there, *ready), here) for here, there in arrived], axis=1
    )
    theirs_1 = [
        jnp.where(inner, held(here, mine_2), held(there, mine_2)) for here, there in arrived
    ]
    theirs_2 = swapped(mine_2)
    mine_3 = along(mine_2)

    in_query, out_query, grad_half = small[:rows], small[rows:split], small[split:]
    packs = by_distance(jnp.concatenate([in_query, eigvals], axis=1))
    grad_other = lax.ppermute(grad_half, "rep", pair)
    grad_proj = jnp.concatenate(
        [
            jnp.where(of_first, grad_half, grad_other),
            jnp.where(of_first, grad_other, grad_half),
        ],
        axis=0,
    )
    total_shape = jax.ShapeDtypeStruct((tokens, LANES), jnp.float32)
    first_total = call(
        first_kernel, total_shape, acts, *half, *other_half, *mine_1, *theirs_1
    )

    cut = mine_3.shape[1] // 2
    left_3 = along(held(theirs_2, first_total, *packs[1:])[:, :cut])
    right_3 = swapped(held(mine_3, first_total, *packs[1:])[:, cut:])
    mixed_width = 2 * query_count * rows
    weights = call(
        functools.partial(weight_kernel, query_count),
        jax.ShapeDtypeStruct((2, mixed_width, width), jnp.bfloat16),
        *packs, out_query,
    )
    total, mixed, sums = call(
        mine_kernel,
        [
            total_shape,
            jax.ShapeDtypeStruct((tokens, mixed_width), jnp.float32),
            jax.ShapeDtypeStruct((seq_count, mixed_width), jnp.float32),
        ],
        acts, mine_2, mine_3, first_total, weights, grad_proj, onehot,
    )
    places = lax.axis_size("blk")
    return call(
        functools.partial(last_kernel, query_count),
        jax.ShapeDtypeStruct((places * query_count, seq_count // places), jnp.float32),
        acts, theirs_2, left_3, right_3, total, mixed, onehot, sums,
    )


def plain_path(acts, out_grads, basis_in, basis_out, eigvals, query_out, query_in, onehot):
    def whole_sum(part):
        return swap_sum(swap_sum(part, "rep"), "eig").astype(jnp.bfloat16)

    in_query = whole_sum(jnp.dot(basis_in, query_in, preferred_element_type=jnp.float32))
    out_query = whole_sum(jnp.dot(basis_out, query_out, preferred_element_type=jnp.float32))
    grad_proj = whole_sum(contract_last(out_grads, basis_out))
    pack = jnp.concatenate([in_query, eigvals], axis=1)
    scores = plain_scores(acts, basis_in, pack, out_query, grad_proj, onehot.astype(jnp.float32))
    queries, columns = scores.shape
    places = lax.axis_size("blk")
    parts = scores.reshape(queries, places, columns // places)
    return parts.transpose(1, 0, 2).reshape(places * queries, columns // places)


def on_device(acts, out_grads, basis_in, basis_out, eigvals, query_out, query_in, seq_ids, owner):
    rows, features = basis_in.shape
    pairs = query_in.shape[1]
    seq_count = owner.shape[0]
    labels = jnp.arange(seq_count, dtype=jnp.int32)
    column_of = jnp.sum(jnp.where(seq_ids[None, :] == labels[:, None], owner[:, None], 0), axis=0)
    onehot = (labels[:, None] == column_of[None, :]).astype(jnp.bfloat16)
    stepped = (
        all(lax.axis_size(axis) == size for axis, size in zip(AXES, (2, 4, 2, 2)))
        and 2 * rows == LANES
        and (rows + basis_out.shape[0]) % 16 == acts.shape[0] % 32 == 0
        and features % (4 * LANES) == 0
        and acts.shape[0] % BLOCK == 0
        and pairs == basis_out.shape[0] == LANES
    )
    way = stepped_scores if stepped else plain_path
    parts = way(acts, out_grads, basis_in, basis_out, eigvals, query_out, query_in, onehot)
    own_queries = pairs // R // lax.axis_size(("eig", "rep"))
    own_columns = seq_count // lax.axis_size("blk")
    parts = lax.all_to_all(parts, ("blk", "eig", "rep"), 0, 0, tiled=True)
    return jnp.sum(parts.reshape(-1, own_queries, own_columns), axis=0)


def solution(mesh):
    return jax.shard_map(
        on_device,
        mesh=mesh,
        in_specs=(
            P(("groups", "blk"), ("eig", "rep")),
            P(("groups", "blk"), ("eig", "rep")),
            P("blk", ("eig", "rep")),
            P(None, ("eig", "rep")),
            P("blk", None),
            P(("eig", "rep"), "groups"),
            P(("eig", "rep"), "groups"),
            P(("groups", "blk")),
            P("groups"),
        ),
        out_specs=P(("groups", "eig", "rep"), "blk"),
        check_vma=False,
    )
```
